32 devices in a mesh: groups: 2 (over y), row: 4 (over z), col: 2 (over x), half: 2 (over core).
Axes of the slice: x: 2, y: 2, z: 4, core: 2. Of those that a mesh axis runs over, the one named last changes fastest.
Arguments:
- log_derivs: bfloat16 [2048, 16384], P(('groups', 'row'), ('col', 'half')), parts along dimension 0, may hold values from -40 to 40
- shift: float32 [2], P('groups'), parts along dimension 0, may hold values from 0.5 to 2
Outputs:
- gram: float32 [2048, 1024], P(('groups', 'row'), ('col', 'half')), parts along dimension 0
The draws below stay inside these ranges and needn't reach their ends.
There are 2 independent parts, one for each index of `groups`. The reference program is written for one: setup_inputs(seed, part) draws one part's arguments, and reference() takes and returns one part's arrays. A program takes and returns all parts, laid end to end along the dimension named above; each array names one. Nothing has to cross between parts.
All inputs are finite; a program needn't handle non-finite values.
Results may differ from the reference program's by a relative error of at most 0.0003.
Values may be sent and summed in bfloat16 or wider, within the bound.
No kernel may reach another device: no remote copies, remote signals or barrier semaphores. Data moves between devices by JAX's collectives and lax.ppermute only.
A program may use at most 64 MiB of HBM per device.

```python
import math
import jax
import jax.numpy as jnp
from jax import lax

PARAMS = 16384
SAMPLES = 1024


def draw_log_derivs(key, part):
    key = jax.random.fold_in(key, 11)
    keys = jax.random.split(key, 6)
    factors = 256
    trend = 1.0 + 2.0 * jnp.arange(SAMPLES, dtype=jnp.float32)[:, None] / (SAMPLES - 1)
    row_scale = jnp.exp(jax.random.uniform(keys[1], (SAMPLES, 1), jnp.float32, -1.2, 1.2))
    column_scale = jnp.exp(jax.random.uniform(keys[2], (1, PARAMS), jnp.float32, -0.1, 0.1))
    left_factor = jax.random.randint(keys[4], (SAMPLES, factors), -3, 4).astype(jnp.float32)
    right_factor = jax.random.randint(keys[5], (factors, PARAMS), -3, 4).astype(jnp.float32)
    shared = jnp.dot(left_factor, right_factor, precision=lax.Precision.HIGHEST) / 64.0
    centre = jnp.clip(jax.random.normal(keys[0], (1, PARAMS), jnp.float32), -4.0, 4.0)
    noise = jnp.clip(jax.random.normal(keys[3], (SAMPLES, PARAMS), jnp.float32), -4.0, 4.0)
    mixed = jnp.clip(0.8 * shared + 0.6 * noise, -4.0, 4.0)
    values = centre * trend + 0.5 * mixed * row_scale * column_scale
    return values.astype(jnp.bfloat16)


def setup_inputs(seed: int = 0, part: int = 0) -> dict:
    key_of = jax.random.split(jax.random.key(seed), 3)
    part_keys = jax.random.split(jax.random.fold_in(key_of[2], part), 3)
    log_derivs = draw_log_derivs(jax.random.fold_in(jax.random.fold_in(key_of[2], part), 71), part)
    shift = jnp.clip(jnp.exp(jax.random.uniform(part_keys[1], (1,), jnp.float32, math.log(0.5), math.log(2.0))), 0.5, 2.0)
    return dict(log_derivs=log_derivs, shift=shift)


def reference(log_derivs, shift):
    values = log_derivs.astype(jnp.float32)
    mean = jnp.sum(values, axis=0) / SAMPLES
    centered = (values - mean[None, :]).astype(jnp.bfloat16)
    product = jnp.dot(centered, centered.T, preferred_element_type=jnp.float32)
    identity = jnp.eye(SAMPLES, dtype=jnp.float32)
    return product / SAMPLES + shift[0] * identity
```

```python
import jax
import jax.numpy as jnp
from jax import lax
from jax.sharding import PartitionSpec as P


def pair_product(left, right):
    return jnp.einsum("ip,jp->ij", left, right, preferred_element_type=jnp.float32)


def add_shift(summed, samples, shift, local_rows):
    width = summed.shape[1]
    first_row = lax.axis_index("row") * local_rows
    block = lax.axis_index("col") * lax.axis_size("half") + lax.axis_index("half")
    row_ids = first_row + lax.broadcasted_iota(jnp.int32, (local_rows, width), 0)
    column_ids = block * width + lax.broadcasted_iota(jnp.int32, (local_rows, width), 1)
    return summed / samples + jnp.where(row_ids == column_ids, shift[0], 0.0)


def gathered(log_derivs, shift):
    local_rows = log_derivs.shape[0]
    samples = local_rows * lax.axis_size("row")
    rows = lax.all_gather(log_derivs, "row", axis=0, tiled=True).astype(jnp.float32)
    mean = jnp.sum(rows, axis=0) / samples
    centered = (rows - mean[None, :]).astype(jnp.bfloat16)
    own = (log_derivs.astype(jnp.float32) - mean[None, :]).astype(jnp.bfloat16)
    tile = pair_product(own, centered)
    summed = lax.psum_scatter(tile, ("col", "half"), scatter_dimension=1, tiled=True)
    return add_shift(summed, samples, shift, local_rows)


def two_centres(log_derivs, shift):
    local_rows, local_params = log_derivs.shape
    samples = local_rows * 4
    half_params = local_params // 2
    row, col, half = (lax.axis_index(name) for name in ("row", "col", "half"))
    upper = (row >= 2).astype(jnp.int32)
    near = lax.dynamic_slice_in_dim(log_derivs, (1 - upper) * half_params, half_params, 1)
    far = lax.dynamic_slice_in_dim(log_derivs, upper * half_params, half_params, 1)

    from_centre = lax.ppermute(far, "row", [(1, 2), (2, 1)])
    from_edge = lax.ppermute(near, "row", [(0, 1), (3, 2)])
    from_far_edge = lax.ppermute(far, "row", [(0, 2), (3, 1)])

    blocks = jnp.stack([from_edge, near, from_centre, from_far_edge]).astype(jnp.float32)
    mean = jnp.sum(blocks, axis=(0, 1)) / samples
    centered = (blocks - mean).astype(jnp.bfloat16)
    rows = centered.reshape(4 * local_rows, half_params)

    def place(c, h):
        k = c * 2 + h
        return jnp.where(upper == 1, 3 - k, k)

    def columns(c, h):
        right = lax.dynamic_index_in_dim(centered, place(c, h), 0, keepdims=False)
        return pair_product(rows, right)

    def swap(value, axis):
        return lax.ppermute(value, axis, [(0, 1), (1, 0)])

    other_both = swap(columns(1 - col, 1 - half), "half")
    other_col = columns(1 - col, half) + other_both
    crossed = swap(other_col, "col")
    other_half = swap(columns(col, 1 - half), "half")
    mine = columns(col, half) + other_half + crossed
    keep, send = mine[: 2 * local_rows], mine[2 * local_rows :]
    arrived = lax.ppermute(send, "row", [(1, 2), (2, 1)])
    centre = keep[local_rows:] + arrived[:local_rows]
    edge = keep[:local_rows] + arrived[local_rows:]
    delivered = lax.ppermute(edge, "row", [(1, 0), (2, 3)])
    is_centre = jnp.logical_or(row == 1, row == 2)
    summed = jnp.where(is_centre, centre, delivered)
    return add_shift(summed, samples, shift, local_rows)


def solution(mesh):
    shape = mesh.shape
    small = shape["row"] == 4 and shape["col"] == 2 and shape["half"] == 2
    return jax.shard_map(
        two_centres if small else gathered,
        mesh=mesh,
        in_specs=(P(("groups", "row"), ("col", "half")), P("groups")),
        out_specs=P(("groups", "row"), ("col", "half")),
        check_vma=False,
    )
```

```python
import jax
import jax.numpy as jnp
from jax import lax
from jax.sharding import PartitionSpec as P


def pair_product(left, right):
    return jnp.einsum("ip,jp->ij", left, right, preferred_element_type=jnp.float32)


def add_shift(summed, samples, shift, local_rows):
    width = summed.shape[1]
    first_row = lax.axis_index("row") * local_rows
    block = lax.axis_index("col") * lax.axis_size("half") + lax.axis_index("half")
    row_ids = first_row + lax.broadcasted_iota(jnp.int32, (local_rows, width), 0)
    column_ids = block * width + lax.broadcasted_iota(jnp.int32, (local_rows, width), 1)
    return summed / samples + jnp.where(row_ids == column_ids, shift[0], 0.0)


def gathered(log_derivs, shift):
    local_rows = log_derivs.shape[0]
    samples = local_rows * lax.axis_size("row")
    rows = lax.all_gather(log_derivs, "row", axis=0, tiled=True).astype(jnp.float32)
    mean = jnp.sum(rows, axis=0) / samples
    centered = (rows - mean[None, :]).astype(jnp.bfloat16)
    own = (log_derivs.astype(jnp.float32) - mean[None, :]).astype(jnp.bfloat16)
    tile = pair_product(own, centered)
    summed = lax.psum_scatter(tile, ("col", "half"), scatter_dimension=1, tiled=True)
    return add_shift(summed, samples, shift, local_rows)


EARLY = (
    (((0, 0), (0, 1)), ((0, 2), (1, 2))),
    (((0, 1), (0, 0)), ((1, 2), (2, 2))),
    (((1, 0), (1, 1)), ((2, 0), (0, 2))),
    (((1, 1), (1, 0)), ((2, 1), (2, 0))),
    ((None, None), ((2, 2), (2, 1))),
)
LATE = (
    (((3, 0), (3, 1)), ((3, 2), (3, 3))),
    (((3, 1), (3, 0)), ((3, 3), (3, 2))),
    (((0, 3), (1, 3)), ((2, 3), None)),
    (((1, 3), (0, 3)), (None, (2, 3))),
)


def device_index(row, col, half):
    return (row * 2 + col) * 2 + half


def round_pairs(blocks):
    pairs = []
    for side in (0, 1):
        for turn in (0, 1):
            for half in (0, 1):
                block = blocks[half][turn]
                if block is None:
                    continue
                i, j = (3 - b if side else b for b in block)
                source = device_index(1 + side, turn ^ side, half)
                pairs.append((source, device_index(i, j // 2, j % 2)))
    return pairs


def two_centres(log_derivs, shift):
    local_rows, local_params = log_derivs.shape
    samples = local_rows * 4
    part = local_params // 2
    everyone = ("row", "col", "half")
    row, col, half = (lax.axis_index(name) for name in everyone)
    side = (row >= 2).astype(jnp.int32)
    turn = jnp.bitwise_xor(col, side)
    near = lax.dynamic_slice_in_dim(log_derivs, (1 - side) * part, part, 1)
    far = lax.dynamic_slice_in_dim(log_derivs, side * part, part, 1)

    to_centre = [(1, 2), (2, 1)]
    to_own = [(0, 1), (3, 2)]
    to_far = [(0, 2), (3, 1)]
    centres = [(r * 2 + h, r * 2 + 1 - h) for r in (1, 2) for h in (0, 1)]

    def swap(value):
        return lax.ppermute(value, ("row", "half"), centres)

    def sums(value):
        return jnp.sum(value.astype(jnp.float32), axis=0, keepdims=True)

    from_centre = lax.ppermute(far, "row", to_centre)
    from_edge = lax.ppermute(near, "row", to_own)
    near_sum, far_sum = sums(near), sums(far)
    total = near_sum + lax.ppermute(near_sum, "row", to_own)
    total = total + lax.ppermute(far_sum, "row", to_centre)
    total = total + lax.ppermute(far_sum, "row", to_far)
    mean = total / samples
    mean = jnp.concatenate([mean, swap(mean)], axis=1)
    from_far_edge = lax.ppermute(far, "row", to_far)

    def centred(own):
        both = jnp.concatenate([own, swap(own)], axis=1).astype(jnp.float32)
        return (both - mean).astype(jnp.bfloat16)

    def scaled(product):
        return (product / samples).astype(jnp.float16)

    edge, centre, other_centre = centred(from_edge), centred(near), centred(from_centre)
    early = jnp.concatenate([edge, centre, other_centre], axis=0)
    early_tile = scaled(pair_product(early, early))

    def pick(blocks):
        table = jnp.array([[b or (0, 0) for b in pair] for pair in blocks], jnp.int32)
        place = table[half, turn] * local_rows
        return lax.dynamic_slice(early_tile, (place[0], place[1]), (local_rows, local_rows))

    def send(value, blocks):
        return lax.ppermute(value, everyone, round_pairs(blocks))

    arrived = [send(pick(blocks), blocks) for blocks in EARLY]

    last = centred(from_far_edge)
    lower = jnp.concatenate([edge, centre], axis=0)
    upper = jnp.concatenate([other_centre, last], axis=0)
    held = jnp.where(half == 0, lower, upper)
    wide = scaled(pair_product(last, held)).reshape(local_rows, 2, local_rows)
    tall = scaled(pair_product(held, last)).reshape(2, local_rows, local_rows)
    flip = (1 - half) * turn
    keep = (1 - half) * (1 - turn)
    late = [
        lax.dynamic_index_in_dim(wide, turn, 1, keepdims=False),
        lax.dynamic_index_in_dim(wide, 1 - turn, 1, keepdims=False),
        lax.dynamic_index_in_dim(tall, flip, 0, keepdims=False),
        lax.dynamic_index_in_dim(tall, keep, 0, keepdims=False),
    ]
    arrived += [send(value, blocks) for value, blocks in zip(late, LATE)]
    summed = sum(block.astype(jnp.float32) for block in arrived)
    return add_shift(summed, 1, shift, local_rows)


def solution(mesh):
    shape = mesh.shape
    small = shape["row"] == 4 and shape["col"] == 2 and shape["half"] == 2
    return jax.shard_map(
        two_centres if small else gathered,
        mesh=mesh,
        in_specs=(P(("groups", "row"), ("col", "half")), P("groups")),
        out_specs=P(("groups", "row"), ("col", "half")),
        check_vma=False,
    )
```

```python
import functools

import jax
import jax.numpy as jnp
from jax import lax
from jax.experimental import pallas as pl
from jax.experimental.pallas import tpu as pltpu
from jax.sharding import PartitionSpec as P


def pair_product(left, right):
    return jnp.einsum("ip,jp->ij", left, right, preferred_element_type=jnp.float32)


def add_shift(summed, samples, shift, local_rows):
    width = summed.shape[1]
    first_row = lax.axis_index("row") * local_rows
    block = lax.axis_index("col") * lax.axis_size("half") + lax.axis_index("half")
    row_ids = first_row + lax.broadcasted_iota(jnp.int32, (local_rows, width), 0)
    column_ids = block * width + lax.broadcasted_iota(jnp.int32, (local_rows, width), 1)
    return summed / samples + jnp.where(row_ids == column_ids, shift[0], 0.0)


def gathered(log_derivs, shift):
    local_rows = log_derivs.shape[0]
    samples = local_rows * lax.axis_size("row")
    rows = lax.all_gather(log_derivs, "row", axis=0, tiled=True).astype(jnp.float32)
    mean = jnp.sum(rows, axis=0) / samples
    centered = (rows - mean[None, :]).astype(jnp.bfloat16)
    own = (log_derivs.astype(jnp.float32) - mean[None, :]).astype(jnp.bfloat16)
    tile = pair_product(own, centered)
    summed = lax.psum_scatter(tile, ("col", "half"), scatter_dimension=1, tiled=True)
    return add_shift(summed, samples, shift, local_rows)


EARLY = (
    (((0, 0), (0, 1)), ((0, 2), (1, 2))),
    (((0, 1), (0, 0)), ((1, 2), (2, 2))),
    (((1, 0), (1, 1)), ((2, 0), (0, 2))),
    (((1, 1), (1, 0)), ((2, 1), (2, 0))),
    ((None, None), ((2, 2), (2, 1))),
)
LATE = (
    (((3, 0), (3, 1)), ((3, 2), (3, 3))),
    (((3, 1), (3, 0)), ((3, 3), (3, 2))),
    (((0, 3), (1, 3)), ((2, 3), None)),
    (((1, 3), (0, 3)), (None, (2, 3))),
)
EARLY_SUMS = (((0, 0), (0, 1), (1, 1)), ((2, 2), (2, 0), (2, 1)))
EARLY_HELD = (
    ((0, 0), (0, 1), (1, 1), (1, 0), (1, 1)),
    ((2, 2), (2, 0), (2, 1), (0, 2), (1, 2)),
)
LATE_SUMS = (((3, 0), (3, 1)), ((3, 2), (3, 3)))
LATE_HELD = (
    ((3, 0), (3, 1), (0, 3), (1, 3)),
    ((3, 2), (3, 3), (2, 3), (3, 3)),
)
EXTRA = 16
HEAD = 64
VMEM = pl.BlockSpec(memory_space=pltpu.VMEM)
SMEM = pl.BlockSpec(memory_space=pltpu.SMEM)
ANY = pl.BlockSpec(memory_space=pl.ANY)
LIMIT = pltpu.CompilerParams(vmem_limit_bytes=40 * 2**20)


def device_index(row, col, half):
    return (row * 2 + col) * 2 + half


def round_pairs(blocks):
    pairs = []
    for side in (0, 1):
        for turn in (0, 1):
            for half in (0, 1):
                block = blocks[half][turn]
                if block is None:
                    continue
                i, j = (3 - b if side else b for b in block)
                source = device_index(1 + side, turn ^ side, half)
                pairs.append((source, device_index(i, j // 2, j % 2)))
    return pairs


def held_place(held, rounds):
    return [
        [[0 if b is None else held[half].index(b) for b in rounds_[half]] for half in (0, 1)]
        for rounds_ in rounds
    ]


def far_kernel(bits, values, far, head, tail, sems):
    part = far.shape[1]
    columns = pl.ds(pl.multiple_of(bits[0] * part, 128), part)
    copies = [
        pltpu.make_async_copy(values.at[:, columns], far, sems.at[0]),
        pltpu.make_async_copy(values.at[pl.ds(0, HEAD), columns], head, sems.at[1]),
        pltpu.make_async_copy(values.at[pl.ds(HEAD, tail.shape[0]), columns], tail, sems.at[2]),
    ]
    for copy in copies:
        copy.start()
    for copy in copies:
        copy.wait()


def near_kernel(bits, values, near, sums):
    rows, part = values.shape[0], values.shape[1] // 2
    step = 512

    @pl.loop(0, part // step)
    def _(i):
        out = pl.ds(pl.multiple_of(i * step, step), step)
        near_columns = pl.ds(pl.multiple_of((1 - bits[0]) * part + i * step, step), step)
        far_columns = pl.ds(pl.multiple_of(bits[0] * part + i * step, step), step)
        block = values[:, near_columns]
        near[pl.ds(0, rows), out] = block
        near_sum = jnp.sum(block.astype(jnp.float32), axis=0, keepdims=True)
        far_sum = jnp.sum(values[:, far_columns].astype(jnp.float32), axis=0, keepdims=True)
        sums[pl.ds(0, 1), out] = near_sum
        sums[pl.ds(1, 1), out] = far_sum
        pieces = []
        for left in (near_sum, far_sum):
            for _ in range(3):
                piece = left.astype(jnp.bfloat16).astype(jnp.float32)
                pieces.append(piece)
                left = left - piece
        pieces.append(jnp.zeros((EXTRA - len(pieces), step), jnp.float32))
        near[pl.ds(rows, EXTRA), out] = jnp.concatenate(pieces, axis=0).astype(jnp.bfloat16)


def block_product(left, right):
    return lax.dot_general(left, right, (((1,), (1,)), ((), ())), preferred_element_type=jnp.float32)


def early_kernel(bits, edge, near, other, sums, arrived, centred, mean, own, send, both):
    rows = other.shape[0]
    pieces = edge[pl.ds(rows, EXTRA), :].astype(jnp.float32)
    edge_sum = pieces[0:1] + pieces[1:2] + pieces[2:3]
    average = (sums[pl.ds(0, 1), :] + edge_sum + arrived[...]) * (1.0 / (4 * rows))
    mean[...] = average
    for i, block in enumerate((edge, near, other)):
        values = block[pl.ds(0, rows), :].astype(jnp.float32)
        centred[i] = (values - average).astype(jnp.bfloat16)
    for core in (0, 1):
        for place, (i, j) in enumerate(EARLY_SUMS[core]):
            both[core, place] = block_product(centred[i], centred[j])
    own[...] = both[bits[1]]
    send[...] = both[1 - bits[1]]


def late_kernel(bits, head, tail, mean, centred, *rest):
    passed = (len(rest) - 4) // 2
    own, send = rest[passed], rest[passed + 1]
    last, both = rest[-2:]
    average = mean[...]
    last[pl.ds(0, HEAD), :] = (head[...].astype(jnp.float32) - average).astype(jnp.bfloat16)
    last[pl.ds(HEAD, tail.shape[0]), :] = (tail[...].astype(jnp.float32) - average).astype(jnp.bfloat16)
    for core in (0, 1):
        for place, (_, j) in enumerate(LATE_SUMS[core]):
            both[core, place] = block_product(last[...], last[...] if j == 3 else centred[j])
    own[...] = both[bits[1]]
    send[...] = both[1 - bits[1]]


def combine_kernel(flips, scale, bits, places, own, other, *rest):
    held = rest[-1]
    count = own.shape[0]
    for i in range(count):
        held[i] = (own[i] + other[i]) * scale
    for n, i in enumerate(flips):
        held[count + n] = held[i].T
    for r, out in enumerate(rest[:-1]):
        out[...] = held[places[r, bits[1], bits[2]]]


def shape_of(shape, dtype):
    return jax.ShapeDtypeStruct(shape, dtype)


def combine(bits, own, other, flips, held, rounds, samples):
    rows = own.shape[1]
    places = jnp.array(held_place(held, rounds), jnp.int32)
    return pl.pallas_call(
        functools.partial(combine_kernel, flips, 1.0 / samples),
        out_shape=[shape_of((rows, rows), jnp.float32)] * len(rounds),
        in_specs=[SMEM, SMEM, VMEM, VMEM],
        out_specs=[VMEM] * len(rounds),
        scratch_shapes=[pltpu.VMEM((len(held[0]), rows, rows), jnp.float32)],
        compiler_params=LIMIT,
    )(bits, places, own, other)


def two_centres(log_derivs, shift):
    local_rows, local_params = log_derivs.shape
    samples = local_rows * 4
    part = local_params // 2
    everyone = ("row", "col", "half")
    row, col, half = (lax.axis_index(name) for name in everyone)
    side = (row >= 2).astype(jnp.int32)
    bits = jnp.stack([side, half, jnp.bitwise_xor(col, side)]).astype(jnp.int32)

    to_centre = [(1, 2), (2, 1)]
    to_own = [(0, 1), (3, 2)]
    to_far = [(0, 2), (3, 1)]
    centres = [(r * 2 + h, r * 2 + 1 - h) for r in (1, 2) for h in (0, 1)]

    def swap(value):
        return lax.ppermute(value, ("row", "half"), centres)

    def send(value, blocks):
        return lax.ppermute(value.astype(jnp.float16), everyone, round_pairs(blocks))

    far, head, tail = pl.pallas_call(
        far_kernel,
        out_shape=[
            shape_of((local_rows, part), jnp.bfloat16),
            shape_of((HEAD, part), jnp.bfloat16),
            shape_of((local_rows - HEAD, part), jnp.bfloat16),
        ],
        in_specs=[SMEM, ANY],
        out_specs=[ANY] * 3,
        scratch_shapes=[pltpu.SemaphoreType.DMA((3,))],
        compiler_params=LIMIT,
    )(bits, log_derivs)
    from_centre = lax.ppermute(far, "row", to_centre)
    from_head = lax.ppermute(head, "row", to_far)
    near, sums = pl.pallas_call(
        near_kernel,
        out_shape=[
            shape_of((local_rows + EXTRA, part), jnp.bfloat16),
            shape_of((2, part), jnp.float32),
        ],
        in_specs=[SMEM, VMEM],
        out_specs=[VMEM] * 2,
        compiler_params=LIMIT,
    )(bits, log_derivs)
    from_edge = lax.ppermute(near, "row", to_own)
    from_tail = lax.ppermute(tail, "row", to_far)
    pieces = from_edge[local_rows : local_rows + EXTRA].astype(jnp.float32)
    passed_on = sums[1:2] + pieces[3:4] + pieces[4:5] + pieces[5:6]
    arrived_sum = lax.ppermute(passed_on, "row", to_centre)

    early_blocks = (3, local_rows, local_rows)
    centred, mean, own, other = pl.pallas_call(
        early_kernel,
        out_shape=[
            shape_of((3, local_rows, part), jnp.bfloat16),
            shape_of((1, part), jnp.float32),
            shape_of(early_blocks, jnp.float32),
            shape_of(early_blocks, jnp.float32),
        ],
        in_specs=[SMEM] + [VMEM] * 5,
        out_specs=[VMEM] * 4,
        scratch_shapes=[pltpu.VMEM((2,) + early_blocks, jnp.float32)],
        compiler_params=LIMIT,
    )(bits, from_edge, near, from_centre, sums, arrived_sum)
    early = combine(bits, own, swap(other), (1, 2), EARLY_HELD, EARLY, samples)
    arrived = [send(early[0], EARLY[0])]

    late_blocks = (2, local_rows, local_rows)
    waiting = early[1:]
    own, other, *waiting = pl.pallas_call(
        late_kernel,
        out_shape=[
            shape_of(late_blocks, jnp.float32),
            shape_of(late_blocks, jnp.float32),
        ]
        + [shape_of(value.shape, value.dtype) for value in waiting],
        in_specs=[SMEM] + [VMEM] * 4 + [ANY] * len(waiting),
        out_specs=[VMEM] * 2 + [ANY] * len(waiting),
        scratch_shapes=[
            pltpu.VMEM((local_rows, part), jnp.bfloat16),
            pltpu.VMEM((2,) + late_blocks, jnp.float32),
        ],
        input_output_aliases={5 + i: 2 + i for i in range(len(waiting))},
        compiler_params=LIMIT,
    )(bits, from_head, from_tail, mean, centred, *waiting)
    other = swap(other)
    arrived += [send(value, blocks) for value, blocks in zip(waiting, EARLY[1:])]
    late = combine(bits, own, other, (0, 1), LATE_HELD, LATE, samples)
    arrived += [send(value, blocks) for value, blocks in zip(late, LATE)]
    summed = sum(block.astype(jnp.float32) for block in arrived)
    return add_shift(summed, 1, shift, local_rows)


def solution(mesh):
    shape = mesh.shape
    small = shape["row"] == 4 and shape["col"] == 2 and shape["half"] == 2
    return jax.shard_map(
        two_centres if small else gathered,
        mesh=mesh,
        in_specs=(P(("groups", "row"), ("col", "half")), P("groups")),
        out_specs=P(("groups", "row"), ("col", "half")),
        check_vma=False,
    )
```

```python
import functools

import jax
import jax.numpy as jnp
from jax import lax
from jax.experimental import pallas as pl
from jax.experimental.pallas import tpu as pltpu
from jax.sharding import PartitionSpec as P


def pair_product(left, right):
    return jnp.einsum("ip,jp->ij", left, right, preferred_element_type=jnp.float32)


def add_shift(summed, samples, shift, local_rows):
    width = summed.shape[1]
    first_row = lax.axis_index("row") * local_rows
    block = lax.axis_index("col") * lax.axis_size("half") + lax.axis_index("half")
    row_ids = first_row + lax.broadcasted_iota(jnp.int32, (local_rows, width), 0)
    column_ids = block * width + lax.broadcasted_iota(jnp.int32, (local_rows, width), 1)
    return summed / samples + jnp.where(row_ids == column_ids, shift[0], 0.0)


def gathered(log_derivs, shift):
    local_rows = log_derivs.shape[0]
    samples = local_rows * lax.axis_size("row")
    rows = lax.all_gather(log_derivs, "row", axis=0, tiled=True).astype(jnp.float32)
    mean = jnp.sum(rows, axis=0) / samples
    centered = (rows - mean[None, :]).astype(jnp.bfloat16)
    own = (log_derivs.astype(jnp.float32) - mean[None, :]).astype(jnp.bfloat16)
    tile = pair_product(own, centered)
    summed = lax.psum_scatter(tile, ("col", "half"), scatter_dimension=1, tiled=True)
    return add_shift(summed, samples, shift, local_rows)


NEAR_ROUNDS = (
    (((0, 0), (0, 1)), ((0, 2), (1, 2))),
    (((0, 1), (0, 0)), ((1, 2), (0, 2))),
    (((1, 0), (1, 1)), (None, None)),
    (((1, 1), (1, 0)), (None, None)),
)
FAR_ROUNDS = (
    ((None, None), ((2, 0), (2, 2))),
    ((None, None), ((2, 2), (2, 0))),
)
LATE_ROUNDS = (
    (((3, 0), (3, 1)), ((3, 2), (3, 3))),
    (((3, 1), (3, 0)), ((3, 3), (3, 2))),
    (((0, 3), (1, 3)), ((2, 3), (2, 1))),
    (((1, 3), (0, 3)), ((2, 1), (2, 3))),
)
EARLY_SUMS = (((0, 0), (0, 1), (1, 1)), ((2, 2), (2, 0), (2, 1)))
EARLY_HELD = (
    ((0, 0), (0, 1), (1, 1), (1, 0), (1, 1)),
    ((2, 2), (2, 0), (2, 1), (0, 2), (1, 2)),
)
SPARE = 2
LATE_SUMS = (((3, 0), (3, 1)), ((3, 2), (3, 3)))
LATE_HELD = (
    ((3, 0), (3, 1), (0, 3), (1, 3), (1, 1)),
    ((3, 2), (3, 3), (2, 3), (3, 3), (2, 1)),
)
EXTRA = 16
VMEM = pl.BlockSpec(memory_space=pltpu.VMEM)
SMEM = pl.BlockSpec(memory_space=pltpu.SMEM)
ANY = pl.BlockSpec(memory_space=pl.ANY)
LIMIT = pltpu.CompilerParams(vmem_limit_bytes=40 * 2**20)
BRIEF = pl.CostEstimate(flops=1024, bytes_accessed=1024, transcendentals=0)


def device_index(row, col, half):
    return (row * 2 + col) * 2 + half


def round_pairs(blocks):
    pairs = []
    for side in (0, 1):
        for turn in (0, 1):
            for half in (0, 1):
                block = blocks[half][turn]
                if block is None:
                    continue
                i, j = (3 - b if side else b for b in block)
                source = device_index(1 + side, turn ^ side, half)
                pairs.append((source, device_index(i, j // 2, j % 2)))
    return pairs


def held_place(held, rounds):
    return [
        [[0 if b is None else held[half].index(b) for b in rounds_[half]] for half in (0, 1)]
        for rounds_ in rounds
    ]


def split_kernel(bits, values, near, far, sums, sems):
    rows, part = far.shape
    step = 512
    copies = []
    for i, (out, start) in enumerate(((near, 1 - bits[0]), (far, bits[0]))):
        columns = pl.ds(pl.multiple_of(start * part, 128), part)
        copies.append(
            pltpu.make_async_copy(values.at[:, columns], out.at[pl.ds(0, rows), :], sems.at[i])
        )
    for copy in copies:
        copy.start()
    for i, (copy, out) in enumerate(zip(copies, (near, far))):
        copy.wait()

        @pl.loop(0, part // step)
        def _(j):
            columns = pl.ds(pl.multiple_of(j * step, step), step)
            block = out[pl.ds(0, rows), columns].astype(jnp.float32)
            sums[pl.ds(i, 1), columns] = jnp.sum(block, axis=0, keepdims=True)

    pieces = []
    for i in (0, 1):
        left = sums[pl.ds(i, 1), :]
        for _ in range(3):
            piece = left.astype(jnp.bfloat16).astype(jnp.float32)
            pieces.append(piece)
            left = left - piece
    pieces.append(jnp.zeros((EXTRA - len(pieces), part), jnp.float32))
    near[pl.ds(rows, EXTRA), :] = jnp.concatenate(pieces, axis=0).astype(jnp.bfloat16)


def block_product(left, right):
    return lax.dot_general(left, right, (((1,), (1,)), ((), ())), preferred_element_type=jnp.float32)


def early_kernel(bits, edge, near, other, sums, arrived, centred, mean, own, *rest):
    sends, both = rest[:-1], rest[-1]
    rows = other.shape[0]
    pieces = edge[pl.ds(rows, EXTRA), :].astype(jnp.float32)
    edge_sum = pieces[0:1] + pieces[1:2] + pieces[2:3]
    average = (sums[pl.ds(0, 1), :] + edge_sum + arrived[...]) * (1.0 / (4 * rows))
    mean[...] = average
    for i, block in enumerate((edge, near, other)):
        values = block[pl.ds(0, rows), :].astype(jnp.float32)
        centred[i] = (values - average).astype(jnp.bfloat16)
    for core in (0, 1):
        for place, (i, j) in enumerate(EARLY_SUMS[core]):
            both[core, place] = block_product(centred[i], centred[j])
    own[...] = both[bits[1]]
    for place, send in enumerate(sends):
        send[...] = both[1 - bits[1], place]


def late_kernel(bits, far_edge, mean, centred, *rest):
    handed = (len(rest) - 5) // 2
    own, *sends = rest[handed : handed + 3]
    last, both = rest[-2:]
    last[...] = (far_edge[...].astype(jnp.float32) - mean[...]).astype(jnp.bfloat16)
    for core in (0, 1):
        for place, (_, j) in enumerate(LATE_SUMS[core]):
            both[core, place] = block_product(last[...], last[...] if j == 3 else centred[j])
    own[...] = both[bits[1]]
    for place, send in enumerate(sends):
        send[...] = both[1 - bits[1], place]


def combine_kernel(flips, scale, spares, bits, places, own, *rest):
    held = rest[-1]
    count = own.shape[0]
    for i in range(count):
        held[i] = (own[i] + rest[i][...]) * scale
    rest = rest[count:]
    for n, i in enumerate(flips):
        held[count + n] = held[i].T
    for i in range(spares):
        held[count + len(flips) + i] = rest[i][...]
    for r, out in enumerate(rest[spares:-1]):
        out[...] = held[places[r, bits[1], bits[2]]]


def shape_of(shape, dtype):
    return jax.ShapeDtypeStruct(shape, dtype)


def combine(bits, own, others, flips, spares, held, places, samples):
    rows = own.shape[1]
    return pl.pallas_call(
        functools.partial(combine_kernel, flips, 1.0 / samples, len(spares)),
        out_shape=[shape_of((rows, rows), jnp.float32)] * len(places),
        in_specs=[SMEM, SMEM] + [VMEM] * (1 + len(others) + len(spares)),
        out_specs=[VMEM] * len(places),
        scratch_shapes=[pltpu.VMEM((len(held[0]), rows, rows), jnp.float32)],
        compiler_params=LIMIT,
        cost_estimate=BRIEF,
    )(bits, jnp.array(places, jnp.int32), own, *others, *spares)


def two_centres(log_derivs, shift):
    local_rows, local_params = log_derivs.shape
    samples = local_rows * 4
    part = local_params // 2
    everyone = ("row", "col", "half")
    row, col, half = (lax.axis_index(name) for name in everyone)
    side = (row >= 2).astype(jnp.int32)
    bits = jnp.stack([side, half, jnp.bitwise_xor(col, side)]).astype(jnp.int32)

    to_centre = [(1, 2), (2, 1)]
    to_own = [(0, 1), (3, 2)]
    to_far = [(0, 2), (3, 1)]
    centres = [(r * 2 + h, r * 2 + 1 - h) for r in (1, 2) for h in (0, 1)]

    def swap(value):
        return lax.ppermute(value, ("row", "half"), centres)

    def send(value, blocks):
        return lax.ppermute(value.astype(jnp.float16), everyone, round_pairs(blocks))

    near, far, sums = pl.pallas_call(
        split_kernel,
        out_shape=[
            shape_of((local_rows + EXTRA, part), jnp.bfloat16),
            shape_of((local_rows, part), jnp.bfloat16),
            shape_of((2, part), jnp.float32),
        ],
        in_specs=[SMEM, ANY],
        out_specs=[VMEM] * 3,
        scratch_shapes=[pltpu.SemaphoreType.DMA((2,))],
        compiler_params=LIMIT,
        cost_estimate=BRIEF,
    )(bits, log_derivs)
    from_centre = lax.ppermute(far, "row", to_centre)
    from_edge = lax.ppermute(near, "row", to_own)
    from_far_edge = lax.ppermute(far, "row", to_far)
    pieces = from_edge[local_rows : local_rows + EXTRA].astype(jnp.float32)
    passed_on = sums[1:2] + pieces[3:4] + pieces[4:5] + pieces[5:6]
    arrived_sum = lax.ppermute(passed_on, "row", to_centre)

    block = shape_of((local_rows, local_rows), jnp.float32)
    early_blocks = (3, local_rows, local_rows)
    centred, mean, own, *others = pl.pallas_call(
        early_kernel,
        out_shape=[
            shape_of((3, local_rows, part), jnp.bfloat16),
            shape_of((1, part), jnp.float32),
            shape_of(early_blocks, jnp.float32),
        ]
        + [block] * 3,
        in_specs=[SMEM] + [VMEM] * 5,
        out_specs=[VMEM] * 6,
        scratch_shapes=[pltpu.VMEM((2,) + early_blocks, jnp.float32)],
        compiler_params=LIMIT,
        cost_estimate=BRIEF,
    )(bits, from_edge, near, from_centre, sums, arrived_sum)
    places = held_place(EARLY_HELD, NEAR_ROUNDS + FAR_ROUNDS) + [[[SPARE] * 2] * 2]
    others = [swap(other) for other in others]
    *early, spare = combine(bits, own, others, (1, 2), (), EARLY_HELD, places, samples)
    near_blocks, far_blocks = early[: len(NEAR_ROUNDS)], early[len(NEAR_ROUNDS) :]
    arrived = [send(value, blocks) for value, blocks in zip(near_blocks, NEAR_ROUNDS)]
    summed = sum(block.astype(jnp.float32) for block in arrived)

    late_blocks = (2, local_rows, local_rows)
    handed = [summed] + far_blocks
    own, *others, summed, first, second = pl.pallas_call(
        late_kernel,
        out_shape=[shape_of(late_blocks, jnp.float32)]
        + [block] * 2
        + [shape_of(value.shape, value.dtype) for value in handed],
        in_specs=[SMEM] + [VMEM] * 3 + [ANY] * len(handed),
        out_specs=[VMEM] * 3 + [ANY] * len(handed),
        scratch_shapes=[
            pltpu.VMEM((local_rows, part), jnp.bfloat16),
            pltpu.VMEM((2,) + late_blocks, jnp.float32),
        ],
        input_output_aliases={4 + i: 3 + i for i in range(len(handed))},
        compiler_params=LIMIT,
        cost_estimate=BRIEF,
    )(bits, from_far_edge, mean, centred, *handed)
    others = [swap(other) for other in others]
    arrived = [send(value, blocks) for value, blocks in zip((first, second), FAR_ROUNDS)]
    places = held_place(LATE_HELD, LATE_ROUNDS)
    late = combine(bits, own, others, (0, 1), (spare,), LATE_HELD, places, samples)
    arrived += [send(value, blocks) for value, blocks in zip(late, LATE_ROUNDS)]
    summed = summed + sum(block.astype(jnp.float32) for block in arrived)
    return add_shift(summed, 1, shift, local_rows)


def solution(mesh):
    shape = mesh.shape
    small = shape["row"] == 4 and shape["col"] == 2 and shape["half"] == 2
    return jax.shard_map(
        two_centres if small else gathered,
        mesh=mesh,
        in_specs=(P(("groups", "row"), ("col", "half")), P("groups")),
        out_specs=P(("groups", "row"), ("col", "half")),
        check_vma=False,
    )
```

```python
import functools

import jax
import jax.numpy as jnp
from jax import lax
from jax.experimental import pallas as pl
from jax.experimental.pallas import tpu as pltpu
from jax.sharding import PartitionSpec as P


def pair_product(left, right):
    return jnp.einsum("ip,jp->ij", left, right, preferred_element_type=jnp.float32)


def add_shift(summed, samples, shift, local_rows):
    width = summed.shape[1]
    first_row = lax.axis_index("row") * local_rows
    block = lax.axis_index("col") * lax.axis_size("half") + lax.axis_index("half")
    row_ids = first_row + lax.broadcasted_iota(jnp.int32, (local_rows, width), 0)
    column_ids = block * width + lax.broadcasted_iota(jnp.int32, (local_rows, width), 1)
    return summed / samples + jnp.where(row_ids == column_ids, shift[0], 0.0)


def gathered(log_derivs, shift):
    local_rows = log_derivs.shape[0]
    samples = local_rows * lax.axis_size("row")
    rows = lax.all_gather(log_derivs, "row", axis=0, tiled=True).astype(jnp.float32)
    mean = jnp.sum(rows, axis=0) / samples
    centered = (rows - mean[None, :]).astype(jnp.bfloat16)
    own = (log_derivs.astype(jnp.float32) - mean[None, :]).astype(jnp.bfloat16)
    tile = pair_product(own, centered)
    summed = lax.psum_scatter(tile, ("col", "half"), scatter_dimension=1, tiled=True)
    return add_shift(summed, samples, shift, local_rows)


NEAR_ROUNDS = (
    (((0, 0), (0, 1)), ((0, 2), (1, 2))),
    (((0, 1), (0, 0)), ((1, 2), (0, 2))),
    (((1, 0), (1, 1)), (None, None)),
    (((1, 1), (1, 0)), (None, None)),
)
FAR_ROUNDS = (
    ((None, None), ((2, 0), (2, 2))),
    ((None, None), ((2, 2), (2, 0))),
)
LATE_ROUNDS = (
    (((3, 0), (3, 1)), ((3, 2), (3, 3))),
    (((3, 1), (3, 0)), ((3, 3), (3, 2))),
    (((0, 3), (1, 3)), ((2, 3), (2, 1))),
    (((1, 3), (0, 3)), ((2, 1), (2, 3))),
)
EARLY_SUMS = (((0, 0), (0, 1), (1, 1)), ((2, 2), (2, 0), (2, 1)))
EARLY_HELD = (
    ((0, 0), (0, 1), (1, 1), (1, 0), (1, 1)),
    ((2, 2), (2, 0), (2, 1), (0, 2), (1, 2)),
)
SPARE = 2
LATE_SUMS = (((3, 0), (3, 1)), ((3, 2), (3, 3)))
LATE_HELD = (
    ((3, 0), (3, 1), (0, 3), (1, 3), (1, 1)),
    ((3, 2), (3, 3), (2, 3), (3, 3), (2, 1)),
)
EXTRA = 16
HEAD = 64
VMEM = pl.BlockSpec(memory_space=pltpu.VMEM)
SMEM = pl.BlockSpec(memory_space=pltpu.SMEM)
ANY = pl.BlockSpec(memory_space=pl.ANY)
HBM = pl.BlockSpec(memory_space=pltpu.HBM)
LIMIT = pltpu.CompilerParams(vmem_limit_bytes=40 * 2**20)
BRIEF = pl.CostEstimate(flops=1024, bytes_accessed=1024, transcendentals=0)


def device_index(row, col, half):
    return (row * 2 + col) * 2 + half


def round_pairs(blocks):
    pairs = []
    for side in (0, 1):
        for turn in (0, 1):
            for half in (0, 1):
                block = blocks[half][turn]
                if block is None:
                    continue
                i, j = (3 - b if side else b for b in block)
                source = device_index(1 + side, turn ^ side, half)
                pairs.append((source, device_index(i, j // 2, j % 2)))
    return pairs


def held_place(held, rounds):
    return [
        [[0 if b is None else held[half].index(b) for b in rounds_[half]] for half in (0, 1)]
        for rounds_ in rounds
    ]


def split_kernel(bits, values, near, far, head, tail, sums, sems):
    rows, part = far.shape
    step = 512
    near_columns = pl.ds(pl.multiple_of((1 - bits[0]) * part, 128), part)
    far_columns = pl.ds(pl.multiple_of(bits[0] * part, 128), part)
    first, rest = pl.ds(0, HEAD), pl.ds(HEAD, rows - HEAD)
    copies = [
        pltpu.make_async_copy(values.at[:, far_columns], far, sems.at[0]),
        pltpu.make_async_copy(values.at[:, near_columns], near, sems.at[1]),
        pltpu.make_async_copy(
            values.at[first, far_columns], head.at[pl.ds(EXTRA, HEAD), :], sems.at[2]
        ),
        pltpu.make_async_copy(values.at[rest, far_columns], tail, sems.at[3]),
    ]
    for copy in copies:
        copy.start()
    copies[0].wait()

    @pl.loop(0, part // step)
    def _(j):
        columns = pl.ds(pl.multiple_of(j * step, step), step)
        left = jnp.sum(far[:, columns].astype(jnp.float32), axis=0, keepdims=True)
        for i in range(3):
            piece = left.astype(jnp.bfloat16).astype(jnp.float32)
            sums[pl.ds(i, 1), columns] = piece
            left = left - piece
        sums[pl.ds(3, EXTRA - 3), columns] = jnp.zeros((EXTRA - 3, step), jnp.float32)

    head[pl.ds(0, EXTRA), :] = sums[...].astype(jnp.bfloat16)
    for copy in copies[1:]:
        copy.wait()


def block_product(left, right):
    return lax.dot_general(left, right, (((1,), (1,)), ((), ())), preferred_element_type=jnp.float32)


def early_kernel(bits, edge, near, other, head, centred, mean, own, *rest):
    sends, both = rest[:-1], rest[-1]
    rows, part = near.shape
    step = 512

    @pl.loop(0, part // step)
    def _(n):
        columns = pl.ds(pl.multiple_of(n * step, step), step)
        values = [block[:, columns].astype(jnp.float32) for block in (edge, near, other)]
        total = jnp.sum(head[pl.ds(0, EXTRA), columns].astype(jnp.float32), axis=0, keepdims=True)
        total = total + jnp.sum(values[0] + values[1] + values[2], axis=0, keepdims=True)
        average = total * (1.0 / (4 * rows))
        mean[:, columns] = average
        for i in range(3):
            centred[i, :, columns] = (values[i] - average).astype(jnp.bfloat16)

    for core in (0, 1):
        for place, (i, j) in enumerate(EARLY_SUMS[core]):
            both[core, place] = block_product(centred[i], centred[j])
    own[...] = both[bits[1]]
    for place, send in enumerate(sends):
        send[...] = both[1 - bits[1], place]


def late_kernel(bits, head, tail, mean, centred, *rest):
    handed = (len(rest) - 5) // 2
    own, *sends = rest[handed : handed + 3]
    last, both = rest[-2:]
    rows = last.shape[0]
    first = head[pl.ds(EXTRA, HEAD), :].astype(jnp.float32) - mean[...]
    last[pl.ds(0, HEAD), :] = first.astype(jnp.bfloat16)
    second = tail[...].astype(jnp.float32) - mean[...]
    last[pl.ds(HEAD, rows - HEAD), :] = second.astype(jnp.bfloat16)
    for core in (0, 1):
        for place, (_, j) in enumerate(LATE_SUMS[core]):
            both[core, place] = block_product(last[...], last[...] if j == 3 else centred[j])
    own[...] = both[bits[1]]
    for place, send in enumerate(sends):
        send[...] = both[1 - bits[1], place]


def combine_kernel(flips, scale, spares, bits, places, own, *rest):
    held = rest[-1]
    count = own.shape[0]
    for i in range(count):
        held[i] = (own[i] + rest[i][...]) * scale
    rest = rest[count:]
    for n, i in enumerate(flips):
        held[count + n] = held[i].T
    for i in range(spares):
        held[count + len(flips) + i] = rest[i][...]
    for r, out in enumerate(rest[spares:-1]):
        out[...] = held[places[r, bits[1], bits[2]]]


def shape_of(shape, dtype):
    return jax.ShapeDtypeStruct(shape, dtype)


def combine(bits, own, others, flips, spares, held, places, samples):
    rows = own.shape[1]
    return pl.pallas_call(
        functools.partial(combine_kernel, flips, 1.0 / samples, len(spares)),
        out_shape=[shape_of((rows, rows), jnp.float32)] * len(places),
        in_specs=[SMEM, SMEM] + [VMEM] * (1 + len(others) + len(spares)),
        out_specs=[VMEM] * len(places),
        scratch_shapes=[pltpu.VMEM((len(held[0]), rows, rows), jnp.float32)],
        compiler_params=LIMIT,
        cost_estimate=BRIEF,
    )(bits, jnp.array(places, jnp.int32), own, *others, *spares)


def two_centres(log_derivs, shift):
    local_rows, local_params = log_derivs.shape
    samples = local_rows * 4
    part = local_params // 2
    everyone = ("row", "col", "half")
    row, col, half = (lax.axis_index(name) for name in everyone)
    side = (row >= 2).astype(jnp.int32)
    bits = jnp.stack([side, half, jnp.bitwise_xor(col, side)]).astype(jnp.int32)

    to_centre = [(1, 2), (2, 1)]
    to_own = [(0, 1), (3, 2)]
    to_far = [(0, 2), (3, 1)]
    centres = [(r * 2 + h, r * 2 + 1 - h) for r in (1, 2) for h in (0, 1)]

    def swap(value):
        return lax.ppermute(value, ("row", "half"), centres)

    def send(value, blocks):
        return lax.ppermute(value.astype(jnp.float16), everyone, round_pairs(blocks))

    near, far, head, tail = pl.pallas_call(
        split_kernel,
        out_shape=[
            shape_of((local_rows, part), jnp.bfloat16),
            shape_of((local_rows, part), jnp.bfloat16),
            shape_of((EXTRA + HEAD, part), jnp.bfloat16),
            shape_of((local_rows - HEAD, part), jnp.bfloat16),
        ],
        in_specs=[SMEM, HBM],
        out_specs=[VMEM] * 4,
        scratch_shapes=[pltpu.VMEM((EXTRA, part), jnp.float32), pltpu.SemaphoreType.DMA((4,))],
        compiler_params=LIMIT,
        cost_estimate=BRIEF,
    )(bits, log_derivs)
    from_centre = lax.ppermute(far, "row", to_centre)
    from_edge = lax.ppermute(near, "row", to_own)
    from_head = lax.ppermute(head, "row", to_far)
    from_tail = lax.ppermute(tail, "row", to_far)

    block = shape_of((local_rows, local_rows), jnp.float32)
    early_blocks = (3, local_rows, local_rows)
    centred, mean, own, *others = pl.pallas_call(
        early_kernel,
        out_shape=[
            shape_of((3, local_rows, part), jnp.bfloat16),
            shape_of((1, part), jnp.float32),
            shape_of(early_blocks, jnp.float32),
        ]
        + [block] * 3,
        in_specs=[SMEM] + [VMEM] * 4,
        out_specs=[VMEM] * 6,
        scratch_shapes=[pltpu.VMEM((2,) + early_blocks, jnp.float32)],
        compiler_params=LIMIT,
        cost_estimate=BRIEF,
    )(bits, from_edge, near, from_centre, from_head)
    places = held_place(EARLY_HELD, NEAR_ROUNDS + FAR_ROUNDS) + [[[SPARE] * 2] * 2]
    others = [swap(other) for other in others]
    *early, spare = combine(bits, own, others, (1, 2), (), EARLY_HELD, places, samples)
    near_blocks, far_blocks = early[: len(NEAR_ROUNDS)], early[len(NEAR_ROUNDS) :]
    arrived = [send(value, blocks) for value, blocks in zip(near_blocks, NEAR_ROUNDS)]
    summed = sum(block.astype(jnp.float32) for block in arrived)

    late_blocks = (2, local_rows, local_rows)
    handed = [summed] + far_blocks
    own, *others, summed, first, second = pl.pallas_call(
        late_kernel,
        out_shape=[shape_of(late_blocks, jnp.float32)]
        + [block] * 2
        + [shape_of(value.shape, value.dtype) for value in handed],
        in_specs=[SMEM] + [VMEM] * 4 + [ANY] * len(handed),
        out_specs=[VMEM] * 3 + [ANY] * len(handed),
        scratch_shapes=[
            pltpu.VMEM((local_rows, part), jnp.bfloat16),
            pltpu.VMEM((2,) + late_blocks, jnp.float32),
        ],
        input_output_aliases={5 + i: 3 + i for i in range(len(handed))},
        compiler_params=LIMIT,
        cost_estimate=BRIEF,
    )(bits, from_head, from_tail, mean, centred, *handed)
    others = [swap(other) for other in others]
    arrived = [send(value, blocks) for value, blocks in zip((first, second), FAR_ROUNDS)]
    places = held_place(LATE_HELD, LATE_ROUNDS)
    late = combine(bits, own, others, (0, 1), (spare,), LATE_HELD, places, samples)
    arrived += [send(value, blocks) for value, blocks in zip(late, LATE_ROUNDS)]
    summed = summed + sum(block.astype(jnp.float32) for block in arrived)
    return add_shift(summed, 1, shift, local_rows)


def solution(mesh):
    shape = mesh.shape
    small = shape["row"] == 4 and shape["col"] == 2 and shape["half"] == 2
    return jax.shard_map(
        two_centres if small else gathered,
        mesh=mesh,
        in_specs=(P(("groups", "row"), ("col", "half")), P("groups")),
        out_specs=P(("groups", "row"), ("col", "half")),
        check_vma=False,
    )
```

```python
import functools

import jax
import jax.numpy as jnp
from jax import lax
from jax.experimental import pallas as pl
from jax.experimental.pallas import tpu as pltpu
from jax.sharding import PartitionSpec as P


def pair_product(left, right):
    return jnp.einsum("ip,jp->ij", left, right, preferred_element_type=jnp.float32)


def add_shift(summed, samples, shift, local_rows):
    width = summed.shape[1]
    first_row = lax.axis_index("row") * local_rows
    block = lax.axis_index("col") * lax.axis_size("half") + lax.axis_index("half")
    row_ids = first_row + lax.broadcasted_iota(jnp.int32, (local_rows, width), 0)
    column_ids = block * width + lax.broadcasted_iota(jnp.int32, (local_rows, width), 1)
    return summed / samples + jnp.where(row_ids == column_ids, shift[0], 0.0)


def gathered(log_derivs, shift):
    local_rows = log_derivs.shape[0]
    samples = local_rows * lax.axis_size("row")
    rows = lax.all_gather(log_derivs, "row", axis=0, tiled=True).astype(jnp.float32)
    mean = jnp.sum(rows, axis=0) / samples
    centered = (rows - mean[None, :]).astype(jnp.bfloat16)
    own = (log_derivs.astype(jnp.float32) - mean[None, :]).astype(jnp.bfloat16)
    tile = pair_product(own, centered)
    summed = lax.psum_scatter(tile, ("col", "half"), scatter_dimension=1, tiled=True)
    return add_shift(summed, samples, shift, local_rows)


NEAR_ROUNDS = (
    (((0, 0), (0, 1)), ((0, 2), (1, 2))),
    (((0, 1), (0, 0)), ((1, 2), (0, 2))),
    (((1, 0), (1, 1)), (None, None)),
    (((1, 1), (1, 0)), (None, None)),
)
FAR_ROUNDS = (
    ((None, None), ((2, 0), (2, 2))),
    ((None, None), ((2, 2), (2, 0))),
)
LATE_ROUNDS = (
    (((3, 0), (3, 1)), ((3, 2), (3, 3))),
    (((3, 1), (3, 0)), ((3, 3), (3, 2))),
    (((0, 3), (1, 3)), ((2, 3), (2, 1))),
    (((1, 3), (0, 3)), ((2, 1), (2, 3))),
)
EARLY_SUMS = (((0, 0), (0, 1), (1, 1)), ((2, 2), (2, 0), (2, 1)))
EARLY_HELD = (
    ((0, 0), (0, 1), (1, 1), (1, 0), (1, 1)),
    ((2, 2), (2, 0), (2, 1), (0, 2), (1, 2)),
)
LATE_SUMS = (((3, 0), (3, 1)), ((3, 2), (3, 3)))
LATE_HELD = (
    ((3, 0), (3, 1), (0, 3), (1, 3)) + EARLY_SUMS[0],
    ((3, 2), (3, 3), (2, 3), (3, 3)) + EARLY_SUMS[1],
)
EXTRA = 16
HEAD = 64
VMEM = pl.BlockSpec(memory_space=pltpu.VMEM)
SMEM = pl.BlockSpec(memory_space=pltpu.SMEM)
ANY = pl.BlockSpec(memory_space=pl.ANY)
HBM = pl.BlockSpec(memory_space=pltpu.HBM)
LIMIT = pltpu.CompilerParams(vmem_limit_bytes=40 * 2**20)
BRIEF = pl.CostEstimate(flops=1024, bytes_accessed=1024, transcendentals=0)


def device_index(row, col, half):
    return (row * 2 + col) * 2 + half


def round_pairs(blocks):
    pairs = []
    for side in (0, 1):
        for turn in (0, 1):
            for half in (0, 1):
                block = blocks[half][turn]
                if block is None:
                    continue
                i, j = (3 - b if side else b for b in block)
                source = device_index(1 + side, turn ^ side, half)
                pairs.append((source, device_index(i, j // 2, j % 2)))
    return pairs


def held_place(held, rounds):
    return [
        [[0 if b is None else held[half].index(b) for b in rounds_[half]] for half in (0, 1)]
        for rounds_ in rounds
    ]


def split_kernel(bits, values, near, far, head, tail, sums, sems):
    rows, part = far.shape
    step = 512
    near_columns = pl.ds(pl.multiple_of((1 - bits[0]) * part, 128), part)
    far_columns = pl.ds(pl.multiple_of(bits[0] * part, 128), part)
    first, rest = pl.ds(0, HEAD), pl.ds(HEAD, rows - HEAD)
    copies = [
        pltpu.make_async_copy(values.at[:, far_columns], far, sems.at[0]),
        pltpu.make_async_copy(values.at[:, near_columns], near, sems.at[1]),
        pltpu.make_async_copy(
            values.at[first, far_columns], head.at[pl.ds(EXTRA, HEAD), :], sems.at[2]
        ),
        pltpu.make_async_copy(values.at[rest, far_columns], tail, sems.at[3]),
    ]
    for copy in copies:
        copy.start()
    copies[0].wait()

    @pl.loop(0, part // step)
    def _(j):
        columns = pl.ds(pl.multiple_of(j * step, step), step)
        left = jnp.sum(far[:, columns].astype(jnp.float32), axis=0, keepdims=True)
        for i in range(3):
            piece = left.astype(jnp.bfloat16).astype(jnp.float32)
            sums[pl.ds(i, 1), columns] = piece
            left = left - piece
        sums[pl.ds(3, EXTRA - 3), columns] = jnp.zeros((EXTRA - 3, step), jnp.float32)

    head[pl.ds(0, EXTRA), :] = sums[...].astype(jnp.bfloat16)
    for copy in copies[1:]:
        copy.wait()


def block_product(left, right):
    return lax.dot_general(left, right, (((1,), (1,)), ((), ())), preferred_element_type=jnp.float32)


def early_kernel(bits, other, edge, head, near, centred, mean, own, *rest):
    sends, both = rest[:-1], rest[-1]
    rows, part = near.shape
    step = 512

    @pl.loop(0, part // step)
    def _(n):
        columns = pl.ds(pl.multiple_of(n * step, step), step)
        values = [block[:, columns].astype(jnp.float32) for block in (edge, near, other)]
        total = jnp.sum(head[pl.ds(0, EXTRA), columns].astype(jnp.float32), axis=0, keepdims=True)
        total = total + jnp.sum(values[0] + values[1] + values[2], axis=0, keepdims=True)
        average = total * (1.0 / (4 * rows))
        mean[:, columns] = average
        for i in range(3):
            centred[i, :, columns] = (values[i] - average).astype(jnp.bfloat16)

    for core in (0, 1):
        for place, (i, j) in enumerate(EARLY_SUMS[core]):
            both[core, place] = block_product(centred[i], centred[j])
    own[...] = both[bits[1]]
    for place, send in enumerate(sends):
        send[...] = both[1 - bits[1], place]


def late_kernel(bits, head, tail, mean, centred, summed, own, send, summed_out, last, both):
    rows = last.shape[0]
    first = head[pl.ds(EXTRA, HEAD), :].astype(jnp.float32) - mean[...]
    last[pl.ds(0, HEAD), :] = first.astype(jnp.bfloat16)
    second = tail[...].astype(jnp.float32) - mean[...]
    last[pl.ds(HEAD, rows - HEAD), :] = second.astype(jnp.bfloat16)
    for core in (0, 1):
        for place, (_, j) in enumerate(LATE_SUMS[core]):
            both[core, place] = block_product(last[...], last[...] if j == 3 else centred[j])
    own[...] = both[bits[1]]
    send[...] = both[1 - bits[1]]


def combine_kernel(flips, scale, pieces, spares, bits, places, own, *rest):
    others, spare = rest[:pieces], rest[pieces : pieces + spares]
    outs, held = rest[pieces + spares : -1], rest[-1]
    count = own.shape[0]
    for i in range(count):
        other = others[0][i] if pieces == 1 else others[i][...]
        held[i] = (own[i] + other) * scale
    for n, i in enumerate(flips):
        held[count + n] = held[i].T
    for i in range(spares):
        held[count + len(flips) + i] = spare[i][...]
    for r, out in enumerate(outs):
        out[...] = held[places[r, bits[1], bits[2]]]


def shape_of(shape, dtype):
    return jax.ShapeDtypeStruct(shape, dtype)


def combine(bits, own, others, flips, spares, held, places, samples):
    rows = own.shape[1]
    return pl.pallas_call(
        functools.partial(combine_kernel, flips, 1.0 / samples, len(others), len(spares)),
        out_shape=[shape_of((rows, rows), jnp.float32)] * len(places),
        in_specs=[SMEM, SMEM] + [VMEM] * (1 + len(others) + len(spares)),
        out_specs=[VMEM] * len(places),
        scratch_shapes=[pltpu.VMEM((len(held[0]), rows, rows), jnp.float32)],
        compiler_params=LIMIT,
        cost_estimate=BRIEF,
    )(bits, jnp.array(places, jnp.int32), own, *others, *spares)


def two_centres(log_derivs, shift):
    local_rows, local_params = log_derivs.shape
    samples = local_rows * 4
    part = local_params // 2
    everyone = ("row", "col", "half")
    row, col, half = (lax.axis_index(name) for name in everyone)
    side = (row >= 2).astype(jnp.int32)
    bits = jnp.stack([side, half, jnp.bitwise_xor(col, side)]).astype(jnp.int32)

    to_centre = [(1, 2), (2, 1)]
    to_own = [(0, 1), (3, 2)]
    to_far = [(0, 2), (3, 1)]
    centres = [(r * 2 + h, r * 2 + 1 - h) for r in (1, 2) for h in (0, 1)]

    def swap(value):
        return lax.ppermute(value, ("row", "half"), centres)

    def send(value, blocks):
        return lax.ppermute(value.astype(jnp.float16), everyone, round_pairs(blocks))

    near, far, head, tail = pl.pallas_call(
        split_kernel,
        out_shape=[
            shape_of((local_rows, part), jnp.bfloat16),
            shape_of((local_rows, part), jnp.bfloat16),
            shape_of((EXTRA + HEAD, part), jnp.bfloat16),
            shape_of((local_rows - HEAD, part), jnp.bfloat16),
        ],
        in_specs=[SMEM, HBM],
        out_specs=[VMEM] * 4,
        scratch_shapes=[pltpu.VMEM((EXTRA, part), jnp.float32), pltpu.SemaphoreType.DMA((4,))],
        compiler_params=LIMIT,
        cost_estimate=BRIEF,
    )(bits, log_derivs)
    from_centre = lax.ppermute(far, "row", to_centre)
    from_edge = lax.ppermute(near, "row", to_own)
    from_head = lax.ppermute(head, "row", to_far)
    from_tail = lax.ppermute(tail, "row", to_far)

    block = shape_of((local_rows, local_rows), jnp.float32)
    early_blocks = (3, local_rows, local_rows)
    centred, mean, own, *others = pl.pallas_call(
        early_kernel,
        out_shape=[
            shape_of((3, local_rows, part), jnp.bfloat16),
            shape_of((1, part), jnp.float32),
            shape_of(early_blocks, jnp.float32),
        ]
        + [block] * 3,
        in_specs=[SMEM] + [VMEM] * 4,
        out_specs=[VMEM] * 6,
        scratch_shapes=[pltpu.VMEM((2,) + early_blocks, jnp.float32)],
        compiler_params=LIMIT,
        cost_estimate=BRIEF,
    )(bits, from_centre, from_edge, from_head, near)
    others = [swap(other) for other in others]
    places = held_place(EARLY_HELD, NEAR_ROUNDS) + [[[i] * 2] * 2 for i in range(3)]
    early = combine(bits, own, others, (1, 2), (), EARLY_HELD, places, samples)
    near_blocks, spares = early[: len(NEAR_ROUNDS)], early[len(NEAR_ROUNDS) :]
    arrived = [send(value, blocks) for value, blocks in zip(near_blocks, NEAR_ROUNDS)]
    summed = sum(block.astype(jnp.float32) for block in arrived)

    late_blocks = shape_of((2, local_rows, local_rows), jnp.float32)
    own, other, summed = pl.pallas_call(
        late_kernel,
        out_shape=[late_blocks, late_blocks, shape_of(summed.shape, summed.dtype)],
        in_specs=[SMEM] + [VMEM] * 4 + [ANY],
        out_specs=[VMEM] * 2 + [ANY],
        scratch_shapes=[
            pltpu.VMEM((local_rows, part), jnp.bfloat16),
            pltpu.VMEM((2,) + late_blocks.shape, jnp.float32),
        ],
        input_output_aliases={5: 2},
        compiler_params=LIMIT,
        cost_estimate=BRIEF,
    )(bits, from_head, from_tail, mean, centred, summed)
    rounds = LATE_ROUNDS + FAR_ROUNDS
    places = held_place(LATE_HELD, rounds)
    late = combine(bits, own, [swap(other)], (0, 1), spares, LATE_HELD, places, samples)
    arrived = [send(value, blocks) for value, blocks in zip(late, rounds)]
    summed = summed + sum(block.astype(jnp.float32) for block in reversed(arrived))
    return add_shift(summed, 1, shift, local_rows)


def solution(mesh):
    shape = mesh.shape
    small = shape["row"] == 4 and shape["col"] == 2 and shape["half"] == 2
    return jax.shard_map(
        two_centres if small else gathered,
        mesh=mesh,
        in_specs=(P(("groups", "row"), ("col", "half")), P("groups")),
        out_specs=P(("groups", "row"), ("col", "half")),
        check_vma=False,
    )
```

```python
import functools

import jax
import jax.numpy as jnp
from jax import lax
from jax.experimental import pallas as pl
from jax.experimental.pallas import tpu as pltpu
from jax.sharding import PartitionSpec as P


def pair_product(left, right):
    return jnp.einsum("ip,jp->ij", left, right, preferred_element_type=jnp.float32)


def add_shift(summed, samples, shift, local_rows):
    width = summed.shape[1]
    first_row = lax.axis_index("row") * local_rows
    block = lax.axis_index("col") * lax.axis_size("half") + lax.axis_index("half")
    row_ids = first_row + lax.broadcasted_iota(jnp.int32, (local_rows, width), 0)
    column_ids = block * width + lax.broadcasted_iota(jnp.int32, (local_rows, width), 1)
    return summed / samples + jnp.where(row_ids == column_ids, shift[0], 0.0)


def gathered(log_derivs, shift):
    local_rows = log_derivs.shape[0]
    samples = local_rows * lax.axis_size("row")
    rows = lax.all_gather(log_derivs, "row", axis=0, tiled=True).astype(jnp.float32)
    mean = jnp.sum(rows, axis=0) / samples
    centered = (rows - mean[None, :]).astype(jnp.bfloat16)
    own = (log_derivs.astype(jnp.float32) - mean[None, :]).astype(jnp.bfloat16)
    tile = pair_product(own, centered)
    summed = lax.psum_scatter(tile, ("col", "half"), scatter_dimension=1, tiled=True)
    return add_shift(summed, samples, shift, local_rows)


EARLY_ROUNDS = (
    (((0, 0), (0, 1)), ((2, 2), (2, 0))),
    (((0, 1), (0, 0)), ((2, 0), (2, 2))),
    (((1, 0), (1, 1)), ((0, 2), (1, 2))),
    (((1, 1), (1, 0)), ((1, 2), (0, 2))),
)
LATE_ROUNDS = (
    (((3, 0), (3, 1)), ((3, 2), (3, 3))),
    (((3, 1), (3, 0)), ((3, 3), (3, 2))),
    (((0, 3), (1, 3)), ((2, 3), (2, 1))),
    (((1, 3), (0, 3)), ((2, 1), (2, 3))),
)
EARLY_SUMS = (((0, 0), (0, 1), (1, 1)), ((2, 2), (2, 0), (2, 1)))
EARLY_HELD = (
    ((0, 0), (0, 1), (1, 1), (1, 0), (1, 1)),
    ((2, 2), (2, 0), (2, 1), (0, 2), (1, 2)),
)
SPARE = 2
LATE_SUMS = (((3, 0), (3, 1)), ((3, 2), (3, 3)))
LATE_HELD = (
    ((3, 0), (3, 1), (0, 3), (1, 3), (1, 1)),
    ((3, 2), (3, 3), (2, 3), (3, 3), (2, 1)),
)
EXTRA = 16
HEAD = 32
VMEM = pl.BlockSpec(memory_space=pltpu.VMEM)
SMEM = pl.BlockSpec(memory_space=pltpu.SMEM)
ANY = pl.BlockSpec(memory_space=pl.ANY)
LIMIT = pltpu.CompilerParams(vmem_limit_bytes=40 * 2**20)
BRIEF = pl.CostEstimate(flops=1024, bytes_accessed=1024, transcendentals=0)


def device_index(row, col, half):
    return (row * 2 + col) * 2 + half


def round_pairs(blocks):
    pairs = []
    for side in (0, 1):
        for turn in (0, 1):
            for half in (0, 1):
                block = blocks[half][turn]
                if block is None:
                    continue
                i, j = (3 - b if side else b for b in block)
                source = device_index(1 + side, turn ^ side, half)
                pairs.append((source, device_index(i, j // 2, j % 2)))
    return pairs


def held_place(held, rounds):
    return [
        [[0 if b is None else held[half].index(b) for b in rounds_[half]] for half in (0, 1)]
        for rounds_ in rounds
    ]


def tail_places(rows):
    return HEAD, HEAD + (rows - HEAD) // 2


def far_kernel(bits, values, far, sem):
    part = far.shape[1]
    columns = pl.ds(pl.multiple_of(bits[0] * part, 128), part)
    copy = pltpu.make_async_copy(values.at[:, columns], far, sem)
    copy.start()
    copy.wait()


def near_kernel(bits, values, far, near, head, *rest):
    tails, (sums, sems) = rest[:-2], rest[-2:]
    rows, part = far.shape
    step = 512
    near_columns = pl.ds(pl.multiple_of((1 - bits[0]) * part, 128), part)
    copies = [
        pltpu.make_async_copy(values.at[:, near_columns], near, sems.at[0]),
        pltpu.make_async_copy(
            far.at[pl.ds(0, HEAD), :], head.at[pl.ds(EXTRA, HEAD), :], sems.at[1]
        ),
    ]
    for i, (first, tail) in enumerate(zip(tail_places(rows), tails)):
        from_rows = far.at[pl.ds(first, tail.shape[0]), :]
        copies.append(pltpu.make_async_copy(from_rows, tail, sems.at[2 + i]))
    for copy in copies:
        copy.start()

    @pl.loop(0, part // step)
    def _(j):
        columns = pl.ds(pl.multiple_of(j * step, step), step)
        left = jnp.sum(far[:, columns].astype(jnp.float32), axis=0, keepdims=True)
        for i in range(3):
            piece = left.astype(jnp.bfloat16).astype(jnp.float32)
            sums[pl.ds(i, 1), columns] = piece
            left = left - piece
        sums[pl.ds(3, EXTRA - 3), columns] = jnp.zeros((EXTRA - 3, step), jnp.float32)

    head[pl.ds(0, EXTRA), :] = sums[...].astype(jnp.bfloat16)
    for copy in copies:
        copy.wait()


def block_product(left, right):
    return lax.dot_general(left, right, (((1,), (1,)), ((), ())), preferred_element_type=jnp.float32)


def sum_kernel(other, near, partial):
    step = 512

    @pl.loop(0, near.shape[1] // step)
    def _(n):
        columns = pl.ds(pl.multiple_of(n * step, step), step)
        rows = other[:, columns].astype(jnp.float32) + near[:, columns].astype(jnp.float32)
        partial[:, columns] = jnp.sum(rows, axis=0, keepdims=True)


def early_kernel(bits, other, edge, head, near, partial, centred, mean, own, *rest):
    sends, both = rest[:-1], rest[-1]
    rows, part = near.shape
    step = 512

    @pl.loop(0, part // step)
    def _(n):
        columns = pl.ds(pl.multiple_of(n * step, step), step)
        values = [block[:, columns].astype(jnp.float32) for block in (edge, near, other)]
        pieces = head[pl.ds(0, EXTRA), columns].astype(jnp.float32)
        total = partial[:, columns] + jnp.sum(pieces, axis=0, keepdims=True)
        total = total + jnp.sum(values[0], axis=0, keepdims=True)
        average = total * (1.0 / (4 * rows))
        mean[:, columns] = average
        for i in range(3):
            centred[i, :, columns] = (values[i] - average).astype(jnp.bfloat16)

    for core in (0, 1):
        for place, (i, j) in enumerate(EARLY_SUMS[core]):
            both[core, place] = block_product(centred[i], centred[j])
    own[...] = both[bits[1]]
    for place, send in enumerate(sends):
        first = place * send.shape[1]
        send[...] = both[1 - bits[1], :, pl.ds(first, send.shape[1]), :]


def late_kernel(bits, head, tail, end, mean, centred, spare, own, send, handed, last, both):
    rows = last.shape[0]
    first = head[pl.ds(EXTRA, HEAD), :].astype(jnp.float32) - mean[...]
    last[pl.ds(0, HEAD), :] = first.astype(jnp.bfloat16)
    for place, block in zip(tail_places(rows), (tail, end)):
        values = block[...].astype(jnp.float32) - mean[...]
        last[pl.ds(place, block.shape[0]), :] = values.astype(jnp.bfloat16)
    for core in (0, 1):
        for place, (_, j) in enumerate(LATE_SUMS[core]):
            both[core, place] = block_product(last[...], last[...] if j == 3 else centred[j])
    own[...] = both[bits[1]]
    send[...] = both[1 - bits[1]]


def combine_kernel(flips, scale, pieces, spares, bits, places, own, *rest):
    others, spare = rest[:pieces], rest[pieces : pieces + spares]
    outs, held = rest[pieces + spares : -1], rest[-1]
    count = own.shape[0]
    for i in range(count):
        other = jnp.concatenate([piece[i] for piece in others], axis=0)
        held[i] = (own[i] + other) * scale
    for n, i in enumerate(flips):
        held[count + n] = held[i].T
    for i in range(spares):
        held[count + len(flips) + i] = spare[i][...]
    for r, out in enumerate(outs):
        out[...] = held[places[r, bits[1], bits[2]]]


def shape_of(shape, dtype):
    return jax.ShapeDtypeStruct(shape, dtype)


def combine(bits, own, others, flips, spares, held, places, samples):
    rows = own.shape[1]
    return pl.pallas_call(
        functools.partial(combine_kernel, flips, 1.0 / samples, len(others), len(spares)),
        out_shape=[shape_of((rows, rows), jnp.float32)] * len(places),
        in_specs=[SMEM, SMEM] + [VMEM] * (1 + len(others) + len(spares)),
        out_specs=[VMEM] * len(places),
        scratch_shapes=[pltpu.VMEM((len(held[0]), rows, rows), jnp.float32)],
        compiler_params=LIMIT,
        cost_estimate=BRIEF,
    )(bits, jnp.array(places, jnp.int32), own, *others, *spares)


def two_centres(log_derivs, shift):
    local_rows, local_params = log_derivs.shape
    samples = local_rows * 4
    part = local_params // 2
    everyone = ("row", "col", "half")
    row, col, half = (lax.axis_index(name) for name in everyone)
    side = (row >= 2).astype(jnp.int32)
    bits = jnp.stack([side, half, jnp.bitwise_xor(col, side)]).astype(jnp.int32)

    to_centre = [(1, 2), (2, 1)]
    to_own = [(0, 1), (3, 2)]
    to_far = [(0, 2), (3, 1)]
    centres = [(r * 2 + h, r * 2 + 1 - h) for r in (1, 2) for h in (0, 1)]

    def swap(value):
        return lax.ppermute(value, ("row", "half"), centres)

    def send(value, blocks):
        return lax.ppermute(value.astype(jnp.float16), everyone, round_pairs(blocks))

    far = pl.pallas_call(
        far_kernel,
        out_shape=shape_of((local_rows, part), jnp.bfloat16),
        in_specs=[SMEM, ANY],
        out_specs=VMEM,
        scratch_shapes=[pltpu.SemaphoreType.DMA],
        compiler_params=LIMIT,
        cost_estimate=BRIEF,
    )(bits, log_derivs)
    near, head, *tails = pl.pallas_call(
        near_kernel,
        out_shape=[
            shape_of((local_rows, part), jnp.bfloat16),
            shape_of((EXTRA + HEAD, part), jnp.bfloat16),
        ]
        + [shape_of(((local_rows - HEAD) // 2, part), jnp.bfloat16)] * 2,
        in_specs=[SMEM, ANY, VMEM],
        out_specs=[VMEM] * 4,
        scratch_shapes=[pltpu.VMEM((EXTRA, part), jnp.float32), pltpu.SemaphoreType.DMA((4,))],
        compiler_params=LIMIT,
        cost_estimate=BRIEF,
    )(bits, log_derivs, far)
    from_centre = lax.ppermute(far, "row", to_centre)
    from_edge = lax.ppermute(near, "row", to_own)
    from_head = lax.ppermute(head, "row", to_far)
    from_tails = [lax.ppermute(tail, "row", to_far) for tail in tails]

    partial = pl.pallas_call(
        sum_kernel,
        out_shape=shape_of((1, part), jnp.float32),
        in_specs=[VMEM] * 2,
        out_specs=VMEM,
        compiler_params=LIMIT,
    )(from_centre, near)
    early_blocks = (3, local_rows, local_rows)
    centred, mean, own, *others = pl.pallas_call(
        early_kernel,
        out_shape=[
            shape_of((3, local_rows, part), jnp.bfloat16),
            shape_of((1, part), jnp.float32),
            shape_of(early_blocks, jnp.float32),
        ]
        + [shape_of((3, local_rows // 2, local_rows), jnp.float32)] * 2,
        in_specs=[SMEM] + [VMEM] * 5,
        out_specs=[VMEM] * 5,
        scratch_shapes=[pltpu.VMEM((2,) + early_blocks, jnp.float32)],
        compiler_params=LIMIT,
        cost_estimate=BRIEF,
    )(bits, from_centre, from_edge, from_head, near, partial)
    others = [swap(other) for other in others]
    places = held_place(EARLY_HELD, EARLY_ROUNDS) + [[[SPARE] * 2] * 2]
    *early, spare = combine(bits, own, others, (1, 2), (), EARLY_HELD, places, samples)
    arrived = [send(value, blocks) for value, blocks in zip(early, EARLY_ROUNDS)]

    late_blocks = shape_of((2, local_rows, local_rows), jnp.float32)
    own, other, spare = pl.pallas_call(
        late_kernel,
        out_shape=[late_blocks, late_blocks, shape_of(spare.shape, spare.dtype)],
        in_specs=[SMEM] + [VMEM] * 5 + [ANY],
        out_specs=[VMEM] * 2 + [ANY],
        scratch_shapes=[
            pltpu.VMEM((local_rows, part), jnp.bfloat16),
            pltpu.VMEM((2,) + late_blocks.shape, jnp.float32),
        ],
        input_output_aliases={6: 2},
        compiler_params=LIMIT,
        cost_estimate=BRIEF,
    )(bits, from_head, *from_tails, mean, centred, spare)
    places = held_place(LATE_HELD, LATE_ROUNDS)
    late = combine(bits, own, [swap(other)], (0, 1), (spare,), LATE_HELD, places, samples)
    arrived += [send(value, blocks) for value, blocks in zip(late, LATE_ROUNDS)]
    summed = sum(block.astype(jnp.float32) for block in reversed(arrived))
    return add_shift(summed, 1, shift, local_rows)


def solution(mesh):
    shape = mesh.shape
    small = shape["row"] == 4 and shape["col"] == 2 and shape["half"] == 2
    return jax.shard_map(
        two_centres if small else gathered,
        mesh=mesh,
        in_specs=(P(("groups", "row"), ("col", "half")), P("groups")),
        out_specs=P(("groups", "row"), ("col", "half")),
        check_vma=False,
    )
```

```python
import functools

import jax
import jax.numpy as jnp
from jax import lax
from jax.experimental import pallas as pl
from jax.experimental.pallas import tpu as pltpu
from jax.sharding import PartitionSpec as P


def pair_product(left, right):
    return jnp.einsum("ip,jp->ij", left, right, preferred_element_type=jnp.float32)


def add_shift(summed, samples, shift, local_rows):
    width = summed.shape[1]
    first_row = lax.axis_index("row") * local_rows
    block = lax.axis_index("col") * lax.axis_size("half") + lax.axis_index("half")
    row_ids = first_row + lax.broadcasted_iota(jnp.int32, (local_rows, width), 0)
    column_ids = block * width + lax.broadcasted_iota(jnp.int32, (local_rows, width), 1)
    return summed / samples + jnp.where(row_ids == column_ids, shift[0], 0.0)


def gathered(log_derivs, shift):
    local_rows = log_derivs.shape[0]
    samples = local_rows * lax.axis_size("row")
    rows = lax.all_gather(log_derivs, "row", axis=0, tiled=True).astype(jnp.float32)
    mean = jnp.sum(rows, axis=0) / samples
    centered = (rows - mean[None, :]).astype(jnp.bfloat16)
    own = (log_derivs.astype(jnp.float32) - mean[None, :]).astype(jnp.bfloat16)
    tile = pair_product(own, centered)
    summed = lax.psum_scatter(tile, ("col", "half"), scatter_dimension=1, tiled=True)
    return add_shift(summed, samples, shift, local_rows)


NEAR_ROUNDS = (
    (((1, 0), (1, 1)), ((0, 2), (1, 2))),
    (((1, 1), (1, 0)), ((1, 2), (0, 2))),
)
FAR_ROUNDS = (
    (((0, 0), (0, 1)), ((2, 2), (2, 0))),
    (((0, 1), (0, 0)), ((2, 0), (2, 2))),
)
LATE_ROUNDS = (
    (((3, 0), (3, 1)), ((3, 2), (3, 3))),
    (((3, 1), (3, 0)), ((3, 3), (3, 2))),
    (((0, 3), (1, 3)), ((2, 3), (2, 1))),
    (((1, 3), (0, 3)), ((2, 1), (2, 3))),
)
EARLY_SUMS = (((0, 0), (0, 1), (1, 1)), ((2, 2), (2, 0), (2, 1)))
EARLY_HELD = (
    ((0, 0), (0, 1), (1, 1), (1, 0), (1, 1)),
    ((2, 2), (2, 0), (2, 1), (0, 2), (1, 2)),
)
SPARE = 2
LATE_SUMS = (((3, 0), (3, 1)), ((3, 2), (3, 3)))
LATE_HELD = (
    ((3, 0), (3, 1), (0, 3), (1, 3), (1, 1)),
    ((3, 2), (3, 3), (2, 3), (3, 3), (2, 1)),
)
EXTRA = 16
HEAD = 48
VMEM = pl.BlockSpec(memory_space=pltpu.VMEM)
SMEM = pl.BlockSpec(memory_space=pltpu.SMEM)
ANY = pl.BlockSpec(memory_space=pl.ANY)
LIMIT = pltpu.CompilerParams(vmem_limit_bytes=40 * 2**20)
BRIEF = pl.CostEstimate(flops=1024, bytes_accessed=1024, transcendentals=0)


def device_index(row, col, half):
    return (row * 2 + col) * 2 + half


def round_pairs(blocks):
    pairs = []
    for side in (0, 1):
        for turn in (0, 1):
            for half in (0, 1):
                block = blocks[half][turn]
                if block is None:
                    continue
                i, j = (3 - b if side else b for b in block)
                source = device_index(1 + side, turn ^ side, half)
                pairs.append((source, device_index(i, j // 2, j % 2)))
    return pairs


def held_place(held, rounds):
    return [
        [[0 if b is None else held[half].index(b) for b in rounds_[half]] for half in (0, 1)]
        for rounds_ in rounds
    ]


def far_kernel(bits, values, far, sem):
    part = far.shape[1]
    columns = pl.ds(pl.multiple_of(bits[0] * part, 128), part)
    copy = pltpu.make_async_copy(values.at[:, columns], far, sem)
    copy.start()
    copy.wait()


def near_kernel(bits, values, far, near, head, tail, sums, sems):
    rows, part = far.shape
    step = 512
    near_columns = pl.ds(pl.multiple_of((1 - bits[0]) * part, 128), part)
    copies = [
        pltpu.make_async_copy(values.at[:, near_columns], near, sems.at[0]),
        pltpu.make_async_copy(
            far.at[pl.ds(0, HEAD), :], head.at[pl.ds(EXTRA, HEAD), :], sems.at[1]
        ),
    ]
    from_rows = far.at[pl.ds(HEAD, rows - HEAD), :]
    copies.append(pltpu.make_async_copy(from_rows, tail, sems.at[2]))
    for copy in copies:
        copy.start()

    @pl.loop(0, part // step)
    def _(j):
        columns = pl.ds(pl.multiple_of(j * step, step), step)
        left = jnp.sum(far[:, columns].astype(jnp.float32), axis=0, keepdims=True)
        for i in range(3):
            piece = left.astype(jnp.bfloat16).astype(jnp.float32)
            sums[pl.ds(i, 1), columns] = piece
            left = left - piece
        sums[pl.ds(3, EXTRA - 3), columns] = jnp.zeros((EXTRA - 3, step), jnp.float32)

    head[pl.ds(0, EXTRA), :] = sums[...].astype(jnp.bfloat16)
    for copy in copies:
        copy.wait()


def block_product(left, right):
    return lax.dot_general(left, right, (((1,), (1,)), ((), ())), preferred_element_type=jnp.float32)


def sum_kernel(other, near, partial):
    step = 512

    @pl.loop(0, near.shape[1] // step)
    def _(n):
        columns = pl.ds(pl.multiple_of(n * step, step), step)
        rows = other[:, columns].astype(jnp.float32) + near[:, columns].astype(jnp.float32)
        partial[:, columns] = jnp.sum(rows, axis=0, keepdims=True)


def early_kernel(bits, other, edge, head, near, partial, centred, mean, own, *rest):
    sends, both = rest[:-1], rest[-1]
    rows, part = near.shape
    step = 512

    @pl.loop(0, part // step)
    def _(n):
        columns = pl.ds(pl.multiple_of(n * step, step), step)
        values = [block[:, columns].astype(jnp.float32) for block in (edge, near, other)]
        pieces = head[pl.ds(0, EXTRA), columns].astype(jnp.float32)
        total = partial[:, columns] + jnp.sum(pieces, axis=0, keepdims=True)
        total = total + jnp.sum(values[0], axis=0, keepdims=True)
        average = total * (1.0 / (4 * rows))
        mean[:, columns] = average
        for i in range(3):
            centred[i, :, columns] = (values[i] - average).astype(jnp.bfloat16)

    for core in (0, 1):
        for place, (i, j) in enumerate(EARLY_SUMS[core]):
            both[core, place] = block_product(centred[i], centred[j])
    own[...] = both[bits[1]]
    for place, send in enumerate(sends):
        send[...] = both[1 - bits[1], pl.ds(place, 1), :, :]


def late_kernel(bits, head, tail, mean, centred, *rest):
    own, send = rest[len(rest) // 2 - 2 : len(rest) // 2]
    last, both = rest[-2:]
    rows = last.shape[0]
    first = head[pl.ds(EXTRA, HEAD), :].astype(jnp.float32) - mean[...]
    last[pl.ds(0, HEAD), :] = first.astype(jnp.bfloat16)
    second = tail[...].astype(jnp.float32) - mean[...]
    last[pl.ds(HEAD, rows - HEAD), :] = second.astype(jnp.bfloat16)
    for core in (0, 1):
        for place, (_, j) in enumerate(LATE_SUMS[core]):
            both[core, place] = block_product(last[...], last[...] if j == 3 else centred[j])
    own[...] = both[bits[1]]
    send[...] = both[1 - bits[1]]


def combine_kernel(flips, scale, pieces, spares, bits, places, own, *rest):
    others, spare = rest[:pieces], rest[pieces : pieces + spares]
    outs, held = rest[pieces + spares : -1], rest[-1]
    count = own.shape[0]
    for i in range(count):
        other = others[0][i] if pieces == 1 else others[i][0]
        held[i] = (own[i] + other) * scale
    for n, i in enumerate(flips):
        held[count + n] = held[i].T
    for i in range(spares):
        held[count + len(flips) + i] = spare[i][...]
    for r, out in enumerate(outs):
        out[...] = held[places[r, bits[1], bits[2]]]


def shape_of(shape, dtype):
    return jax.ShapeDtypeStruct(shape, dtype)


def combine(bits, own, others, flips, spares, held, places, samples):
    rows = own.shape[1]
    return pl.pallas_call(
        functools.partial(combine_kernel, flips, 1.0 / samples, len(others), len(spares)),
        out_shape=[shape_of((rows, rows), jnp.float32)] * len(places),
        in_specs=[SMEM, SMEM] + [VMEM] * (1 + len(others) + len(spares)),
        out_specs=[VMEM] * len(places),
        scratch_shapes=[pltpu.VMEM((len(held[0]), rows, rows), jnp.float32)],
        compiler_params=LIMIT,
        cost_estimate=BRIEF,
    )(bits, jnp.array(places, jnp.int32), own, *others, *spares)


def two_centres(log_derivs, shift):
    local_rows, local_params = log_derivs.shape
    samples = local_rows * 4
    part = local_params // 2
    everyone = ("row", "col", "half")
    row, col, half = (lax.axis_index(name) for name in everyone)
    side = (row >= 2).astype(jnp.int32)
    bits = jnp.stack([side, half, jnp.bitwise_xor(col, side)]).astype(jnp.int32)

    to_centre = [(1, 2), (2, 1)]
    to_own = [(0, 1), (3, 2)]
    to_far = [(0, 2), (3, 1)]
    centres = [(r * 2 + h, r * 2 + 1 - h) for r in (1, 2) for h in (0, 1)]

    def swap(value):
        return lax.ppermute(value, ("row", "half"), centres)

    def send(value, blocks):
        return lax.ppermute(value.astype(jnp.float16), everyone, round_pairs(blocks))

    far = pl.pallas_call(
        far_kernel,
        out_shape=shape_of((local_rows, part), jnp.bfloat16),
        in_specs=[SMEM, ANY],
        out_specs=VMEM,
        scratch_shapes=[pltpu.SemaphoreType.DMA],
        compiler_params=LIMIT,
        cost_estimate=BRIEF,
    )(bits, log_derivs)
    near, head, tail = pl.pallas_call(
        near_kernel,
        out_shape=[
            shape_of((local_rows, part), jnp.bfloat16),
            shape_of((EXTRA + HEAD, part), jnp.bfloat16),
            shape_of((local_rows - HEAD, part), jnp.bfloat16),
        ],
        in_specs=[SMEM, ANY, VMEM],
        out_specs=[VMEM] * 3,
        scratch_shapes=[pltpu.VMEM((EXTRA, part), jnp.float32), pltpu.SemaphoreType.DMA((3,))],
        compiler_params=LIMIT,
        cost_estimate=BRIEF,
    )(bits, log_derivs, far)
    from_centre = lax.ppermute(far, "row", to_centre)
    from_edge = lax.ppermute(near, "row", to_own)
    from_head = lax.ppermute(head, "row", to_far)
    from_tail = lax.ppermute(tail, "row", to_far)

    partial = pl.pallas_call(
        sum_kernel,
        out_shape=shape_of((1, part), jnp.float32),
        in_specs=[VMEM] * 2,
        out_specs=VMEM,
        compiler_params=LIMIT,
    )(from_centre, near)
    early_blocks = (3, local_rows, local_rows)
    centred, mean, own, *others = pl.pallas_call(
        early_kernel,
        out_shape=[
            shape_of((3, local_rows, part), jnp.bfloat16),
            shape_of((1, part), jnp.float32),
            shape_of(early_blocks, jnp.float32),
        ]
        + [shape_of((1, local_rows, local_rows), jnp.float32)] * 3,
        in_specs=[SMEM] + [VMEM] * 5,
        out_specs=[VMEM] * 6,
        scratch_shapes=[pltpu.VMEM((2,) + early_blocks, jnp.float32)],
        compiler_params=LIMIT,
        cost_estimate=BRIEF,
    )(bits, from_centre, from_edge, from_head, near, partial)
    others = [swap(other) for other in others]
    places = held_place(EARLY_HELD, NEAR_ROUNDS + FAR_ROUNDS) + [[[SPARE] * 2] * 2]
    *early, spare = combine(bits, own, others, (1, 2), (), EARLY_HELD, places, samples)
    near_blocks, far_blocks = early[: len(NEAR_ROUNDS)], early[len(NEAR_ROUNDS) :]
    arrived = [send(value, blocks) for value, blocks in zip(near_blocks, NEAR_ROUNDS)]
    summed = sum(block.astype(jnp.float32) for block in arrived)

    late_blocks = shape_of((2, local_rows, local_rows), jnp.float32)
    handed = [summed] + far_blocks
    own, other, summed, *far_blocks = pl.pallas_call(
        late_kernel,
        out_shape=[late_blocks, late_blocks]
        + [shape_of(value.shape, value.dtype) for value in handed],
        in_specs=[SMEM] + [VMEM] * 4 + [ANY] * len(handed),
        out_specs=[VMEM] * 2 + [ANY] * len(handed),
        scratch_shapes=[
            pltpu.VMEM((local_rows, part), jnp.bfloat16),
            pltpu.VMEM((2,) + late_blocks.shape, jnp.float32),
        ],
        input_output_aliases={5 + i: 2 + i for i in range(len(handed))},
        compiler_params=LIMIT,
        cost_estimate=BRIEF,
    )(bits, from_head, from_tail, mean, centred, *handed)
    other = swap(other)
    arrived = [send(value, blocks) for value, blocks in zip(far_blocks, FAR_ROUNDS)]
    places = held_place(LATE_HELD, LATE_ROUNDS)
    late = combine(bits, own, [other], (0, 1), (spare,), LATE_HELD, places, samples)
    arrived += [send(value, blocks) for value, blocks in zip(late, LATE_ROUNDS)]
    summed = summed + sum(block.astype(jnp.float32) for block in reversed(arrived))
    return add_shift(summed, 1, shift, local_rows)


def solution(mesh):
    shape = mesh.shape
    small = shape["row"] == 4 and shape["col"] == 2 and shape["half"] == 2
    return jax.shard_map(
        two_centres if small else gathered,
        mesh=mesh,
        in_specs=(P(("groups", "row"), ("col", "half")), P("groups")),
        out_specs=P(("groups", "row"), ("col", "half")),
        check_vma=False,
    )
```

```python
import functools

import jax
import jax.numpy as jnp
from jax import lax
from jax.experimental import pallas as pl
from jax.experimental.pallas import tpu as pltpu
from jax.sharding import PartitionSpec as P


def pair_product(left, right):
    return jnp.einsum("ip,jp->ij", left, right, preferred_element_type=jnp.float32)


def add_shift(summed, samples, shift, local_rows):
    width = summed.shape[1]
    first_row = lax.axis_index("row") * local_rows
    block = lax.axis_index("col") * lax.axis_size("half") + lax.axis_index("half")
    row_ids = first_row + lax.broadcasted_iota(jnp.int32, (local_rows, width), 0)
    column_ids = block * width + lax.broadcasted_iota(jnp.int32, (local_rows, width), 1)
    return summed / samples + jnp.where(row_ids == column_ids, shift[0], 0.0)


def gathered(log_derivs, shift):
    local_rows = log_derivs.shape[0]
    samples = local_rows * lax.axis_size("row")
    rows = lax.all_gather(log_derivs, "row", axis=0, tiled=True).astype(jnp.float32)
    mean = jnp.sum(rows, axis=0) / samples
    centered = (rows - mean[None, :]).astype(jnp.bfloat16)
    own = (log_derivs.astype(jnp.float32) - mean[None, :]).astype(jnp.bfloat16)
    tile = pair_product(own, centered)
    summed = lax.psum_scatter(tile, ("col", "half"), scatter_dimension=1, tiled=True)
    return add_shift(summed, samples, shift, local_rows)


NEAR_ROUNDS = (
    (((0, 0), (0, 1)), ((0, 2), (1, 2))),
    (((0, 1), (0, 0)), ((1, 2), (0, 2))),
    (((1, 0), (1, 1)), (None, None)),
    (((1, 1), (1, 0)), (None, None)),
)
FAR_ROUNDS = (
    ((None, None), ((2, 0), (2, 2))),
    ((None, None), ((2, 2), (2, 0))),
)
LATE_ROUNDS = (
    (((1, 3), (0, 3)), ((2, 1), (2, 3))),
    (((0, 3), (1, 3)), ((2, 3), (2, 1))),
    (((3, 1), (3, 0)), ((3, 3), (3, 2))),
    (((3, 0), (3, 1)), ((3, 2), (3, 3))),
)
EARLY_SUMS = (((0, 0), (0, 1), (1, 1)), ((2, 2), (2, 0), (2, 1)))
EARLY_HELD = (
    ((0, 0), (0, 1), (1, 1), (1, 0), (1, 1)),
    ((2, 2), (2, 0), (2, 1), (0, 2), (1, 2)),
)
SPARE = 2
LATE_SUMS = (((3, 0), (3, 1)), ((3, 2), (3, 3)))
LATE_HELD = (
    ((3, 0), (3, 1), (0, 3), (1, 3), (1, 1)),
    ((3, 2), (3, 3), (2, 3), (3, 3), (2, 1)),
)
VMEM = pl.BlockSpec(memory_space=pltpu.VMEM)
SMEM = pl.BlockSpec(memory_space=pltpu.SMEM)
ANY = pl.BlockSpec(memory_space=pl.ANY)
LIMIT = pltpu.CompilerParams(vmem_limit_bytes=40 * 2**20)
BRIEF = pl.CostEstimate(flops=1024, bytes_accessed=1024, transcendentals=0)
LONG = pl.CostEstimate(flops=3 * 2**31, bytes_accessed=1024, transcendentals=0)


def device_index(row, col, half):
    return (row * 2 + col) * 2 + half


def round_pairs(blocks):
    pairs = []
    for side in (0, 1):
        for turn in (0, 1):
            for half in (0, 1):
                block = blocks[half][turn]
                if block is None:
                    continue
                i, j = (3 - b if side else b for b in block)
                source = device_index(1 + side, turn ^ side, half)
                pairs.append((source, device_index(i, j // 2, j % 2)))
    return pairs


def held_place(held, rounds):
    return [
        [[0 if b is None else held[half].index(b) for b in rounds_[half]] for half in (0, 1)]
        for rounds_ in rounds
    ]


def split_kernel(bits, values, near, far, far_sum, sems):
    part = far.shape[1]
    step = 512
    copies = []
    for i, (out, start) in enumerate(((far, bits[0]), (near, 1 - bits[0]))):
        columns = pl.ds(pl.multiple_of(start * part, 128), part)
        copies.append(pltpu.make_async_copy(values.at[:, columns], out, sems.at[i]))
    for copy in copies:
        copy.start()
    copies[0].wait()

    @pl.loop(0, part // step)
    def _(j):
        columns = pl.ds(pl.multiple_of(j * step, step), step)
        block = far[:, columns].astype(jnp.float32)
        far_sum[:, columns] = jnp.sum(block, axis=0, keepdims=True)

    copies[1].wait()


def block_product(left, right):
    return lax.dot_general(left, right, (((1,), (1,)), ((), ())), preferred_element_type=jnp.float32)


def sum_kernel(other, near, far_sum, partial):
    step = 512

    @pl.loop(0, near.shape[1] // step)
    def _(n):
        columns = pl.ds(pl.multiple_of(n * step, step), step)
        rows = other[:, columns].astype(jnp.float32) + near[:, columns].astype(jnp.float32)
        partial[:, columns] = far_sum[:, columns] + jnp.sum(rows, axis=0, keepdims=True)


def early_kernel(bits, other, edge, near, partial, centred, mean, own, *rest):
    sends, both = rest[:-1], rest[-1]
    rows, part = near.shape
    step = 512

    @pl.loop(0, part // step)
    def _(n):
        columns = pl.ds(pl.multiple_of(n * step, step), step)
        values = [block[:, columns].astype(jnp.float32) for block in (edge, near, other)]
        total = partial[:, columns] + jnp.sum(values[0], axis=0, keepdims=True)
        average = total * (1.0 / (4 * rows))
        mean[:, columns] = average
        for i in range(3):
            centred[i, :, columns] = (values[i] - average).astype(jnp.bfloat16)

    for core in (0, 1):
        for place, (i, j) in enumerate(EARLY_SUMS[core]):
            both[core, place] = block_product(centred[i], centred[j])
    own[...] = both[bits[1]]
    for place, send in enumerate(sends):
        send[...] = both[1 - bits[1], pl.ds(place, 1), :, :]


def late_kernel(bits, far_edge, mean, centred, *rest):
    own, send = rest[len(rest) // 2 - 2 : len(rest) // 2]
    last, both = rest[-2:]
    last[...] = (far_edge[...].astype(jnp.float32) - mean[...]).astype(jnp.bfloat16)
    for core in (0, 1):
        for place, (_, j) in enumerate(LATE_SUMS[core]):
            both[core, place] = block_product(last[...], last[...] if j == 3 else centred[j])
    own[...] = both[bits[1]]
    send[...] = both[1 - bits[1]]


def combine_kernel(flips, scale, pieces, spares, bits, places, own, *rest):
    others, spare = rest[:pieces], rest[pieces : pieces + spares]
    outs, held = rest[pieces + spares : -1], rest[-1]
    count = own.shape[0]
    for i in range(count):
        other = others[0][i] if pieces == 1 else others[i][0]
        held[i] = (own[i] + other) * scale
    for n, i in enumerate(flips):
        held[count + n] = held[i].T
    for i in range(spares):
        held[count + len(flips) + i] = spare[i][...]
    for r, out in enumerate(outs):
        out[...] = held[places[r, bits[1], bits[2]]]


def shape_of(shape, dtype):
    return jax.ShapeDtypeStruct(shape, dtype)


def combine(bits, own, others, flips, spares, held, places, samples):
    rows = own.shape[1]
    return pl.pallas_call(
        functools.partial(combine_kernel, flips, 1.0 / samples, len(others), len(spares)),
        out_shape=[shape_of((rows, rows), jnp.float32)] * len(places),
        in_specs=[SMEM, SMEM] + [VMEM] * (1 + len(others) + len(spares)),
        out_specs=[VMEM] * len(places),
        scratch_shapes=[pltpu.VMEM((len(held[0]), rows, rows), jnp.float32)],
        compiler_params=LIMIT,
        cost_estimate=BRIEF,
    )(bits, jnp.array(places, jnp.int32), own, *others, *spares)


def two_centres(log_derivs, shift):
    local_rows, local_params = log_derivs.shape
    samples = local_rows * 4
    part = local_params // 2
    everyone = ("row", "col", "half")
    row, col, half = (lax.axis_index(name) for name in everyone)
    side = (row >= 2).astype(jnp.int32)
    bits = jnp.stack([side, half, jnp.bitwise_xor(col, side)]).astype(jnp.int32)

    to_centre = [(1, 2), (2, 1)]
    to_own = [(0, 1), (3, 2)]
    to_far = [(0, 2), (3, 1)]
    centres = [(r * 2 + h, r * 2 + 1 - h) for r in (1, 2) for h in (0, 1)]

    def swap(value):
        return lax.ppermute(value, ("row", "half"), centres)

    def send(value, blocks):
        return lax.ppermute(value.astype(jnp.float16), everyone, round_pairs(blocks))

    near, far, far_sum = pl.pallas_call(
        split_kernel,
        out_shape=[
            shape_of((local_rows, part), jnp.bfloat16),
            shape_of((local_rows, part), jnp.bfloat16),
            shape_of((1, part), jnp.float32),
        ],
        in_specs=[SMEM, ANY],
        out_specs=[VMEM] * 3,
        scratch_shapes=[pltpu.SemaphoreType.DMA((2,))],
        compiler_params=LIMIT,
        cost_estimate=BRIEF,
    )(bits, log_derivs)
    from_centre = lax.ppermute(far, "row", to_centre)
    from_sum = lax.ppermute(far_sum, "row", to_far)
    from_edge = lax.ppermute(near, "row", to_own)
    from_far_edge = lax.ppermute(far, "row", to_far)

    partial = pl.pallas_call(
        sum_kernel,
        out_shape=shape_of((1, part), jnp.float32),
        in_specs=[VMEM] * 3,
        out_specs=VMEM,
        compiler_params=LIMIT,
        cost_estimate=LONG,
    )(from_centre, near, from_sum)
    early_blocks = (3, local_rows, local_rows)
    centred, mean, own, *others = pl.pallas_call(
        early_kernel,
        out_shape=[
            shape_of((3, local_rows, part), jnp.bfloat16),
            shape_of((1, part), jnp.float32),
            shape_of(early_blocks, jnp.float32),
        ]
        + [shape_of((1, local_rows, local_rows), jnp.float32)] * 3,
        in_specs=[SMEM] + [VMEM] * 4,
        out_specs=[VMEM] * 6,
        scratch_shapes=[pltpu.VMEM((2,) + early_blocks, jnp.float32)],
        compiler_params=LIMIT,
        cost_estimate=BRIEF,
    )(bits, from_centre, from_edge, near, partial)
    others = [swap(other) for other in others]
    places = held_place(EARLY_HELD, NEAR_ROUNDS + FAR_ROUNDS) + [[[SPARE] * 2] * 2]
    *early, spare = combine(bits, own, others, (1, 2), (), EARLY_HELD, places, samples)
    near_blocks, far_blocks = early[: len(NEAR_ROUNDS)], early[len(NEAR_ROUNDS) :]
    arrived = [send(value, blocks) for value, blocks in zip(near_blocks, NEAR_ROUNDS)]
    summed = sum(block.astype(jnp.float32) for block in arrived)

    late_blocks = shape_of((2, local_rows, local_rows), jnp.float32)
    handed = [summed] + far_blocks
    own, other, summed, *far_blocks = pl.pallas_call(
        late_kernel,
        out_shape=[late_blocks, late_blocks]
        + [shape_of(value.shape, value.dtype) for value in handed],
        in_specs=[SMEM] + [VMEM] * 3 + [ANY] * len(handed),
        out_specs=[VMEM] * 2 + [ANY] * len(handed),
        scratch_shapes=[
            pltpu.VMEM((local_rows, part), jnp.bfloat16),
            pltpu.VMEM((2,) + late_blocks.shape, jnp.float32),
        ],
        input_output_aliases={4 + i: 2 + i for i in range(len(handed))},
        compiler_params=LIMIT,
        cost_estimate=BRIEF,
    )(bits, from_far_edge, mean, centred, *handed)
    other = swap(other)
    arrived = [send(value, blocks) for value, blocks in zip(far_blocks, FAR_ROUNDS)]
    places = held_place(LATE_HELD, LATE_ROUNDS)
    late = combine(bits, own, [other], (0, 1), (spare,), LATE_HELD, places, samples)
    arrived += [send(value, blocks) for value, blocks in zip(late, LATE_ROUNDS)]
    summed = summed + sum(block.astype(jnp.float32) for block in reversed(arrived))
    return add_shift(summed, 1, shift, local_rows)


def solution(mesh):
    shape = mesh.shape
    small = shape["row"] == 4 and shape["col"] == 2 and shape["half"] == 2
    return jax.shard_map(
        two_centres if small else gathered,
        mesh=mesh,
        in_specs=(P(("groups", "row"), ("col", "half")), P("groups")),
        out_specs=P(("groups", "row"), ("col", "half")),
        check_vma=False,
    )
```

```python
import functools

import jax
import jax.numpy as jnp
from jax import lax
from jax.experimental import pallas as pl
from jax.experimental.pallas import tpu as pltpu
from jax.sharding import PartitionSpec as P


def pair_product(left, right):
    return jnp.einsum("ip,jp->ij", left, right, preferred_element_type=jnp.float32)


def add_shift(summed, samples, shift, local_rows):
    width = summed.shape[1]
    first_row = lax.axis_index("row") * local_rows
    block = lax.axis_index("col") * lax.axis_size("half") + lax.axis_index("half")
    row_ids = first_row + lax.broadcasted_iota(jnp.int32, (local_rows, width), 0)
    column_ids = block * width + lax.broadcasted_iota(jnp.int32, (local_rows, width), 1)
    return summed / samples + jnp.where(row_ids == column_ids, shift[0], 0.0)


def gathered(log_derivs, shift):
    local_rows = log_derivs.shape[0]
    samples = local_rows * lax.axis_size("row")
    rows = lax.all_gather(log_derivs, "row", axis=0, tiled=True).astype(jnp.float32)
    mean = jnp.sum(rows, axis=0) / samples
    centered = (rows - mean[None, :]).astype(jnp.bfloat16)
    own = (log_derivs.astype(jnp.float32) - mean[None, :]).astype(jnp.bfloat16)
    tile = pair_product(own, centered)
    summed = lax.psum_scatter(tile, ("col", "half"), scatter_dimension=1, tiled=True)
    return add_shift(summed, samples, shift, local_rows)


NEAR_ROUNDS = (
    (((1, 0), (1, 1)), ((0, 2), (1, 2))),
    (((1, 1), (1, 0)), ((1, 2), (0, 2))),
)
FAR_ROUNDS = (
    (((0, 0), (0, 1)), ((2, 2), (2, 0))),
    (((0, 1), (0, 0)), ((2, 0), (2, 2))),
)
LATE_ROUNDS = (
    (((1, 3), (0, 3)), ((2, 1), (2, 3))),
    (((0, 3), (1, 3)), ((2, 3), (2, 1))),
    (((3, 1), (3, 0)), ((3, 3), (3, 2))),
    (((3, 0), (3, 1)), ((3, 2), (3, 3))),
)
EARLY_SUMS = (((0, 0), (0, 1), (1, 1)), ((2, 2), (2, 0), (2, 1)))
EARLY_HELD = (
    ((0, 0), (0, 1), (1, 1), (1, 0), (1, 1)),
    ((2, 2), (2, 0), (2, 1), (0, 2), (1, 2)),
)
SPARE = 2
LATE_SUMS = (((3, 0), (3, 1)), ((3, 2), (3, 3)))
LATE_HELD = (
    ((3, 0), (3, 1), (0, 3), (1, 3), (1, 1)),
    ((3, 2), (3, 3), (2, 3), (3, 3), (2, 1)),
)
VMEM = pl.BlockSpec(memory_space=pltpu.VMEM)
SMEM = pl.BlockSpec(memory_space=pltpu.SMEM)
ANY = pl.BlockSpec(memory_space=pl.ANY)
LIMIT = pltpu.CompilerParams(vmem_limit_bytes=40 * 2**20)
BRIEF = pl.CostEstimate(flops=1024, bytes_accessed=1024, transcendentals=0)
LONG = pl.CostEstimate(flops=3 * 2**31, bytes_accessed=1024, transcendentals=0)


def device_index(row, col, half):
    return (row * 2 + col) * 2 + half


def round_pairs(blocks):
    pairs = []
    for side in (0, 1):
        for turn in (0, 1):
            for half in (0, 1):
                block = blocks[half][turn]
                if block is None:
                    continue
                i, j = (3 - b if side else b for b in block)
                source = device_index(1 + side, turn ^ side, half)
                pairs.append((source, device_index(i, j // 2, j % 2)))
    return pairs


def held_place(held, rounds):
    return [
        [[0 if b is None else held[half].index(b) for b in rounds_[half]] for half in (0, 1)]
        for rounds_ in rounds
    ]


def split_kernel(bits, values, near, far, far_sum, sems):
    part = far.shape[1]
    step = 512
    copies = []
    for i, (out, start) in enumerate(((far, bits[0]), (near, 1 - bits[0]))):
        columns = pl.ds(pl.multiple_of(start * part, 128), part)
        copies.append(pltpu.make_async_copy(values.at[:, columns], out, sems.at[i]))
    for copy in copies:
        copy.start()
    copies[0].wait()

    @pl.loop(0, part // step)
    def _(j):
        columns = pl.ds(pl.multiple_of(j * step, step), step)
        block = far[:, columns].astype(jnp.float32)
        far_sum[:, columns] = jnp.sum(block, axis=0, keepdims=True)

    copies[1].wait()


def block_product(left, right):
    return lax.dot_general(left, right, (((1,), (1,)), ((), ())), preferred_element_type=jnp.float32)


def sum_kernel(other, near, far_sum, partial):
    step = 512

    @pl.loop(0, near.shape[1] // step)
    def _(n):
        columns = pl.ds(pl.multiple_of(n * step, step), step)
        rows = other[:, columns].astype(jnp.float32) + near[:, columns].astype(jnp.float32)
        partial[:, columns] = far_sum[:, columns] + jnp.sum(rows, axis=0, keepdims=True)


def early_kernel(bits, other, edge, near, partial, centred, mean, own, *rest):
    sends, both = rest[:-1], rest[-1]
    rows, part = near.shape
    step = 512

    @pl.loop(0, part // step)
    def _(n):
        columns = pl.ds(pl.multiple_of(n * step, step), step)
        values = [block[:, columns].astype(jnp.float32) for block in (edge, near, other)]
        total = partial[:, columns] + jnp.sum(values[0], axis=0, keepdims=True)
        average = total * (1.0 / (4 * rows))
        mean[:, columns] = average
        for i in range(3):
            centred[i, :, columns] = (values[i] - average).astype(jnp.bfloat16)

    for core in (0, 1):
        for place, (i, j) in enumerate(EARLY_SUMS[core]):
            both[core, place] = block_product(centred[i], centred[j])
    own[...] = both[bits[1]]
    for place, send in enumerate(sends):
        send[...] = both[1 - bits[1], pl.ds(place, 1), :, :]


def late_products(core, last, centred, out):
    for place, (_, j) in enumerate(LATE_SUMS[core]):
        out[place] = block_product(last[...], last[...] if j == 3 else centred[j])


def late_kernel(bits, far_edge, mean, centred, *rest):
    last, send = rest[(len(rest) - 2) // 2 :][:2]
    last[...] = (far_edge[...].astype(jnp.float32) - mean[...]).astype(jnp.bfloat16)
    for core in (0, 1):

        @pl.when(bits[1] != core)
        def _():
            late_products(core, last, centred, send)


def keep_kernel(bits, last, centred, own):
    for core in (0, 1):

        @pl.when(bits[1] == core)
        def _():
            late_products(core, last, centred, own)


def combine_kernel(flips, scale, pieces, spares, bits, places, own, *rest):
    others, spare = rest[:pieces], rest[pieces : pieces + spares]
    outs, held = rest[pieces + spares : -1], rest[-1]
    count = own.shape[0]
    for i in range(count):
        other = others[0][i] if pieces == 1 else others[i][0]
        held[i] = (own[i] + other) * scale
    for n, i in enumerate(flips):
        held[count + n] = held[i].T
    for i in range(spares):
        held[count + len(flips) + i] = spare[i][...]
    for r, out in enumerate(outs):
        out[...] = held[places[r, bits[1], bits[2]]]


def shape_of(shape, dtype):
    return jax.ShapeDtypeStruct(shape, dtype)


def combine(bits, own, others, flips, spares, held, places, samples):
    rows = own.shape[1]
    return pl.pallas_call(
        functools.partial(combine_kernel, flips, 1.0 / samples, len(others), len(spares)),
        out_shape=[shape_of((rows, rows), jnp.float32)] * len(places),
        in_specs=[SMEM, SMEM] + [VMEM] * (1 + len(others) + len(spares)),
        out_specs=[VMEM] * len(places),
        scratch_shapes=[pltpu.VMEM((len(held[0]), rows, rows), jnp.float32)],
        compiler_params=LIMIT,
        cost_estimate=BRIEF,
    )(bits, jnp.array(places, jnp.int32), own, *others, *spares)


def two_centres(log_derivs, shift):
    local_rows, local_params = log_derivs.shape
    samples = local_rows * 4
    part = local_params // 2
    everyone = ("row", "col", "half")
    row, col, half = (lax.axis_index(name) for name in everyone)
    side = (row >= 2).astype(jnp.int32)
    bits = jnp.stack([side, half, jnp.bitwise_xor(col, side)]).astype(jnp.int32)

    to_centre = [(1, 2), (2, 1)]
    to_own = [(0, 1), (3, 2)]
    to_far = [(0, 2), (3, 1)]
    centres = [(r * 2 + h, r * 2 + 1 - h) for r in (1, 2) for h in (0, 1)]

    def swap(value):
        return lax.ppermute(value, ("row", "half"), centres)

    def send(value, blocks):
        return lax.ppermute(value.astype(jnp.float16), everyone, round_pairs(blocks))

    near, far, far_sum = pl.pallas_call(
        split_kernel,
        out_shape=[
            shape_of((local_rows, part), jnp.bfloat16),
            shape_of((local_rows, part), jnp.bfloat16),
            shape_of((1, part), jnp.float32),
        ],
        in_specs=[SMEM, ANY],
        out_specs=[VMEM] * 3,
        scratch_shapes=[pltpu.SemaphoreType.DMA((2,))],
        compiler_params=LIMIT,
        cost_estimate=BRIEF,
    )(bits, log_derivs)
    from_centre = lax.ppermute(far, "row", to_centre)
    from_sum = lax.ppermute(far_sum, "row", to_far)
    from_edge = lax.ppermute(near, "row", to_own)
    from_far_edge = lax.ppermute(far, "row", to_far)

    partial = pl.pallas_call(
        sum_kernel,
        out_shape=shape_of((1, part), jnp.float32),
        in_specs=[VMEM] * 3,
        out_specs=VMEM,
        compiler_params=LIMIT,
        cost_estimate=LONG,
    )(from_centre, near, from_sum)
    early_blocks = (3, local_rows, local_rows)
    centred, mean, own, *others = pl.pallas_call(
        early_kernel,
        out_shape=[
            shape_of((3, local_rows, part), jnp.bfloat16),
            shape_of((1, part), jnp.float32),
            shape_of(early_blocks, jnp.float32),
        ]
        + [shape_of((1, local_rows, local_rows), jnp.float32)] * 3,
        in_specs=[SMEM] + [VMEM] * 4,
        out_specs=[VMEM] * 6,
        scratch_shapes=[pltpu.VMEM((2,) + early_blocks, jnp.float32)],
        compiler_params=LIMIT,
        cost_estimate=BRIEF,
    )(bits, from_centre, from_edge, near, partial)
    others = [swap(other) for other in others]
    places = held_place(EARLY_HELD, NEAR_ROUNDS + FAR_ROUNDS) + [[[SPARE] * 2] * 2]
    *early, spare = combine(bits, own, others, (1, 2), (), EARLY_HELD, places, samples)
    near_blocks, far_blocks = early[: len(NEAR_ROUNDS)], early[len(NEAR_ROUNDS) :]
    arrived = [send(value, blocks) for value, blocks in zip(near_blocks, NEAR_ROUNDS)]
    summed = sum(block.astype(jnp.float32) for block in arrived)

    late_blocks = shape_of((2, local_rows, local_rows), jnp.float32)
    handed = [summed] + far_blocks
    last, other, summed, *far_blocks = pl.pallas_call(
        late_kernel,
        out_shape=[shape_of((local_rows, part), jnp.bfloat16), late_blocks]
        + [shape_of(value.shape, value.dtype) for value in handed],
        in_specs=[SMEM] + [VMEM] * 3 + [ANY] * len(handed),
        out_specs=[VMEM] * 2 + [ANY] * len(handed),
        input_output_aliases={4 + i: 2 + i for i in range(len(handed))},
        compiler_params=LIMIT,
        cost_estimate=BRIEF,
    )(bits, from_far_edge, mean, centred, *handed)
    own = pl.pallas_call(
        keep_kernel,
        out_shape=late_blocks,
        in_specs=[SMEM] + [VMEM] * 2,
        out_specs=VMEM,
        compiler_params=LIMIT,
        cost_estimate=BRIEF,
    )(bits, last, centred)
    other = swap(other)
    arrived = [send(value, blocks) for value, blocks in zip(far_blocks, FAR_ROUNDS)]
    places = held_place(LATE_HELD, LATE_ROUNDS)
    late = combine(bits, own, [other], (0, 1), (spare,), LATE_HELD, places, samples)
    arrived += [send(value, blocks) for value, blocks in zip(late, LATE_ROUNDS)]
    summed = summed + sum(block.astype(jnp.float32) for block in reversed(arrived))
    return add_shift(summed, 1, shift, local_rows)


def solution(mesh):
    shape = mesh.shape
    small = shape["row"] == 4 and shape["col"] == 2 and shape["half"] == 2
    return jax.shard_map(
        two_centres if small else gathered,
        mesh=mesh,
        in_specs=(P(("groups", "row"), ("col", "half")), P("groups")),
        out_specs=P(("groups", "row"), ("col", "half")),
        check_vma=False,
    )
```

```python
import functools

import jax
import jax.numpy as jnp
from jax import lax
from jax.experimental import pallas as pl
from jax.experimental.pallas import tpu as pltpu
from jax.sharding import PartitionSpec as P


def pair_product(left, right):
    return jnp.einsum("ip,jp->ij", left, right, preferred_element_type=jnp.float32)


def add_shift(summed, samples, shift, local_rows):
    width = summed.shape[1]
    first_row = lax.axis_index("row") * local_rows
    block = lax.axis_index("col") * lax.axis_size("half") + lax.axis_index("half")
    row_ids = first_row + lax.broadcasted_iota(jnp.int32, (local_rows, width), 0)
    column_ids = block * width + lax.broadcasted_iota(jnp.int32, (local_rows, width), 1)
    return summed / samples + jnp.where(row_ids == column_ids, shift[0], 0.0)


def gathered(log_derivs, shift):
    local_rows = log_derivs.shape[0]
    samples = local_rows * lax.axis_size("row")
    rows = lax.all_gather(log_derivs, "row", axis=0, tiled=True).astype(jnp.float32)
    mean = jnp.sum(rows, axis=0) / samples
    centered = (rows - mean[None, :]).astype(jnp.bfloat16)
    own = (log_derivs.astype(jnp.float32) - mean[None, :]).astype(jnp.bfloat16)
    tile = pair_product(own, centered)
    summed = lax.psum_scatter(tile, ("col", "half"), scatter_dimension=1, tiled=True)
    return add_shift(summed, samples, shift, local_rows)


NEAR_ROUNDS = (
    (((1, 0), (1, 1)), ((0, 2), (1, 2))),
    (((1, 1), (1, 0)), ((1, 2), (0, 2))),
)
MIDDLE_ROUNDS = (
    (((0, 0), (0, 1)), ((2, 2), (2, 0))),
)
LATE_ROUNDS = (
    (((0, 1), (0, 0)), ((2, 0), (2, 2))),
    (((1, 3), (0, 3)), ((2, 1), (2, 3))),
    (((0, 3), (1, 3)), ((2, 3), (2, 1))),
    (((3, 1), (3, 0)), ((3, 3), (3, 2))),
    (((3, 0), (3, 1)), ((3, 2), (3, 3))),
)
EARLY_SUMS = (((0, 0), (0, 1), (1, 1)), ((2, 2), (2, 0), (2, 1)))
EARLY_HELD = (
    ((0, 0), (0, 1), (1, 1), (1, 0), (1, 1)),
    ((2, 2), (2, 0), (2, 1), (0, 2), (1, 2)),
)
LATE_SUMS = (((3, 0), (3, 1)), ((3, 2), (3, 3)))
LATE_HELD = (
    ((3, 0), (3, 1), (0, 3), (1, 3)) + EARLY_SUMS[0],
    ((3, 2), (3, 3), (2, 3), (3, 3)) + EARLY_SUMS[1],
)
VMEM = pl.BlockSpec(memory_space=pltpu.VMEM)
SMEM = pl.BlockSpec(memory_space=pltpu.SMEM)
ANY = pl.BlockSpec(memory_space=pl.ANY)
LIMIT = pltpu.CompilerParams(vmem_limit_bytes=40 * 2**20)
BRIEF = pl.CostEstimate(flops=1024, bytes_accessed=1024, transcendentals=0)
LONG = pl.CostEstimate(flops=3 * 2**31, bytes_accessed=1024, transcendentals=0)


def device_index(row, col, half):
    return (row * 2 + col) * 2 + half


def round_pairs(blocks):
    pairs = []
    for side in (0, 1):
        for turn in (0, 1):
            for half in (0, 1):
                block = blocks[half][turn]
                if block is None:
                    continue
                i, j = (3 - b if side else b for b in block)
                source = device_index(1 + side, turn ^ side, half)
                pairs.append((source, device_index(i, j // 2, j % 2)))
    return pairs


def held_place(held, rounds):
    return [
        [[0 if b is None else held[half].index(b) for b in rounds_[half]] for half in (0, 1)]
        for rounds_ in rounds
    ]


def split_kernel(bits, values, near, far, far_sum, sems):
    part = far.shape[1]
    step = 512
    copies = []
    for i, (out, start) in enumerate(((far, bits[0]), (near, 1 - bits[0]))):
        columns = pl.ds(pl.multiple_of(start * part, 128), part)
        copies.append(pltpu.make_async_copy(values.at[:, columns], out, sems.at[i]))
    for copy in copies:
        copy.start()
    copies[0].wait()

    @pl.loop(0, part // step)
    def _(j):
        columns = pl.ds(pl.multiple_of(j * step, step), step)
        block = far[:, columns].astype(jnp.float32)
        far_sum[:, columns] = jnp.sum(block, axis=0, keepdims=True)

    copies[1].wait()


def block_product(left, right):
    return lax.dot_general(left, right, (((1,), (1,)), ((), ())), preferred_element_type=jnp.float32)


def sum_kernel(other, near, far_sum, partial):
    step = 512

    @pl.loop(0, near.shape[1] // step)
    def _(n):
        columns = pl.ds(pl.multiple_of(n * step, step), step)
        rows = other[:, columns].astype(jnp.float32) + near[:, columns].astype(jnp.float32)
        partial[:, columns] = far_sum[:, columns] + jnp.sum(rows, axis=0, keepdims=True)


def early_kernel(bits, other, edge, near, partial, centred, mean, own, *rest):
    sends, both = rest[:-1], rest[-1]
    rows, part = near.shape
    step = 512

    @pl.loop(0, part // step)
    def _(n):
        columns = pl.ds(pl.multiple_of(n * step, step), step)
        values = [block[:, columns].astype(jnp.float32) for block in (edge, near, other)]
        total = partial[:, columns] + jnp.sum(values[0], axis=0, keepdims=True)
        average = total * (1.0 / (4 * rows))
        mean[:, columns] = average
        for i in range(3):
            centred[i, :, columns] = (values[i] - average).astype(jnp.bfloat16)

    for core in (0, 1):
        for place, (i, j) in enumerate(EARLY_SUMS[core]):
            both[core, place] = block_product(centred[i], centred[j])
    own[...] = both[bits[1]]
    for place, send in enumerate(sends):
        send[...] = both[1 - bits[1], pl.ds(place, 1), :, :]


def late_products(core, last, centred, out):
    for place, (_, j) in enumerate(LATE_SUMS[core]):
        out[place] = block_product(last[...], last[...] if j == 3 else centred[j])


def late_kernel(bits, far_edge, mean, centred, *rest):
    last, send = rest[(len(rest) - 2) // 2 :][:2]
    last[...] = (far_edge[...].astype(jnp.float32) - mean[...]).astype(jnp.bfloat16)
    for core in (0, 1):

        @pl.when(bits[1] != core)
        def _():
            late_products(core, last, centred, send)


def keep_kernel(bits, last, centred, own):
    for core in (0, 1):

        @pl.when(bits[1] == core)
        def _():
            late_products(core, last, centred, own)


def combine_kernel(flips, scale, pieces, spares, bits, places, own, *rest):
    others, spare = rest[:pieces], rest[pieces : pieces + spares]
    outs, held = rest[pieces + spares : -1], rest[-1]
    count = own.shape[0]
    for i in range(count):
        other = others[0][i] if pieces == 1 else others[i][0]
        held[i] = (own[i] + other) * scale
    for n, i in enumerate(flips):
        held[count + n] = held[i].T
    for i in range(spares):
        held[count + len(flips) + i] = spare[i][...]
    for r, out in enumerate(outs):
        out[...] = held[places[r, bits[1], bits[2]]]


def shape_of(shape, dtype):
    return jax.ShapeDtypeStruct(shape, dtype)


def combine(bits, own, others, flips, spares, held, places, samples):
    rows = own.shape[1]
    return pl.pallas_call(
        functools.partial(combine_kernel, flips, 1.0 / samples, len(others), len(spares)),
        out_shape=[shape_of((rows, rows), jnp.float32)] * len(places),
        in_specs=[SMEM, SMEM] + [VMEM] * (1 + len(others) + len(spares)),
        out_specs=[VMEM] * len(places),
        scratch_shapes=[pltpu.VMEM((len(held[0]), rows, rows), jnp.float32)],
        compiler_params=LIMIT,
        cost_estimate=BRIEF,
    )(bits, jnp.array(places, jnp.int32), own, *others, *spares)


def two_centres(log_derivs, shift):
    local_rows, local_params = log_derivs.shape
    samples = local_rows * 4
    part = local_params // 2
    everyone = ("row", "col", "half")
    row, col, half = (lax.axis_index(name) for name in everyone)
    side = (row >= 2).astype(jnp.int32)
    bits = jnp.stack([side, half, jnp.bitwise_xor(col, side)]).astype(jnp.int32)

    to_centre = [(1, 2), (2, 1)]
    to_own = [(0, 1), (3, 2)]
    to_far = [(0, 2), (3, 1)]
    centres = [(r * 2 + h, r * 2 + 1 - h) for r in (1, 2) for h in (0, 1)]

    def swap(value):
        return lax.ppermute(value, ("row", "half"), centres)

    def send(value, blocks):
        return lax.ppermute(value.astype(jnp.float16), everyone, round_pairs(blocks))

    near, far, far_sum = pl.pallas_call(
        split_kernel,
        out_shape=[
            shape_of((local_rows, part), jnp.bfloat16),
            shape_of((local_rows, part), jnp.bfloat16),
            shape_of((1, part), jnp.float32),
        ],
        in_specs=[SMEM, ANY],
        out_specs=[VMEM] * 3,
        scratch_shapes=[pltpu.SemaphoreType.DMA((2,))],
        compiler_params=LIMIT,
        cost_estimate=BRIEF,
    )(bits, log_derivs)
    from_centre = lax.ppermute(far, "row", to_centre)
    from_sum = lax.ppermute(far_sum, "row", to_far)
    from_edge = lax.ppermute(near, "row", to_own)
    from_far_edge = lax.ppermute(far, "row", to_far)

    partial = pl.pallas_call(
        sum_kernel,
        out_shape=shape_of((1, part), jnp.float32),
        in_specs=[VMEM] * 3,
        out_specs=VMEM,
        compiler_params=LIMIT,
        cost_estimate=LONG,
    )(from_centre, near, from_sum)
    early_blocks = (3, local_rows, local_rows)
    centred, mean, own, *others = pl.pallas_call(
        early_kernel,
        out_shape=[
            shape_of((3, local_rows, part), jnp.bfloat16),
            shape_of((1, part), jnp.float32),
            shape_of(early_blocks, jnp.float32),
        ]
        + [shape_of((1, local_rows, local_rows), jnp.float32)] * 3,
        in_specs=[SMEM] + [VMEM] * 4,
        out_specs=[VMEM] * 6,
        scratch_shapes=[pltpu.VMEM((2,) + early_blocks, jnp.float32)],
        compiler_params=LIMIT,
        cost_estimate=BRIEF,
    )(bits, from_centre, from_edge, near, partial)
    others = [swap(other) for other in others]
    places = held_place(EARLY_HELD, NEAR_ROUNDS + MIDDLE_ROUNDS)
    places += [[[i] * 2] * 2 for i in range(3)]
    early = list(combine(bits, own, others, (1, 2), (), EARLY_HELD, places, samples))
    near_blocks, middle_blocks, spares = early[:2], early[2:3], early[3:]
    arrived = [send(value, blocks) for value, blocks in zip(near_blocks, NEAR_ROUNDS)]
    summed = sum(block.astype(jnp.float32) for block in arrived)

    late_blocks = shape_of((2, local_rows, local_rows), jnp.float32)
    handed = [summed] + middle_blocks
    last, other, summed, *middle_blocks = pl.pallas_call(
        late_kernel,
        out_shape=[shape_of((local_rows, part), jnp.bfloat16), late_blocks]
        + [shape_of(value.shape, value.dtype) for value in handed],
        in_specs=[SMEM] + [VMEM] * 3 + [ANY] * len(handed),
        out_specs=[VMEM] * 2 + [ANY] * len(handed),
        input_output_aliases={4 + i: 2 + i for i in range(len(handed))},
        compiler_params=LIMIT,
        cost_estimate=BRIEF,
    )(bits, from_far_edge, mean, centred, *handed)
    own = pl.pallas_call(
        keep_kernel,
        out_shape=late_blocks,
        in_specs=[SMEM] + [VMEM] * 2,
        out_specs=VMEM,
        compiler_params=LIMIT,
        cost_estimate=BRIEF,
    )(bits, last, centred)
    other = swap(other)
    arrived = [send(value, blocks) for value, blocks in zip(middle_blocks, MIDDLE_ROUNDS)]
    places = held_place(LATE_HELD, LATE_ROUNDS)
    late = combine(bits, own, [other], (0, 1), spares, LATE_HELD, places, samples)
    arrived += [send(value, blocks) for value, blocks in zip(late, LATE_ROUNDS)]
    summed = summed + sum(block.astype(jnp.float32) for block in reversed(arrived))
    return add_shift(summed, 1, shift, local_rows)


def solution(mesh):
    shape = mesh.shape
    small = shape["row"] == 4 and shape["col"] == 2 and shape["half"] == 2
    return jax.shard_map(
        two_centres if small else gathered,
        mesh=mesh,
        in_specs=(P(("groups", "row"), ("col", "half")), P("groups")),
        out_specs=P(("groups", "row"), ("col", "half")),
        check_vma=False,
    )
```

```python
import functools

import jax
import jax.numpy as jnp
from jax import lax
from jax.experimental import pallas as pl
from jax.experimental.pallas import tpu as pltpu
from jax.sharding import PartitionSpec as P


def pair_product(left, right):
    return jnp.einsum("ip,jp->ij", left, right, preferred_element_type=jnp.float32)


def add_shift(summed, samples, shift, local_rows):
    width = summed.shape[1]
    first_row = lax.axis_index("row") * local_rows
    block = lax.axis_index("col") * lax.axis_size("half") + lax.axis_index("half")
    row_ids = first_row + lax.broadcasted_iota(jnp.int32, (local_rows, width), 0)
    column_ids = block * width + lax.broadcasted_iota(jnp.int32, (local_rows, width), 1)
    return summed / samples + jnp.where(row_ids == column_ids, shift[0], 0.0)


def gathered(log_derivs, shift):
    local_rows = log_derivs.shape[0]
    samples = local_rows * lax.axis_size("row")
    rows = lax.all_gather(log_derivs, "row", axis=0, tiled=True).astype(jnp.float32)
    mean = jnp.sum(rows, axis=0) / samples
    centered = (rows - mean[None, :]).astype(jnp.bfloat16)
    own = (log_derivs.astype(jnp.float32) - mean[None, :]).astype(jnp.bfloat16)
    tile = pair_product(own, centered)
    summed = lax.psum_scatter(tile, ("col", "half"), scatter_dimension=1, tiled=True)
    return add_shift(summed, samples, shift, local_rows)


NEAR_ROUNDS = (
    (((1, 1), (0, 2)), ((1, 0), (1, 2))),
    (((0, 2), (1, 1)), ((1, 2), (1, 0))),
)
FAR_ROUNDS = (
    (((2, 0), (0, 0)), ((0, 1), (2, 2))),
    (((0, 0), (2, 0)), ((2, 2), (0, 1))),
)
LATE_ROUNDS = (
    (((1, 3), (0, 3)), ((3, 3), (3, 2))),
    (((3, 1), (3, 0)), ((2, 1), (2, 3))),
    (((0, 3), (1, 3)), ((3, 2), (3, 3))),
    (((3, 0), (3, 1)), ((2, 3), (2, 1))),
)
EARLY_SUMS = (((1, 1), (2, 0), (0, 0)), ((2, 2), (0, 1), (2, 1)))
EARLY_HELD = (
    ((1, 1), (2, 0), (0, 0), (0, 2), (0, 0)),
    ((2, 2), (0, 1), (2, 1), (1, 0), (1, 2)),
)
SPARE = 2
LATE_SUMS = (((3, 0), (3, 1)), ((3, 2), (3, 3)))
LATE_HELD = (
    ((3, 0), (3, 1), (0, 3), (1, 3), (0, 0)),
    ((3, 2), (3, 3), (2, 3), (3, 3), (2, 1)),
)
VMEM = pl.BlockSpec(memory_space=pltpu.VMEM)
SMEM = pl.BlockSpec(memory_space=pltpu.SMEM)
ANY = pl.BlockSpec(memory_space=pl.ANY)
LIMIT = pltpu.CompilerParams(vmem_limit_bytes=40 * 2**20)
BRIEF = pl.CostEstimate(flops=1024, bytes_accessed=1024, transcendentals=0)
LONG = pl.CostEstimate(flops=3 * 2**31, bytes_accessed=1024, transcendentals=0)


def device_index(row, col, half):
    return (row * 2 + col) * 2 + half


def round_pairs(blocks):
    pairs = []
    for side in (0, 1):
        for turn in (0, 1):
            for half in (0, 1):
                block = blocks[half][turn]
                if block is None:
                    continue
                i, j = (3 - b if side else b for b in block)
                source = device_index(1 + side, turn ^ side, half)
                pairs.append((source, device_index(i, j // 2, j % 2)))
    return pairs


def held_place(held, rounds):
    return [
        [[0 if b is None else held[half].index(b) for b in rounds_[half]] for half in (0, 1)]
        for rounds_ in rounds
    ]


def split_kernel(bits, values, near, far, far_sum, sems):
    part = far.shape[1]
    step = 512
    copies = []
    for i, (out, start) in enumerate(((far, bits[0]), (near, 1 - bits[0]))):
        columns = pl.ds(pl.multiple_of(start * part, 128), part)
        copies.append(pltpu.make_async_copy(values.at[:, columns], out, sems.at[i]))
    for copy in copies:
        copy.start()
    copies[0].wait()

    @pl.loop(0, part // step)
    def _(j):
        columns = pl.ds(pl.multiple_of(j * step, step), step)
        block = far[:, columns].astype(jnp.float32)
        far_sum[:, columns] = jnp.sum(block, axis=0, keepdims=True)

    copies[1].wait()


def block_product(left, right):
    return lax.dot_general(left, right, (((1,), (1,)), ((), ())), preferred_element_type=jnp.float32)


def sum_kernel(other, near, far_sum, partial):
    step = 512

    @pl.loop(0, near.shape[1] // step)
    def _(n):
        columns = pl.ds(pl.multiple_of(n * step, step), step)
        rows = other[:, columns].astype(jnp.float32) + near[:, columns].astype(jnp.float32)
        partial[:, columns] = far_sum[:, columns] + jnp.sum(rows, axis=0, keepdims=True)


def early_kernel(bits, other, edge, near, partial, centred, mean, own, *rest):
    sends, both = rest[:-1], rest[-1]
    rows, part = near.shape
    step = 512

    @pl.loop(0, part // step)
    def _(n):
        columns = pl.ds(pl.multiple_of(n * step, step), step)
        values = [block[:, columns].astype(jnp.float32) for block in (edge, near, other)]
        total = partial[:, columns] + jnp.sum(values[0], axis=0, keepdims=True)
        average = total * (1.0 / (4 * rows))
        mean[:, columns] = average
        for i in range(3):
            centred[i, :, columns] = (values[i] - average).astype(jnp.bfloat16)

    for core in (0, 1):
        for place, (i, j) in enumerate(EARLY_SUMS[core]):
            both[core, place] = block_product(centred[i], centred[j])
    own[...] = both[bits[1]]
    for place, send in enumerate(sends):
        send[...] = both[1 - bits[1], pl.ds(place, 1), :, :]


def late_products(core, last, centred, out):
    for place, (_, j) in enumerate(LATE_SUMS[core]):
        out[place] = block_product(last[...], last[...] if j == 3 else centred[j])


def late_kernel(bits, far_edge, mean, centred, *rest):
    last, send = rest[(len(rest) - 2) // 2 :][:2]
    last[...] = (far_edge[...].astype(jnp.float32) - mean[...]).astype(jnp.bfloat16)
    for core in (0, 1):

        @pl.when(bits[1] != core)
        def _():
            late_products(core, last, centred, send)


def keep_kernel(bits, last, centred, own):
    for core in (0, 1):

        @pl.when(bits[1] == core)
        def _():
            late_products(core, last, centred, own)


def combine_kernel(flips, scale, pieces, spares, bits, places, own, *rest):
    others, spare = rest[:pieces], rest[pieces : pieces + spares]
    outs, held = rest[pieces + spares : -1], rest[-1]
    count = own.shape[0]
    for i in range(count):
        other = others[0][i] if pieces == 1 else others[i][0]
        held[i] = (own[i] + other) * scale
    for n, i in enumerate(flips):
        held[count + n] = held[i].T
    for i in range(spares):
        held[count + len(flips) + i] = spare[i][...]
    for r, out in enumerate(outs):
        out[...] = held[places[r, bits[1], bits[2]]]


def shape_of(shape, dtype):
    return jax.ShapeDtypeStruct(shape, dtype)


def combine(bits, own, others, flips, spares, held, places, samples):
    rows = own.shape[1]
    return pl.pallas_call(
        functools.partial(combine_kernel, flips, 1.0 / samples, len(others), len(spares)),
        out_shape=[shape_of((rows, rows), jnp.float32)] * len(places),
        in_specs=[SMEM, SMEM] + [VMEM] * (1 + len(others) + len(spares)),
        out_specs=[VMEM] * len(places),
        scratch_shapes=[pltpu.VMEM((len(held[0]), rows, rows), jnp.float32)],
        compiler_params=LIMIT,
        cost_estimate=BRIEF,
    )(bits, jnp.array(places, jnp.int32), own, *others, *spares)


def two_centres(log_derivs, shift):
    local_rows, local_params = log_derivs.shape
    samples = local_rows * 4
    part = local_params // 2
    everyone = ("row", "col", "half")
    row, col, half = (lax.axis_index(name) for name in everyone)
    side = (row >= 2).astype(jnp.int32)
    bits = jnp.stack([side, half, jnp.bitwise_xor(col, side)]).astype(jnp.int32)

    to_centre = [(1, 2), (2, 1)]
    to_own = [(0, 1), (3, 2)]
    to_far = [(0, 2), (3, 1)]
    centres = [(r * 2 + h, r * 2 + 1 - h) for r in (1, 2) for h in (0, 1)]

    def swap(value):
        return lax.ppermute(value, ("row", "half"), centres)

    def send(value, blocks):
        return lax.ppermute(value.astype(jnp.float16), everyone, round_pairs(blocks))

    near, far, far_sum = pl.pallas_call(
        split_kernel,
        out_shape=[
            shape_of((local_rows, part), jnp.bfloat16),
            shape_of((local_rows, part), jnp.bfloat16),
            shape_of((1, part), jnp.float32),
        ],
        in_specs=[SMEM, ANY],
        out_specs=[VMEM] * 3,
        scratch_shapes=[pltpu.SemaphoreType.DMA((2,))],
        compiler_params=LIMIT,
        cost_estimate=BRIEF,
    )(bits, log_derivs)
    from_centre = lax.ppermute(far, "row", to_centre)
    from_sum = lax.ppermute(far_sum, "row", to_far)
    from_edge = lax.ppermute(near, "row", to_own)
    from_far_edge = lax.ppermute(far, "row", to_far)

    partial = pl.pallas_call(
        sum_kernel,
        out_shape=shape_of((1, part), jnp.float32),
        in_specs=[VMEM] * 3,
        out_specs=VMEM,
        compiler_params=LIMIT,
        cost_estimate=LONG,
    )(from_centre, near, from_sum)
    early_blocks = (3, local_rows, local_rows)
    centred, mean, own, *others = pl.pallas_call(
        early_kernel,
        out_shape=[
            shape_of((3, local_rows, part), jnp.bfloat16),
            shape_of((1, part), jnp.float32),
            shape_of(early_blocks, jnp.float32),
        ]
        + [shape_of((1, local_rows, local_rows), jnp.float32)] * 3,
        in_specs=[SMEM] + [VMEM] * 4,
        out_specs=[VMEM] * 6,
        scratch_shapes=[pltpu.VMEM((2,) + early_blocks, jnp.float32)],
        compiler_params=LIMIT,
        cost_estimate=BRIEF,
    )(bits, from_centre, from_edge, near, partial)
    others = [swap(other) for other in others]
    places = held_place(EARLY_HELD, NEAR_ROUNDS + FAR_ROUNDS) + [[[SPARE] * 2] * 2]
    *early, spare = combine(bits, own, others, (1, 2), (), EARLY_HELD, places, samples)
    near_blocks, far_blocks = early[: len(NEAR_ROUNDS)], early[len(NEAR_ROUNDS) :]
    arrived = [send(value, blocks) for value, blocks in zip(near_blocks, NEAR_ROUNDS)]
    summed = sum(block.astype(jnp.float32) for block in arrived)

    late_blocks = shape_of((2, local_rows, local_rows), jnp.float32)
    handed = [summed] + far_blocks
    last, other, summed, *far_blocks = pl.pallas_call(
        late_kernel,
        out_shape=[shape_of((local_rows, part), jnp.bfloat16), late_blocks]
        + [shape_of(value.shape, value.dtype) for value in handed],
        in_specs=[SMEM] + [VMEM] * 3 + [ANY] * len(handed),
        out_specs=[VMEM] * 2 + [ANY] * len(handed),
        input_output_aliases={4 + i: 2 + i for i in range(len(handed))},
        compiler_params=LIMIT,
        cost_estimate=BRIEF,
    )(bits, from_far_edge, mean, centred, *handed)
    own = pl.pallas_call(
        keep_kernel,
        out_shape=late_blocks,
        in_specs=[SMEM] + [VMEM] * 2,
        out_specs=VMEM,
        compiler_params=LIMIT,
        cost_estimate=BRIEF,
    )(bits, last, centred)
    other = swap(other)
    arrived = [send(value, blocks) for value, blocks in zip(far_blocks, FAR_ROUNDS)]
    places = held_place(LATE_HELD, LATE_ROUNDS)
    late = combine(bits, own, [other], (0, 1), (spare,), LATE_HELD, places, samples)
    arrived += [send(value, blocks) for value, blocks in zip(late, LATE_ROUNDS)]
    summed = summed + sum(block.astype(jnp.float32) for block in reversed(arrived))
    return add_shift(summed, 1, shift, local_rows)


def solution(mesh):
    shape = mesh.shape
    small = shape["row"] == 4 and shape["col"] == 2 and shape["half"] == 2
    return jax.shard_map(
        two_centres if small else gathered,
        mesh=mesh,
        in_specs=(P(("groups", "row"), ("col", "half")), P("groups")),
        out_specs=P(("groups", "row"), ("col", "half")),
        check_vma=False,
    )
```

```python
import functools

import jax
import jax.numpy as jnp
from jax import lax
from jax.experimental import pallas as pl
from jax.experimental.pallas import tpu as pltpu
from jax.sharding import PartitionSpec as P


def pair_product(left, right):
    return jnp.einsum("ip,jp->ij", left, right, preferred_element_type=jnp.float32)


def add_shift(summed, samples, shift, local_rows):
    width = summed.shape[1]
    first_row = lax.axis_index("row") * local_rows
    block = lax.axis_index("col") * lax.axis_size("half") + lax.axis_index("half")
    row_ids = first_row + lax.broadcasted_iota(jnp.int32, (local_rows, width), 0)
    column_ids = block * width + lax.broadcasted_iota(jnp.int32, (local_rows, width), 1)
    return summed / samples + jnp.where(row_ids == column_ids, shift[0], 0.0)


def gathered(log_derivs, shift):
    local_rows = log_derivs.shape[0]
    samples = local_rows * lax.axis_size("row")
    rows = lax.all_gather(log_derivs, "row", axis=0, tiled=True).astype(jnp.float32)
    mean = jnp.sum(rows, axis=0) / samples
    centered = (rows - mean[None, :]).astype(jnp.bfloat16)
    own = (log_derivs.astype(jnp.float32) - mean[None, :]).astype(jnp.bfloat16)
    tile = pair_product(own, centered)
    summed = lax.psum_scatter(tile, ("col", "half"), scatter_dimension=1, tiled=True)
    return add_shift(summed, samples, shift, local_rows)


NEAR_ROUNDS = (
    (((1, 0), (1, 1)), ((0, 2), (1, 2))),
    (((1, 1), (1, 0)), ((1, 2), (0, 2))),
)
FAR_ROUNDS = (
    (((0, 0), (0, 1)), ((2, 2), (2, 0))),
    (((0, 1), (0, 0)), ((2, 0), (2, 2))),
)
LATE_ROUNDS = (
    (((1, 3), (0, 3)), ((2, 1), (2, 3))),
    (((0, 3), (1, 3)), ((2, 3), (2, 1))),
    (((3, 1), (3, 0)), ((3, 3), (3, 2))),
    (((3, 0), (3, 1)), ((3, 2), (3, 3))),
)
EARLY_SUMS = (((0, 0), (0, 1), (1, 1)), ((2, 2), (2, 0), (2, 1)))
EARLY_HELD = (
    ((0, 0), (0, 1), (1, 1), (1, 0), (1, 1)),
    ((2, 2), (2, 0), (2, 1), (0, 2), (1, 2)),
)
SPARE = 2
LATE_SUMS = (((3, 0), (3, 1)), ((3, 2), (3, 3)))
LATE_HELD = (
    ((3, 0), (3, 1), (0, 3), (1, 3), (1, 1)),
    ((3, 2), (3, 3), (2, 3), (3, 3), (2, 1)),
)
VMEM = pl.BlockSpec(memory_space=pltpu.VMEM)
SMEM = pl.BlockSpec(memory_space=pltpu.SMEM)
ANY = pl.BlockSpec(memory_space=pl.ANY)
LIMIT = pltpu.CompilerParams(vmem_limit_bytes=40 * 2**20)
BRIEF = pl.CostEstimate(flops=1024, bytes_accessed=1024, transcendentals=0)
LONG = pl.CostEstimate(flops=3 * 2**31, bytes_accessed=1024, transcendentals=0)


def device_index(row, col, half):
    return (row * 2 + col) * 2 + half


def round_pairs(blocks):
    pairs = []
    for side in (0, 1):
        for turn in (0, 1):
            for half in (0, 1):
                block = blocks[half][turn]
                if block is None:
                    continue
                i, j = (3 - b if side else b for b in block)
                source = device_index(1 + side, turn ^ side, half)
                pairs.append((source, device_index(i, j // 2, j % 2)))
    return pairs


def held_place(held, rounds):
    return [
        [[0 if b is None else held[half].index(b) for b in rounds_[half]] for half in (0, 1)]
        for rounds_ in rounds
    ]


def split_kernel(bits, values, near, far, far_sum, sems):
    part = far.shape[1]
    step = 512
    copies = []
    for i, (out, start) in enumerate(((far, bits[0]), (near, 1 - bits[0]))):
        columns = pl.ds(pl.multiple_of(start * part, 128), part)
        copies.append(pltpu.make_async_copy(values.at[:, columns], out, sems.at[i]))
    for copy in copies:
        copy.start()
    copies[0].wait()

    @pl.loop(0, part // step)
    def _(j):
        columns = pl.ds(pl.multiple_of(j * step, step), step)
        block = far[:, columns].astype(jnp.float32)
        far_sum[:, columns] = jnp.sum(block, axis=0, keepdims=True)

    copies[1].wait()


def block_product(left, right):
    return lax.dot_general(left, right, (((1,), (1,)), ((), ())), preferred_element_type=jnp.float32)


def sum_kernel(other, near, far_sum, partial):
    step = 512

    @pl.loop(0, near.shape[1] // step)
    def _(n):
        columns = pl.ds(pl.multiple_of(n * step, step), step)
        rows = other[:, columns].astype(jnp.float32) + near[:, columns].astype(jnp.float32)
        partial[:, columns] = far_sum[:, columns] + jnp.sum(rows, axis=0, keepdims=True)


def early_kernel(bits, other, edge, near, partial, centred, mean, own, *rest):
    sends, both = rest[:-1], rest[-1]
    rows, part = near.shape
    step = 512

    @pl.loop(0, part // step)
    def _(n):
        columns = pl.ds(pl.multiple_of(n * step, step), step)
        values = [block[:, columns].astype(jnp.float32) for block in (edge, near, other)]
        total = partial[:, columns] + jnp.sum(values[0], axis=0, keepdims=True)
        average = total * (1.0 / (4 * rows))
        mean[:, columns] = average
        for i in range(3):
            centred[i, :, columns] = (values[i] - average).astype(jnp.bfloat16)

    for core in (0, 1):
        for place, (i, j) in enumerate(EARLY_SUMS[core]):
            both[core, place] = block_product(centred[i], centred[j])
    own[...] = both[bits[1]]
    for place, send in enumerate(sends):
        send[...] = both[1 - bits[1], pl.ds(place, 1), :, :]


def late_products(core, last, centred, out):
    for place, (_, j) in enumerate(LATE_SUMS[core]):
        product = block_product(last[...], last[...] if j == 3 else centred[j])
        out[place] = product * (1.0 / (4 * last.shape[0]))


def late_kernel(bits, far_edge, mean, centred, *rest):
    last, send = rest[(len(rest) - 2) // 2 :][:2]
    last[...] = (far_edge[...].astype(jnp.float32) - mean[...]).astype(jnp.bfloat16)
    for core in (0, 1):

        @pl.when(bits[1] != core)
        def _():
            late_products(core, last, centred, send)


def keep_kernel(bits, last, centred, own):
    for core in (0, 1):

        @pl.when(bits[1] == core)
        def _():
            late_products(core, last, centred, own)


def combine_kernel(flips, scale, pieces, spares, bits, places, own, *rest):
    others, spare = rest[:pieces], rest[pieces : pieces + spares]
    outs, held = rest[pieces + spares : -1], rest[-1]
    count = own.shape[0]
    for i in range(count):
        other = others[0][i] if pieces == 1 else others[i][0]
        held[i] = (own[i] + other) * scale
    for n, i in enumerate(flips):
        held[count + n] = held[i].T
    for i in range(spares):
        held[count + len(flips) + i] = spare[i][...]
    for r, out in enumerate(outs):
        out[...] = held[places[r, bits[1], bits[2]]]


def shape_of(shape, dtype):
    return jax.ShapeDtypeStruct(shape, dtype)


def combine(bits, own, others, flips, spares, held, places, samples):
    rows = own.shape[1]
    return pl.pallas_call(
        functools.partial(combine_kernel, flips, 1.0 / samples, len(others), len(spares)),
        out_shape=[shape_of((rows, rows), jnp.float32)] * len(places),
        in_specs=[SMEM, SMEM] + [VMEM] * (1 + len(others) + len(spares)),
        out_specs=[VMEM] * len(places),
        scratch_shapes=[pltpu.VMEM((len(held[0]), rows, rows), jnp.float32)],
        compiler_params=LIMIT,
        cost_estimate=BRIEF,
    )(bits, jnp.array(places, jnp.int32), own, *others, *spares)


def two_centres(log_derivs, shift):
    local_rows, local_params = log_derivs.shape
    samples = local_rows * 4
    part = local_params // 2
    everyone = ("row", "col", "half")
    row, col, half = (lax.axis_index(name) for name in everyone)
    side = (row >= 2).astype(jnp.int32)
    bits = jnp.stack([side, half, jnp.bitwise_xor(col, side)]).astype(jnp.int32)

    to_centre = [(1, 2), (2, 1)]
    to_own = [(0, 1), (3, 2)]
    to_far = [(0, 2), (3, 1)]
    centres = [(r * 2 + h, r * 2 + 1 - h) for r in (1, 2) for h in (0, 1)]

    def swap(value):
        return lax.ppermute(value, ("row", "half"), centres)

    def send(value, blocks):
        return lax.ppermute(value.astype(jnp.float16), everyone, round_pairs(blocks))

    near, far, far_sum = pl.pallas_call(
        split_kernel,
        out_shape=[
            shape_of((local_rows, part), jnp.bfloat16),
            shape_of((local_rows, part), jnp.bfloat16),
            shape_of((1, part), jnp.float32),
        ],
        in_specs=[SMEM, ANY],
        out_specs=[VMEM] * 3,
        scratch_shapes=[pltpu.SemaphoreType.DMA((2,))],
        compiler_params=LIMIT,
        cost_estimate=BRIEF,
    )(bits, log_derivs)
    from_centre = lax.ppermute(far, "row", to_centre)
    from_sum = lax.ppermute(far_sum, "row", to_far)
    from_edge = lax.ppermute(near, "row", to_own)
    from_far_edge = lax.ppermute(far, "row", to_far)

    partial = pl.pallas_call(
        sum_kernel,
        out_shape=shape_of((1, part), jnp.float32),
        in_specs=[VMEM] * 3,
        out_specs=VMEM,
        compiler_params=LIMIT,
        cost_estimate=LONG,
    )(from_centre, near, from_sum)
    early_blocks = (3, local_rows, local_rows)
    centred, mean, own, *others = pl.pallas_call(
        early_kernel,
        out_shape=[
            shape_of((3, local_rows, part), jnp.bfloat16),
            shape_of((1, part), jnp.float32),
            shape_of(early_blocks, jnp.float32),
        ]
        + [shape_of((1, local_rows, local_rows), jnp.float32)] * 3,
        in_specs=[SMEM] + [VMEM] * 4,
        out_specs=[VMEM] * 6,
        scratch_shapes=[pltpu.VMEM((2,) + early_blocks, jnp.float32)],
        compiler_params=LIMIT,
        cost_estimate=BRIEF,
    )(bits, from_centre, from_edge, near, partial)
    others = [swap(other) for other in others]
    places = held_place(EARLY_HELD, NEAR_ROUNDS + FAR_ROUNDS) + [[[SPARE] * 2] * 2]
    *early, spare = combine(bits, own, others, (1, 2), (), EARLY_HELD, places, samples)
    near_blocks, far_blocks = early[: len(NEAR_ROUNDS)], early[len(NEAR_ROUNDS) :]
    arrived = [send(value, blocks) for value, blocks in zip(near_blocks, NEAR_ROUNDS)]
    summed = sum(block.astype(jnp.float32) for block in arrived)

    late_blocks = shape_of((2, local_rows, local_rows), jnp.float32)
    handed = [summed] + far_blocks
    last, other, summed, *far_blocks = pl.pallas_call(
        late_kernel,
        out_shape=[shape_of((local_rows, part), jnp.bfloat16), late_blocks]
        + [shape_of(value.shape, value.dtype) for value in handed],
        in_specs=[SMEM] + [VMEM] * 3 + [ANY] * len(handed),
        out_specs=[VMEM] * 2 + [ANY] * len(handed),
        input_output_aliases={4 + i: 2 + i for i in range(len(handed))},
        compiler_params=LIMIT,
        cost_estimate=BRIEF,
    )(bits, from_far_edge, mean, centred, *handed)
    own = pl.pallas_call(
        keep_kernel,
        out_shape=late_blocks,
        in_specs=[SMEM] + [VMEM] * 2,
        out_specs=VMEM,
        compiler_params=LIMIT,
        cost_estimate=BRIEF,
    )(bits, last, centred)
    other = swap(other.astype(jnp.float16)).astype(jnp.float32)
    arrived = [send(value, blocks) for value, blocks in zip(far_blocks, FAR_ROUNDS)]
    places = held_place(LATE_HELD, LATE_ROUNDS)
    late = combine(bits, own, [other], (0, 1), (spare,), LATE_HELD, places, 1)
    arrived += [send(value, blocks) for value, blocks in zip(late, LATE_ROUNDS)]
    summed = summed + sum(block.astype(jnp.float32) for block in reversed(arrived))
    return add_shift(summed, 1, shift, local_rows)


def solution(mesh):
    shape = mesh.shape
    small = shape["row"] == 4 and shape["col"] == 2 and shape["half"] == 2
    return jax.shard_map(
        two_centres if small else gathered,
        mesh=mesh,
        in_specs=(P(("groups", "row"), ("col", "half")), P("groups")),
        out_specs=P(("groups", "row"), ("col", "half")),
        check_vma=False,
    )
```

```python
import functools

import jax
import jax.numpy as jnp
from jax import lax
from jax.experimental import pallas as pl
from jax.experimental.pallas import tpu as pltpu
from jax.sharding import PartitionSpec as P


def pair_product(left, right):
    return jnp.einsum("ip,jp->ij", left, right, preferred_element_type=jnp.float32)


def add_shift(summed, samples, shift, local_rows):
    width = summed.shape[1]
    first_row = lax.axis_index("row") * local_rows
    block = lax.axis_index("col") * lax.axis_size("half") + lax.axis_index("half")
    row_ids = first_row + lax.broadcasted_iota(jnp.int32, (local_rows, width), 0)
    column_ids = block * width + lax.broadcasted_iota(jnp.int32, (local_rows, width), 1)
    return summed / samples + jnp.where(row_ids == column_ids, shift[0], 0.0)


def gathered(log_derivs, shift):
    local_rows = log_derivs.shape[0]
    samples = local_rows * lax.axis_size("row")
    rows = lax.all_gather(log_derivs, "row", axis=0, tiled=True).astype(jnp.float32)
    mean = jnp.sum(rows, axis=0) / samples
    centered = (rows - mean[None, :]).astype(jnp.bfloat16)
    own = (log_derivs.astype(jnp.float32) - mean[None, :]).astype(jnp.bfloat16)
    tile = pair_product(own, centered)
    summed = lax.psum_scatter(tile, ("col", "half"), scatter_dimension=1, tiled=True)
    return add_shift(summed, samples, shift, local_rows)


NEAR_ROUNDS = (
    (((1, 1), (0, 2)), ((1, 0), (1, 2))),
    (((0, 2), (1, 1)), ((1, 2), (1, 0))),
)
EDGE_ROUNDS = (
    (((0, 0), None), (None, (0, 1))),
    ((None, (0, 0)), ((0, 1), None)),
)
LATE_ROUNDS = (
    (((0, 3), (1, 3)), ((2, 2), (2, 3))),
    (((1, 3), (0, 3)), ((2, 1), (2, 2))),
    (((2, 0), (3, 0)), ((2, 3), (2, 1))),
    (((3, 1), (2, 0)), ((3, 3), (3, 2))),
    (((3, 0), (3, 1)), ((3, 2), (3, 3))),
)
EARLY_SUMS = (((1, 1), (2, 0), (0, 0)), ((2, 1), (0, 1), (2, 2)))
EARLY_HELD = (
    ((1, 1), (2, 0), (0, 0), (1, 1), (0, 2)),
    ((2, 1), (0, 1), (2, 2), (1, 2), (1, 0)),
)
LATE_SUMS = (((3, 0), (3, 1)), ((3, 2), (3, 3)))
LATE_HELD = (
    ((3, 0), (3, 1), (0, 3), (1, 3)) + EARLY_SUMS[0],
    ((3, 2), (3, 3), (2, 3), (3, 3)) + EARLY_SUMS[1],
)
VMEM = pl.BlockSpec(memory_space=pltpu.VMEM)
SMEM = pl.BlockSpec(memory_space=pltpu.SMEM)
ANY = pl.BlockSpec(memory_space=pl.ANY)
LIMIT = pltpu.CompilerParams(vmem_limit_bytes=40 * 2**20)
BRIEF = pl.CostEstimate(flops=1024, bytes_accessed=1024, transcendentals=0)
LONG = pl.CostEstimate(flops=3 * 2**31, bytes_accessed=1024, transcendentals=0)


def device_index(row, col, half):
    return (row * 2 + col) * 2 + half


def round_pairs(blocks):
    pairs = []
    for side in (0, 1):
        for turn in (0, 1):
            for half in (0, 1):
                block = blocks[half][turn]
                if block is None:
                    continue
                i, j = (3 - b if side else b for b in block)
                source = device_index(1 + side, turn ^ side, half)
                pairs.append((source, device_index(i, j // 2, j % 2)))
    return pairs


def held_place(held, rounds):
    return [
        [[0 if b is None else held[half].index(b) for b in rounds_[half]] for half in (0, 1)]
        for rounds_ in rounds
    ]


def split_kernel(bits, values, near, far, far_sum, sems):
    part = far.shape[1]
    step = 512
    copies = []
    for i, (out, start) in enumerate(((far, bits[0]), (near, 1 - bits[0]))):
        columns = pl.ds(pl.multiple_of(start * part, 128), part)
        copies.append(pltpu.make_async_copy(values.at[:, columns], out, sems.at[i]))
    for copy in copies:
        copy.start()
    copies[0].wait()

    @pl.loop(0, part // step)
    def _(j):
        columns = pl.ds(pl.multiple_of(j * step, step), step)
        block = far[:, columns].astype(jnp.float32)
        far_sum[:, columns] = jnp.sum(block, axis=0, keepdims=True)

    copies[1].wait()


def block_product(left, right):
    return lax.dot_general(left, right, (((1,), (1,)), ((), ())), preferred_element_type=jnp.float32)


def sum_kernel(other, near, far_sum, partial):
    step = 512

    @pl.loop(0, near.shape[1] // step)
    def _(n):
        columns = pl.ds(pl.multiple_of(n * step, step), step)
        rows = other[:, columns].astype(jnp.float32) + near[:, columns].astype(jnp.float32)
        partial[:, columns] = far_sum[:, columns] + jnp.sum(rows, axis=0, keepdims=True)


def early_kernel(bits, other, edge, near, partial, centred, mean, own, *rest):
    sends, both = rest[:-1], rest[-1]
    rows, part = near.shape
    step = 512

    @pl.loop(0, part // step)
    def _(n):
        columns = pl.ds(pl.multiple_of(n * step, step), step)
        values = [block[:, columns].astype(jnp.float32) for block in (edge, near, other)]
        total = partial[:, columns] + jnp.sum(values[0], axis=0, keepdims=True)
        average = total * (1.0 / (4 * rows))
        mean[:, columns] = average
        for i in range(3):
            centred[i, :, columns] = (values[i] - average).astype(jnp.bfloat16)

    for core in (0, 1):
        for place, (i, j) in enumerate(EARLY_SUMS[core]):
            both[core, place] = block_product(centred[i], centred[j])
    own[...] = both[bits[1]]
    for place, send in enumerate(sends):
        send[...] = both[1 - bits[1], pl.ds(place, 1), :, :]


def late_products(core, last, centred, out):
    for place, (_, j) in enumerate(LATE_SUMS[core]):
        out[place] = block_product(last[...], last[...] if j == 3 else centred[j])


def late_kernel(bits, far_edge, mean, centred, *rest):
    last, send = rest[(len(rest) - 2) // 2 :][:2]
    last[...] = (far_edge[...].astype(jnp.float32) - mean[...]).astype(jnp.bfloat16)
    for core in (0, 1):

        @pl.when(bits[1] != core)
        def _():
            late_products(core, last, centred, send)


def keep_kernel(bits, last, centred, own):
    for core in (0, 1):

        @pl.when(bits[1] == core)
        def _():
            late_products(core, last, centred, own)


def combine_kernel(flips, scale, pieces, spares, bits, places, own, *rest):
    others, spare = rest[:pieces], rest[pieces : pieces + spares]
    outs, held = rest[pieces + spares : -1], rest[-1]
    count = own.shape[0]
    for i in range(count):
        other = others[0][i] if pieces == 1 else others[i][0]
        held[i] = (own[i] + other) * scale
    for n, i in enumerate(flips):
        held[count + n] = held[i].T
    for i in range(spares):
        held[count + len(flips) + i] = spare[i][...]
    for r, out in enumerate(outs):
        out[...] = held[places[r, bits[1], bits[2]]]


def shape_of(shape, dtype):
    return jax.ShapeDtypeStruct(shape, dtype)


def combine(bits, own, others, flips, spares, held, places, samples):
    rows = own.shape[1]
    return pl.pallas_call(
        functools.partial(combine_kernel, flips, 1.0 / samples, len(others), len(spares)),
        out_shape=[shape_of((rows, rows), jnp.float32)] * len(places),
        in_specs=[SMEM, SMEM] + [VMEM] * (1 + len(others) + len(spares)),
        out_specs=[VMEM] * len(places),
        scratch_shapes=[pltpu.VMEM((len(held[0]), rows, rows), jnp.float32)],
        compiler_params=LIMIT,
        cost_estimate=BRIEF,
    )(bits, jnp.array(places, jnp.int32), own, *others, *spares)


def two_centres(log_derivs, shift):
    local_rows, local_params = log_derivs.shape
    samples = local_rows * 4
    part = local_params // 2
    everyone = ("row", "col", "half")
    row, col, half = (lax.axis_index(name) for name in everyone)
    side = (row >= 2).astype(jnp.int32)
    bits = jnp.stack([side, half, jnp.bitwise_xor(col, side)]).astype(jnp.int32)

    to_centre = [(1, 2), (2, 1)]
    to_own = [(0, 1), (3, 2)]
    to_far = [(0, 2), (3, 1)]
    centres = [(r * 2 + h, r * 2 + 1 - h) for r in (1, 2) for h in (0, 1)]

    def swap(value):
        return lax.ppermute(value, ("row", "half"), centres)

    def send(value, blocks):
        return lax.ppermute(value.astype(jnp.float16), everyone, round_pairs(blocks))

    near, far, far_sum = pl.pallas_call(
        split_kernel,
        out_shape=[
            shape_of((local_rows, part), jnp.bfloat16),
            shape_of((local_rows, part), jnp.bfloat16),
            shape_of((1, part), jnp.float32),
        ],
        in_specs=[SMEM, ANY],
        out_specs=[VMEM] * 3,
        scratch_shapes=[pltpu.SemaphoreType.DMA((2,))],
        compiler_params=LIMIT,
        cost_estimate=BRIEF,
    )(bits, log_derivs)
    from_centre = lax.ppermute(far, "row", to_centre)
    from_sum = lax.ppermute(far_sum, "row", to_far)
    from_edge = lax.ppermute(near, "row", to_own)
    from_far_edge = lax.ppermute(far, "row", to_far)

    partial = pl.pallas_call(
        sum_kernel,
        out_shape=shape_of((1, part), jnp.float32),
        in_specs=[VMEM] * 3,
        out_specs=VMEM,
        compiler_params=LIMIT,
        cost_estimate=LONG,
    )(from_centre, near, from_sum)
    early_blocks = (3, local_rows, local_rows)
    centred, mean, own, *others = pl.pallas_call(
        early_kernel,
        out_shape=[
            shape_of((3, local_rows, part), jnp.bfloat16),
            shape_of((1, part), jnp.float32),
            shape_of(early_blocks, jnp.float32),
        ]
        + [shape_of((1, local_rows, local_rows), jnp.float32)] * 3,
        in_specs=[SMEM] + [VMEM] * 4,
        out_specs=[VMEM] * 6,
        scratch_shapes=[pltpu.VMEM((2,) + early_blocks, jnp.float32)],
        compiler_params=LIMIT,
        cost_estimate=BRIEF,
    )(bits, from_centre, from_edge, near, partial)
    others = [swap(other) for other in others]
    places = held_place(EARLY_HELD, NEAR_ROUNDS + EDGE_ROUNDS)
    places += [[[i] * 2] * 2 for i in range(3)]
    early = list(combine(bits, own, others, (0, 1), (), EARLY_HELD, places, samples))
    near_blocks, edge_blocks, spares = early[:2], early[2:4], early[4:]
    arrived = [send(value, blocks) for value, blocks in zip(near_blocks, NEAR_ROUNDS)]
    summed = sum(block.astype(jnp.float32) for block in arrived)

    late_blocks = shape_of((2, local_rows, local_rows), jnp.float32)
    handed = [summed] + edge_blocks
    last, other, summed, *edge_blocks = pl.pallas_call(
        late_kernel,
        out_shape=[shape_of((local_rows, part), jnp.bfloat16), late_blocks]
        + [shape_of(value.shape, value.dtype) for value in handed],
        in_specs=[SMEM] + [VMEM] * 3 + [ANY] * len(handed),
        out_specs=[VMEM] * 2 + [ANY] * len(handed),
        input_output_aliases={4 + i: 2 + i for i in range(len(handed))},
        compiler_params=LIMIT,
        cost_estimate=BRIEF,
    )(bits, from_far_edge, mean, centred, *handed)
    own = pl.pallas_call(
        keep_kernel,
        out_shape=late_blocks,
        in_specs=[SMEM] + [VMEM] * 2,
        out_specs=VMEM,
        compiler_params=LIMIT,
        cost_estimate=BRIEF,
    )(bits, last, centred)
    other = swap(other)
    arrived = [send(value, blocks) for value, blocks in zip(edge_blocks, EDGE_ROUNDS)]
    places = held_place(LATE_HELD, LATE_ROUNDS)
    late = combine(bits, own, [other], (0, 1), spares, LATE_HELD, places, samples)
    arrived += [send(value, blocks) for value, blocks in zip(late, LATE_ROUNDS)]
    summed = summed + sum(block.astype(jnp.float32) for block in reversed(arrived))
    return add_shift(summed, 1, shift, local_rows)


def solution(mesh):
    shape = mesh.shape
    small = shape["row"] == 4 and shape["col"] == 2 and shape["half"] == 2
    return jax.shard_map(
        two_centres if small else gathered,
        mesh=mesh,
        in_specs=(P(("groups", "row"), ("col", "half")), P("groups")),
        out_specs=P(("groups", "row"), ("col", "half")),
        check_vma=False,
    )
```

```python
import functools

import jax
import jax.numpy as jnp
from jax import lax
from jax.experimental import pallas as pl
from jax.experimental.pallas import tpu as pltpu
from jax.sharding import PartitionSpec as P


def pair_product(left, right):
    return jnp.einsum("ip,jp->ij", left, right, preferred_element_type=jnp.float32)


def add_shift(summed, samples, shift, local_rows):
    width = summed.shape[1]
    first_row = lax.axis_index("row") * local_rows
    block = lax.axis_index("col") * lax.axis_size("half") + lax.axis_index("half")
    row_ids = first_row + lax.broadcasted_iota(jnp.int32, (local_rows, width), 0)
    column_ids = block * width + lax.broadcasted_iota(jnp.int32, (local_rows, width), 1)
    return summed / samples + jnp.where(row_ids == column_ids, shift[0], 0.0)


def gathered(log_derivs, shift):
    local_rows = log_derivs.shape[0]
    samples = local_rows * lax.axis_size("row")
    rows = lax.all_gather(log_derivs, "row", axis=0, tiled=True).astype(jnp.float32)
    mean = jnp.sum(rows, axis=0) / samples
    centered = (rows - mean[None, :]).astype(jnp.bfloat16)
    own = (log_derivs.astype(jnp.float32) - mean[None, :]).astype(jnp.bfloat16)
    tile = pair_product(own, centered)
    summed = lax.psum_scatter(tile, ("col", "half"), scatter_dimension=1, tiled=True)
    return add_shift(summed, samples, shift, local_rows)


NEAR_ROUNDS = (
    (((1, 0), (1, 1)), ((0, 2), (1, 2))),
    (((1, 1), (1, 0)), ((1, 2), (0, 2))),
)
FAR_ROUNDS = (
    (((0, 0), (0, 1)), ((2, 2), (2, 0))),
    (((0, 1), (0, 0)), ((2, 0), (2, 2))),
)
LATE_ROUNDS = (
    (((1, 3), (0, 3)), ((2, 1), (2, 3))),
    (((0, 3), (1, 3)), ((2, 3), (2, 1))),
    (((3, 1), (3, 0)), ((3, 3), (3, 2))),
    (((3, 0), (3, 1)), ((3, 2), (3, 3))),
)
EARLY_SUMS = (((0, 0), (0, 1), (1, 1)), ((2, 2), (2, 0), (2, 1)))
EARLY_HELD = (
    ((0, 0), (0, 1), (1, 1), (1, 0), (1, 1)),
    ((2, 2), (2, 0), (2, 1), (0, 2), (1, 2)),
)
SPARE = 2
LATE_SUMS = (((3, 0), (3, 1)), ((3, 2), (3, 3)))
LATE_HELD = (
    ((3, 0), (3, 1), (0, 3), (1, 3), (1, 1)),
    ((3, 2), (3, 3), (2, 3), (3, 3), (2, 1)),
)
VMEM = pl.BlockSpec(memory_space=pltpu.VMEM)
SMEM = pl.BlockSpec(memory_space=pltpu.SMEM)
ANY = pl.BlockSpec(memory_space=pl.ANY)
LIMIT = pltpu.CompilerParams(vmem_limit_bytes=40 * 2**20)
BRIEF = pl.CostEstimate(flops=1024, bytes_accessed=1024, transcendentals=0)
LONG = pl.CostEstimate(flops=3 * 2**31, bytes_accessed=1024, transcendentals=0)


def device_index(row, col, half):
    return (row * 2 + col) * 2 + half


def round_pairs(blocks):
    pairs = []
    for side in (0, 1):
        for turn in (0, 1):
            for half in (0, 1):
                block = blocks[half][turn]
                if block is None:
                    continue
                i, j = (3 - b if side else b for b in block)
                source = device_index(1 + side, turn ^ side, half)
                pairs.append((source, device_index(i, j // 2, j % 2)))
    return pairs


def held_place(held, rounds):
    return [
        [[0 if b is None else held[half].index(b) for b in rounds_[half]] for half in (0, 1)]
        for rounds_ in rounds
    ]


def split_kernel(bits, values, near, far, far_sum, sems):
    part = far.shape[1]
    step = 512
    copies = []
    for i, (out, start) in enumerate(((far, bits[0]), (near, 1 - bits[0]))):
        columns = pl.ds(pl.multiple_of(start * part, 128), part)
        copies.append(pltpu.make_async_copy(values.at[:, columns], out, sems.at[i]))
    for copy in copies:
        copy.start()
    copies[0].wait()

    @pl.loop(0, part // step)
    def _(j):
        columns = pl.ds(pl.multiple_of(j * step, step), step)
        block = far[:, columns].astype(jnp.float32)
        far_sum[:, columns] = jnp.sum(block, axis=0, keepdims=True)

    copies[1].wait()


def block_product(left, right):
    return lax.dot_general(left, right, (((1,), (1,)), ((), ())), preferred_element_type=jnp.float32)


def sum_kernel(other, near, far_sum, partial):
    step = 512

    @pl.loop(0, near.shape[1] // step)
    def _(n):
        columns = pl.ds(pl.multiple_of(n * step, step), step)
        rows = other[:, columns].astype(jnp.float32) + near[:, columns].astype(jnp.float32)
        partial[:, columns] = far_sum[:, columns] + jnp.sum(rows, axis=0, keepdims=True)


def early_kernel(bits, other, edge, near, partial, centred, mean, own, *rest):
    sends, both = rest[:-1], rest[-1]
    rows, part = near.shape
    step = 512

    @pl.loop(0, part // step)
    def _(n):
        columns = pl.ds(pl.multiple_of(n * step, step), step)
        values = [block[:, columns].astype(jnp.float32) for block in (edge, near, other)]
        total = partial[:, columns] + jnp.sum(values[0], axis=0, keepdims=True)
        average = total * (1.0 / (4 * rows))
        mean[:, columns] = average
        for i in range(3):
            centred[i, :, columns] = (values[i] - average).astype(jnp.bfloat16)

    for core in (0, 1):
        for place, (i, j) in enumerate(EARLY_SUMS[core]):
            both[core, place] = block_product(centred[i], centred[j])
    own[...] = both[bits[1]]
    for place, send in enumerate(sends):
        send[...] = both[1 - bits[1], pl.ds(place, 1), :, :]


def late_products(core, last, centred, out):
    for place, (_, j) in enumerate(LATE_SUMS[core]):
        out[place] = block_product(last[...], last[...] if j == 3 else centred[j])


def late_kernel(bits, far_edge, mean, centred, *rest):
    own, send = rest[(len(rest) - 3) // 2 :][:2]
    last = rest[-1]
    last[...] = (far_edge[...].astype(jnp.float32) - mean[...]).astype(jnp.bfloat16)
    for core in (0, 1):

        @pl.when(bits[1] == core)
        def _():
            late_products(core, last, centred, own)
            late_products(1 - core, last, centred, send)


def combine_kernel(flips, scale, pieces, spares, bits, places, own, *rest):
    others, spare = rest[:pieces], rest[pieces : pieces + spares]
    outs, held = rest[pieces + spares : -1], rest[-1]
    count = own.shape[0]
    for i in range(count):
        other = others[0][i] if pieces == 1 else others[i][0]
        held[i] = (own[i] + other) * scale
    for n, i in enumerate(flips):
        held[count + n] = held[i].T
    for i in range(spares):
        held[count + len(flips) + i] = spare[i][...]
    for r, out in enumerate(outs):
        out[...] = held[places[r, bits[1], bits[2]]]


def shape_of(shape, dtype):
    return jax.ShapeDtypeStruct(shape, dtype)


def combine(bits, own, others, flips, spares, held, places, samples):
    rows = own.shape[1]
    return pl.pallas_call(
        functools.partial(combine_kernel, flips, 1.0 / samples, len(others), len(spares)),
        out_shape=[shape_of((rows, rows), jnp.float32)] * len(places),
        in_specs=[SMEM, SMEM] + [VMEM] * (1 + len(others) + len(spares)),
        out_specs=[VMEM] * len(places),
        scratch_shapes=[pltpu.VMEM((len(held[0]), rows, rows), jnp.float32)],
        compiler_params=LIMIT,
        cost_estimate=BRIEF,
    )(bits, jnp.array(places, jnp.int32), own, *others, *spares)


def two_centres(log_derivs, shift):
    local_rows, local_params = log_derivs.shape
    samples = local_rows * 4
    part = local_params // 2
    everyone = ("row", "col", "half")
    row, col, half = (lax.axis_index(name) for name in everyone)
    side = (row >= 2).astype(jnp.int32)
    bits = jnp.stack([side, half, jnp.bitwise_xor(col, side)]).astype(jnp.int32)

    to_centre = [(1, 2), (2, 1)]
    to_own = [(0, 1), (3, 2)]
    to_far = [(0, 2), (3, 1)]
    centres = [(r * 2 + h, r * 2 + 1 - h) for r in (1, 2) for h in (0, 1)]

    def swap(value):
        return lax.ppermute(value, ("row", "half"), centres)

    def send(value, blocks):
        return lax.ppermute(value.astype(jnp.float16), everyone, round_pairs(blocks))

    near, far, far_sum = pl.pallas_call(
        split_kernel,
        out_shape=[
            shape_of((local_rows, part), jnp.bfloat16),
            shape_of((local_rows, part), jnp.bfloat16),
            shape_of((1, part), jnp.float32),
        ],
        in_specs=[SMEM, ANY],
        out_specs=[VMEM] * 3,
        scratch_shapes=[pltpu.SemaphoreType.DMA((2,))],
        compiler_params=LIMIT,
        cost_estimate=BRIEF,
    )(bits, log_derivs)
    from_centre = lax.ppermute(far, "row", to_centre)
    from_sum = lax.ppermute(far_sum, "row", to_far)
    from_edge = lax.ppermute(near, "row", to_own)
    from_far_edge = lax.ppermute(far, "row", to_far)

    partial = pl.pallas_call(
        sum_kernel,
        out_shape=shape_of((1, part), jnp.float32),
        in_specs=[VMEM] * 3,
        out_specs=VMEM,
        compiler_params=LIMIT,
        cost_estimate=LONG,
    )(from_centre, near, from_sum)
    early_blocks = (3, local_rows, local_rows)
    centred, mean, own, *others = pl.pallas_call(
        early_kernel,
        out_shape=[
            shape_of((3, local_rows, part), jnp.bfloat16),
            shape_of((1, part), jnp.float32),
            shape_of(early_blocks, jnp.float32),
        ]
        + [shape_of((1, local_rows, local_rows), jnp.float32)] * 3,
        in_specs=[SMEM] + [VMEM] * 4,
        out_specs=[VMEM] * 6,
        scratch_shapes=[pltpu.VMEM((2,) + early_blocks, jnp.float32)],
        compiler_params=LIMIT,
        cost_estimate=BRIEF,
    )(bits, from_centre, from_edge, near, partial)
    others = [swap(other) for other in others]
    places = held_place(EARLY_HELD, NEAR_ROUNDS + FAR_ROUNDS) + [[[SPARE] * 2] * 2]
    *early, spare = combine(bits, own, others, (1, 2), (), EARLY_HELD, places, samples)
    near_blocks, far_blocks = early[: len(NEAR_ROUNDS)], early[len(NEAR_ROUNDS) :]
    arrived = [send(value, blocks) for value, blocks in zip(near_blocks, NEAR_ROUNDS)]
    summed = sum(block.astype(jnp.float32) for block in arrived)

    late_blocks = shape_of((2, local_rows, local_rows), jnp.float32)
    handed = [summed] + far_blocks
    own, other, summed, *far_blocks = pl.pallas_call(
        late_kernel,
        out_shape=[late_blocks, late_blocks]
        + [shape_of(value.shape, value.dtype) for value in handed],
        in_specs=[SMEM] + [VMEM] * 3 + [ANY] * len(handed),
        out_specs=[VMEM] * 2 + [ANY] * len(handed),
        scratch_shapes=[pltpu.VMEM((local_rows, part), jnp.bfloat16)],
        input_output_aliases={4 + i: 2 + i for i in range(len(handed))},
        compiler_params=LIMIT,
        cost_estimate=BRIEF,
    )(bits, from_far_edge, mean, centred, *handed)
    other = swap(other)
    arrived = [send(value, blocks) for value, blocks in zip(far_blocks, FAR_ROUNDS)]
    places = held_place(LATE_HELD, LATE_ROUNDS)
    late = combine(bits, own, [other], (0, 1), (spare,), LATE_HELD, places, samples)
    arrived += [send(value, blocks) for value, blocks in zip(late, LATE_ROUNDS)]
    summed = summed + sum(block.astype(jnp.float32) for block in reversed(arrived))
    return add_shift(summed, 1, shift, local_rows)


def solution(mesh):
    shape = mesh.shape
    small = shape["row"] == 4 and shape["col"] == 2 and shape["half"] == 2
    return jax.shard_map(
        two_centres if small else gathered,
        mesh=mesh,
        in_specs=(P(("groups", "row"), ("col", "half")), P("groups")),
        out_specs=P(("groups", "row"), ("col", "half")),
        check_vma=False,
    )
```

```python
import functools

import jax
import jax.numpy as jnp
from jax import lax
from jax.experimental import pallas as pl
from jax.experimental.pallas import tpu as pltpu
from jax.sharding import PartitionSpec as P


def pair_product(left, right):
    return jnp.einsum("ip,jp->ij", left, right, preferred_element_type=jnp.float32)


def add_shift(summed, samples, shift, local_rows):
    width = summed.shape[1]
    first_row = lax.axis_index("row") * local_rows
    block = lax.axis_index("col") * lax.axis_size("half") + lax.axis_index("half")
    row_ids = first_row + lax.broadcasted_iota(jnp.int32, (local_rows, width), 0)
    column_ids = block * width + lax.broadcasted_iota(jnp.int32, (local_rows, width), 1)
    return summed / samples + jnp.where(row_ids == column_ids, shift[0], 0.0)


def gathered(log_derivs, shift):
    local_rows = log_derivs.shape[0]
    samples = local_rows * lax.axis_size("row")
    rows = lax.all_gather(log_derivs, "row", axis=0, tiled=True).astype(jnp.float32)
    mean = jnp.sum(rows, axis=0) / samples
    centered = (rows - mean[None, :]).astype(jnp.bfloat16)
    own = (log_derivs.astype(jnp.float32) - mean[None, :]).astype(jnp.bfloat16)
    tile = pair_product(own, centered)
    summed = lax.psum_scatter(tile, ("col", "half"), scatter_dimension=1, tiled=True)
    return add_shift(summed, samples, shift, local_rows)


NEAR_ROUNDS = (
    (((1, 0), (1, 1)), ((0, 2), (1, 2))),
    (((1, 1), (1, 0)), ((1, 2), (0, 2))),
)
FAR_ROUNDS = (
    (((0, 0), (0, 1)), ((2, 2), (2, 0))),
    (((0, 1), (0, 0)), ((2, 0), (2, 2))),
)
LATE_ROUNDS = (
    (((3, 0), (3, 1)), ((3, 2), (3, 3))),
    (((3, 1), (3, 0)), ((3, 3), (3, 2))),
    (((0, 3), (1, 3)), ((2, 3), (2, 1))),
    (((1, 3), (0, 3)), ((2, 1), (2, 3))),
)
EARLY_SUMS = (((0, 0), (0, 1), (1, 1)), ((2, 2), (2, 0), (2, 1)))
EARLY_HELD = (
    ((0, 0), (0, 1), (1, 1), (1, 0), (1, 1)),
    ((2, 2), (2, 0), (2, 1), (0, 2), (1, 2)),
)
SPARE = 2
LATE_SUMS = (((3, 0), (3, 1)), ((3, 2), (3, 3)))
LATE_HELD = (
    ((3, 0), (3, 1), (0, 3), (1, 3), (1, 1)),
    ((3, 2), (3, 3), (2, 3), (3, 3), (2, 1)),
)
VMEM = pl.BlockSpec(memory_space=pltpu.VMEM)
SMEM = pl.BlockSpec(memory_space=pltpu.SMEM)
ANY = pl.BlockSpec(memory_space=pl.ANY)
LIMIT = pltpu.CompilerParams(vmem_limit_bytes=40 * 2**20)
BRIEF = pl.CostEstimate(flops=1024, bytes_accessed=1024, transcendentals=0)
LONG = pl.CostEstimate(flops=3 * 2**31, bytes_accessed=1024, transcendentals=0)


def device_index(row, col, half):
    return (row * 2 + col) * 2 + half


def round_pairs(blocks):
    pairs = []
    for side in (0, 1):
        for turn in (0, 1):
            for half in (0, 1):
                block = blocks[half][turn]
                if block is None:
                    continue
                i, j = (3 - b if side else b for b in block)
                source = device_index(1 + side, turn ^ side, half)
                pairs.append((source, device_index(i, j // 2, j % 2)))
    return pairs


def held_place(held, rounds):
    return [
        [[0 if b is None else held[half].index(b) for b in rounds_[half]] for half in (0, 1)]
        for rounds_ in rounds
    ]


def split_kernel(bits, values, near, far, far_sum, sems):
    part = far.shape[1]
    step = 512
    copies = []
    for i, (out, start) in enumerate(((far, bits[0]), (near, 1 - bits[0]))):
        columns = pl.ds(pl.multiple_of(start * part, 128), part)
        copies.append(pltpu.make_async_copy(values.at[:, columns], out, sems.at[i]))
    for copy in copies:
        copy.start()
    copies[0].wait()

    @pl.loop(0, part // step)
    def _(j):
        columns = pl.ds(pl.multiple_of(j * step, step), step)
        block = far[:, columns].astype(jnp.float32)
        far_sum[:, columns] = jnp.sum(block, axis=0, keepdims=True)

    copies[1].wait()


def block_product(left, right):
    return lax.dot_general(left, right, (((1,), (1,)), ((), ())), preferred_element_type=jnp.float32)


def sum_kernel(other, near, far_sum, partial):
    step = 512

    @pl.loop(0, near.shape[1] // step)
    def _(n):
        columns = pl.ds(pl.multiple_of(n * step, step), step)
        rows = other[:, columns].astype(jnp.float32) + near[:, columns].astype(jnp.float32)
        partial[:, columns] = far_sum[:, columns] + jnp.sum(rows, axis=0, keepdims=True)


def early_kernel(bits, other, edge, near, partial, centred, mean, own, send, both):
    rows, part = near.shape
    step = 512

    @pl.loop(0, part // step)
    def _(n):
        columns = pl.ds(pl.multiple_of(n * step, step), step)
        values = [block[:, columns].astype(jnp.float32) for block in (edge, near, other)]
        total = partial[:, columns] + jnp.sum(values[0], axis=0, keepdims=True)
        average = total * (1.0 / (4 * rows))
        mean[:, columns] = average
        for i in range(3):
            centred[i, :, columns] = (values[i] - average).astype(jnp.bfloat16)

    for core in (0, 1):
        for place, (i, j) in enumerate(EARLY_SUMS[core]):
            both[core, place] = block_product(centred[i], centred[j]) * (1.0 / (4 * rows))
    own[...] = both[bits[1]]
    send[...] = both[1 - bits[1]]


def late_products(core, last, centred, out):
    for place, (_, j) in enumerate(LATE_SUMS[core]):
        product = block_product(last[...], last[...] if j == 3 else centred[j])
        out[place] = product * (1.0 / (4 * last.shape[0]))


def late_kernel(bits, far_edge, mean, centred, *rest):
    own, send = rest[(len(rest) - 3) // 2 :][:2]
    last = rest[-1]
    last[...] = (far_edge[...].astype(jnp.float32) - mean[...]).astype(jnp.bfloat16)
    for core in (0, 1):

        @pl.when(bits[1] == core)
        def _():
            late_products(core, last, centred, own)
            late_products(1 - core, last, centred, send)


def combine_kernel(flips, pieces, spares, bits, places, own, *rest):
    others, spare = rest[:pieces], rest[pieces : pieces + spares]
    outs, held = rest[pieces + spares : -1], rest[-1]
    count = own.shape[0]
    for i in range(count):
        other = others[0][i] if pieces == 1 else others[i][0]
        held[i] = own[i] + other
    for n, i in enumerate(flips):
        held[count + n] = held[i].T
    for i in range(spares):
        held[count + len(flips) + i] = spare[i][...]
    for r, out in enumerate(outs):
        out[...] = held[places[r, bits[1], bits[2]]]


def shape_of(shape, dtype):
    return jax.ShapeDtypeStruct(shape, dtype)


def combine(bits, own, others, flips, spares, held, places):
    rows = own.shape[1]
    return pl.pallas_call(
        functools.partial(combine_kernel, flips, len(others), len(spares)),
        out_shape=[shape_of((rows, rows), jnp.float32)] * len(places),
        in_specs=[SMEM, SMEM] + [VMEM] * (1 + len(others) + len(spares)),
        out_specs=[VMEM] * len(places),
        scratch_shapes=[pltpu.VMEM((len(held[0]), rows, rows), jnp.float32)],
        compiler_params=LIMIT,
        cost_estimate=BRIEF,
    )(bits, jnp.array(places, jnp.int32), own, *others, *spares)


def two_centres(log_derivs, shift):
    local_rows, local_params = log_derivs.shape
    part = local_params // 2
    everyone = ("row", "col", "half")
    row, col, half = (lax.axis_index(name) for name in everyone)
    side = (row >= 2).astype(jnp.int32)
    bits = jnp.stack([side, half, jnp.bitwise_xor(col, side)]).astype(jnp.int32)

    to_centre = [(1, 2), (2, 1)]
    to_own = [(0, 1), (3, 2)]
    to_far = [(0, 2), (3, 1)]
    centres = [(r * 2 + h, r * 2 + 1 - h) for r in (1, 2) for h in (0, 1)]

    def swap(value):
        narrow = lax.ppermute(value.astype(jnp.float16), ("row", "half"), centres)
        return narrow.astype(jnp.float32)

    def send(value, blocks):
        return lax.ppermute(value.astype(jnp.float16), everyone, round_pairs(blocks))

    near, far, far_sum = pl.pallas_call(
        split_kernel,
        out_shape=[
            shape_of((local_rows, part), jnp.bfloat16),
            shape_of((local_rows, part), jnp.bfloat16),
            shape_of((1, part), jnp.float32),
        ],
        in_specs=[SMEM, ANY],
        out_specs=[VMEM] * 3,
        scratch_shapes=[pltpu.SemaphoreType.DMA((2,))],
        compiler_params=LIMIT,
        cost_estimate=BRIEF,
    )(bits, log_derivs)
    from_centre = lax.ppermute(far, "row", to_centre)
    from_sum = lax.ppermute(far_sum, "row", to_far)
    from_edge = lax.ppermute(near, "row", to_own)
    from_far_edge = lax.ppermute(far, "row", to_far)

    partial = pl.pallas_call(
        sum_kernel,
        out_shape=shape_of((1, part), jnp.float32),
        in_specs=[VMEM] * 3,
        out_specs=VMEM,
        compiler_params=LIMIT,
        cost_estimate=LONG,
    )(from_centre, near, from_sum)
    early_blocks = (3, local_rows, local_rows)
    centred, mean, own, other = pl.pallas_call(
        early_kernel,
        out_shape=[
            shape_of((3, local_rows, part), jnp.bfloat16),
            shape_of((1, part), jnp.float32),
            shape_of(early_blocks, jnp.float32),
            shape_of(early_blocks, jnp.float32),
        ],
        in_specs=[SMEM] + [VMEM] * 4,
        out_specs=[VMEM] * 4,
        scratch_shapes=[pltpu.VMEM((2,) + early_blocks, jnp.float32)],
        compiler_params=LIMIT,
        cost_estimate=BRIEF,
    )(bits, from_centre, from_edge, near, partial)
    others = [swap(other)]
    places = held_place(EARLY_HELD, NEAR_ROUNDS + FAR_ROUNDS) + [[[SPARE] * 2] * 2]
    *early, spare = combine(bits, own, others, (1, 2), (), EARLY_HELD, places)
    near_blocks, far_blocks = early[: len(NEAR_ROUNDS)], early[len(NEAR_ROUNDS) :]
    arrived = [send(value, blocks) for value, blocks in zip(near_blocks, NEAR_ROUNDS)]
    summed = sum(block.astype(jnp.float32) for block in arrived)

    late_blocks = shape_of((2, local_rows, local_rows), jnp.float32)
    handed = [summed] + far_blocks
    own, other, summed, *far_blocks = pl.pallas_call(
        late_kernel,
        out_shape=[late_blocks, late_blocks]
        + [shape_of(value.shape, value.dtype) for value in handed],
        in_specs=[SMEM] + [VMEM] * 3 + [ANY] * len(handed),
        out_specs=[VMEM] * 2 + [ANY] * len(handed),
        scratch_shapes=[pltpu.VMEM((local_rows, part), jnp.bfloat16)],
        input_output_aliases={4 + i: 2 + i for i in range(len(handed))},
        compiler_params=LIMIT,
        cost_estimate=BRIEF,
    )(bits, from_far_edge, mean, centred, *handed)
    other = swap(other)
    arrived = [send(value, blocks) for value, blocks in zip(far_blocks, FAR_ROUNDS)]
    places = held_place(LATE_HELD, LATE_ROUNDS)
    late = combine(bits, own, [other], (0, 1), (spare,), LATE_HELD, places)
    arrived += [send(value, blocks) for value, blocks in zip(late, LATE_ROUNDS)]
    summed = summed + sum(block.astype(jnp.float32) for block in reversed(arrived))
    return add_shift(summed, 1, shift, local_rows)


def solution(mesh):
    shape = mesh.shape
    small = shape["row"] == 4 and shape["col"] == 2 and shape["half"] == 2
    return jax.shard_map(
        two_centres if small else gathered,
        mesh=mesh,
        in_specs=(P(("groups", "row"), ("col", "half")), P("groups")),
        out_specs=P(("groups", "row"), ("col", "half")),
        check_vma=False,
    )
```

```python
import functools

import jax
import jax.numpy as jnp
from jax import lax
from jax.experimental import pallas as pl
from jax.experimental.pallas import tpu as pltpu
from jax.sharding import PartitionSpec as P


def pair_product(left, right):
    return jnp.einsum("ip,jp->ij", left, right, preferred_element_type=jnp.float32)


def add_shift(summed, samples, shift, local_rows):
    width = summed.shape[1]
    first_row = lax.axis_index("row") * local_rows
    block = lax.axis_index("col") * lax.axis_size("half") + lax.axis_index("half")
    row_ids = first_row + lax.broadcasted_iota(jnp.int32, (local_rows, width), 0)
    column_ids = block * width + lax.broadcasted_iota(jnp.int32, (local_rows, width), 1)
    return summed / samples + jnp.where(row_ids == column_ids, shift[0], 0.0)


def gathered(log_derivs, shift):
    local_rows = log_derivs.shape[0]
    samples = local_rows * lax.axis_size("row")
    rows = lax.all_gather(log_derivs, "row", axis=0, tiled=True).astype(jnp.float32)
    mean = jnp.sum(rows, axis=0) / samples
    centered = (rows - mean[None, :]).astype(jnp.bfloat16)
    own = (log_derivs.astype(jnp.float32) - mean[None, :]).astype(jnp.bfloat16)
    tile = pair_product(own, centered)
    summed = lax.psum_scatter(tile, ("col", "half"), scatter_dimension=1, tiled=True)
    return add_shift(summed, samples, shift, local_rows)


NEAR_ROUNDS = (
    (((1, 0), (1, 1)), ((0, 2), (1, 2))),
    (((1, 1), (1, 0)), ((1, 2), (0, 2))),
    (((0, 0), (0, 1)), (None, None)),
)
FAR_ROUNDS = (
    ((None, None), ((2, 2), (2, 0))),
    (((0, 1), (0, 0)), ((2, 0), (2, 2))),
)
LATE_ROUNDS = (
    (((3, 0), (3, 1)), ((3, 2), (3, 3))),
    (((3, 1), (3, 0)), ((3, 3), (3, 2))),
    (((0, 3), (1, 3)), ((2, 3), (2, 1))),
    (((1, 3), (0, 3)), ((2, 1), (2, 3))),
)
EARLY_SUMS = (((0, 0), (0, 1), (1, 1)), ((2, 2), (2, 0), (2, 1)))
EARLY_HELD = (
    ((0, 0), (0, 1), (1, 1), (1, 0), (1, 1)),
    ((2, 2), (2, 0), (2, 1), (0, 2), (1, 2)),
)
SPARE = 2
LATE_SUMS = (((3, 0), (3, 1)), ((3, 2), (3, 3)))
LATE_HELD = (
    ((3, 0), (3, 1), (0, 3), (1, 3), (1, 1)),
    ((3, 2), (3, 3), (2, 3), (3, 3), (2, 1)),
)
VMEM = pl.BlockSpec(memory_space=pltpu.VMEM)
SMEM = pl.BlockSpec(memory_space=pltpu.SMEM)
ANY = pl.BlockSpec(memory_space=pl.ANY)
LIMIT = pltpu.CompilerParams(vmem_limit_bytes=40 * 2**20)
BRIEF = pl.CostEstimate(flops=1024, bytes_accessed=1024, transcendentals=0)
LONG = pl.CostEstimate(flops=3 * 2**31, bytes_accessed=1024, transcendentals=0)


def device_index(row, col, half):
    return (row * 2 + col) * 2 + half


def round_pairs(blocks):
    pairs = []
    for side in (0, 1):
        for turn in (0, 1):
            for half in (0, 1):
                block = blocks[half][turn]
                if block is None:
                    continue
                i, j = (3 - b if side else b for b in block)
                source = device_index(1 + side, turn ^ side, half)
                pairs.append((source, device_index(i, j // 2, j % 2)))
    return pairs


def held_place(held, rounds):
    return [
        [[0 if b is None else held[half].index(b) for b in rounds_[half]] for half in (0, 1)]
        for rounds_ in rounds
    ]


def split_kernel(bits, values, near, far, far_sum, sems):
    part = far.shape[1]
    step = 512
    copies = []
    for i, (out, start) in enumerate(((far, bits[0]), (near, 1 - bits[0]))):
        columns = pl.ds(pl.multiple_of(start * part, 128), part)
        copies.append(pltpu.make_async_copy(values.at[:, columns], out, sems.at[i]))
    for copy in copies:
        copy.start()
    copies[0].wait()

    @pl.loop(0, part // step)
    def _(j):
        columns = pl.ds(pl.multiple_of(j * step, step), step)
        block = far[:, columns].astype(jnp.float32)
        far_sum[:, columns] = jnp.sum(block, axis=0, keepdims=True)

    copies[1].wait()


def block_product(left, right):
    return lax.dot_general(left, right, (((1,), (1,)), ((), ())), preferred_element_type=jnp.float32)


def sum_kernel(other, near, far_sum, partial):
    step = 512

    @pl.loop(0, near.shape[1] // step)
    def _(n):
        columns = pl.ds(pl.multiple_of(n * step, step), step)
        rows = other[:, columns].astype(jnp.float32) + near[:, columns].astype(jnp.float32)
        partial[:, columns] = far_sum[:, columns] + jnp.sum(rows, axis=0, keepdims=True)


def early_kernel(bits, other, edge, near, partial, centred, mean, own, send, both):
    rows, part = near.shape
    step = 512

    @pl.loop(0, part // step)
    def _(n):
        columns = pl.ds(pl.multiple_of(n * step, step), step)
        values = [block[:, columns].astype(jnp.float32) for block in (edge, near, other)]
        total = partial[:, columns] + jnp.sum(values[0], axis=0, keepdims=True)
        average = total * (1.0 / (4 * rows))
        mean[:, columns] = average
        for i in range(3):
            centred[i, :, columns] = (values[i] - average).astype(jnp.bfloat16)

    for core in (0, 1):
        for place, (i, j) in enumerate(EARLY_SUMS[core]):
            both[core, place] = block_product(centred[i], centred[j]) * (1.0 / (4 * rows))
    own[...] = both[bits[1]]
    send[...] = both[1 - bits[1]]


def late_products(core, last, centred, out):
    for place, (_, j) in enumerate(LATE_SUMS[core]):
        product = block_product(last[...], last[...] if j == 3 else centred[j])
        out[place] = product * (1.0 / (4 * last.shape[0]))


def late_kernel(bits, far_edge, mean, centred, *rest):
    own, send = rest[(len(rest) - 3) // 2 :][:2]
    last = rest[-1]
    last[...] = (far_edge[...].astype(jnp.float32) - mean[...]).astype(jnp.bfloat16)
    for core in (0, 1):

        @pl.when(bits[1] == core)
        def _():
            late_products(core, last, centred, own)
            late_products(1 - core, last, centred, send)


def combine_kernel(flips, pieces, spares, bits, places, own, *rest):
    others, spare = rest[:pieces], rest[pieces : pieces + spares]
    outs, held = rest[pieces + spares : -1], rest[-1]
    count = own.shape[0]
    for i in range(count):
        other = others[0][i] if pieces == 1 else others[i][0]
        held[i] = own[i] + other
    for n, i in enumerate(flips):
        held[count + n] = held[i].T
    for i in range(spares):
        held[count + len(flips) + i] = spare[i][...]
    for r, out in enumerate(outs):
        out[...] = held[places[r, bits[1], bits[2]]]


def shape_of(shape, dtype):
    return jax.ShapeDtypeStruct(shape, dtype)


def combine(bits, own, others, flips, spares, held, places):
    rows = own.shape[1]
    return pl.pallas_call(
        functools.partial(combine_kernel, flips, len(others), len(spares)),
        out_shape=[shape_of((rows, rows), jnp.float32)] * len(places),
        in_specs=[SMEM, SMEM] + [VMEM] * (1 + len(others) + len(spares)),
        out_specs=[VMEM] * len(places),
        scratch_shapes=[pltpu.VMEM((len(held[0]), rows, rows), jnp.float32)],
        compiler_params=LIMIT,
        cost_estimate=BRIEF,
    )(bits, jnp.array(places, jnp.int32), own, *others, *spares)


def two_centres(log_derivs, shift):
    local_rows, local_params = log_derivs.shape
    part = local_params // 2
    everyone = ("row", "col", "half")
    row, col, half = (lax.axis_index(name) for name in everyone)
    side = (row >= 2).astype(jnp.int32)
    bits = jnp.stack([side, half, jnp.bitwise_xor(col, side)]).astype(jnp.int32)

    to_centre = [(1, 2), (2, 1)]
    to_own = [(0, 1), (3, 2)]
    to_far = [(0, 2), (3, 1)]
    centres = [(r * 2 + h, r * 2 + 1 - h) for r in (1, 2) for h in (0, 1)]

    def swap(value):
        narrow = lax.ppermute(value.astype(jnp.float16), ("row", "half"), centres)
        return narrow.astype(jnp.float32)

    def send(value, blocks):
        return lax.ppermute(value.astype(jnp.float16), everyone, round_pairs(blocks))

    near, far, far_sum = pl.pallas_call(
        split_kernel,
        out_shape=[
            shape_of((local_rows, part), jnp.bfloat16),
            shape_of((local_rows, part), jnp.bfloat16),
            shape_of((1, part), jnp.float32),
        ],
        in_specs=[SMEM, ANY],
        out_specs=[VMEM] * 3,
        scratch_shapes=[pltpu.SemaphoreType.DMA((2,))],
        compiler_params=LIMIT,
        cost_estimate=BRIEF,
    )(bits, log_derivs)
    from_centre = lax.ppermute(far, "row", to_centre)
    from_sum = lax.ppermute(far_sum, "row", to_far)
    from_edge = lax.ppermute(near, "row", to_own)
    from_far_edge = lax.ppermute(far, "row", to_far)

    partial = pl.pallas_call(
        sum_kernel,
        out_shape=shape_of((1, part), jnp.float32),
        in_specs=[VMEM] * 3,
        out_specs=VMEM,
        compiler_params=LIMIT,
        cost_estimate=LONG,
    )(from_centre, near, from_sum)
    early_blocks = (3, local_rows, local_rows)
    centred, mean, own, other = pl.pallas_call(
        early_kernel,
        out_shape=[
            shape_of((3, local_rows, part), jnp.bfloat16),
            shape_of((1, part), jnp.float32),
            shape_of(early_blocks, jnp.float32),
            shape_of(early_blocks, jnp.float32),
        ],
        in_specs=[SMEM] + [VMEM] * 4,
        out_specs=[VMEM] * 4,
        scratch_shapes=[pltpu.VMEM((2,) + early_blocks, jnp.float32)],
        compiler_params=LIMIT,
        cost_estimate=BRIEF,
    )(bits, from_centre, from_edge, near, partial)
    others = [swap(other)]
    places = held_place(EARLY_HELD, NEAR_ROUNDS + FAR_ROUNDS) + [[[SPARE] * 2] * 2]
    *early, spare = combine(bits, own, others, (1, 2), (), EARLY_HELD, places)
    near_blocks, far_blocks = early[: len(NEAR_ROUNDS)], early[len(NEAR_ROUNDS) :]
    arrived = [send(value, blocks) for value, blocks in zip(near_blocks, NEAR_ROUNDS)]
    summed = sum(block.astype(jnp.float32) for block in arrived)

    late_blocks = shape_of((2, local_rows, local_rows), jnp.float32)
    handed = [summed] + far_blocks
    own, other, summed, *far_blocks = pl.pallas_call(
        late_kernel,
        out_shape=[late_blocks, late_blocks]
        + [shape_of(value.shape, value.dtype) for value in handed],
        in_specs=[SMEM] + [VMEM] * 3 + [ANY] * len(handed),
        out_specs=[VMEM] * 2 + [ANY] * len(handed),
        scratch_shapes=[pltpu.VMEM((local_rows, part), jnp.bfloat16)],
        input_output_aliases={4 + i: 2 + i for i in range(len(handed))},
        compiler_params=LIMIT,
        cost_estimate=BRIEF,
    )(bits, from_far_edge, mean, centred, *handed)
    other = swap(other)
    arrived = [send(value, blocks) for value, blocks in zip(far_blocks, FAR_ROUNDS)]
    places = held_place(LATE_HELD, LATE_ROUNDS)
    late = combine(bits, own, [other], (0, 1), (spare,), LATE_HELD, places)
    arrived += [send(value, blocks) for value, blocks in zip(late, LATE_ROUNDS)]
    summed = summed + sum(block.astype(jnp.float32) for block in reversed(arrived))
    return add_shift(summed, 1, shift, local_rows)


def solution(mesh):
    shape = mesh.shape
    small = shape["row"] == 4 and shape["col"] == 2 and shape["half"] == 2
    return jax.shard_map(
        two_centres if small else gathered,
        mesh=mesh,
        in_specs=(P(("groups", "row"), ("col", "half")), P("groups")),
        out_specs=P(("groups", "row"), ("col", "half")),
        check_vma=False,
    )
```

```python
import functools

import jax
import jax.numpy as jnp
from jax import lax
from jax.experimental import pallas as pl
from jax.experimental.pallas import tpu as pltpu
from jax.sharding import PartitionSpec as P


def pair_product(left, right):
    return jnp.einsum("ip,jp->ij", left, right, preferred_element_type=jnp.float32)


def add_shift(summed, samples, shift, local_rows):
    width = summed.shape[1]
    first_row = lax.axis_index("row") * local_rows
    block = lax.axis_index("col") * lax.axis_size("half") + lax.axis_index("half")
    row_ids = first_row + lax.broadcasted_iota(jnp.int32, (local_rows, width), 0)
    column_ids = block * width + lax.broadcasted_iota(jnp.int32, (local_rows, width), 1)
    return summed / samples + jnp.where(row_ids == column_ids, shift[0], 0.0)


def gathered(log_derivs, shift):
    local_rows = log_derivs.shape[0]
    samples = local_rows * lax.axis_size("row")
    rows = lax.all_gather(log_derivs, "row", axis=0, tiled=True).astype(jnp.float32)
    mean = jnp.sum(rows, axis=0) / samples
    centered = (rows - mean[None, :]).astype(jnp.bfloat16)
    own = (log_derivs.astype(jnp.float32) - mean[None, :]).astype(jnp.bfloat16)
    tile = pair_product(own, centered)
    summed = lax.psum_scatter(tile, ("col", "half"), scatter_dimension=1, tiled=True)
    return add_shift(summed, samples, shift, local_rows)


NEAR_ROUNDS = (
    (((1, 0), (1, 1)), ((0, 2), (1, 2))),
    (((1, 1), (1, 0)), ((1, 2), (0, 2))),
    (((0, 0), (0, 1)), (None, None)),
)
FAR_ROUNDS = (
    ((None, None), ((2, 2), (2, 0))),
    (((0, 1), (0, 0)), ((2, 0), (2, 2))),
)
LATE_ROUNDS = (
    (((1, 3), (0, 3)), ((2, 1), (2, 3))),
    (((3, 0), (3, 1)), ((3, 2), (3, 3))),
    (((3, 1), (3, 0)), ((3, 3), (3, 2))),
    (((0, 3), (1, 3)), ((2, 3), (2, 1))),
)
EARLY_SUMS = (((0, 0), (0, 1), (1, 1)), ((2, 2), (2, 0), (2, 1)))
EARLY_HELD = (
    ((0, 0), (0, 1), (1, 1), (1, 0), (1, 1)),
    ((2, 2), (2, 0), (2, 1), (0, 2), (1, 2)),
)
SPARE = 2
LATE_SUMS = (((3, 0), (3, 1)), ((3, 2), (3, 3)))
LATE_HELD = (
    ((3, 0), (3, 1), (0, 3), (1, 3), (1, 1)),
    ((3, 2), (3, 3), (2, 3), (3, 3), (2, 1)),
)
VMEM = pl.BlockSpec(memory_space=pltpu.VMEM)
SMEM = pl.BlockSpec(memory_space=pltpu.SMEM)
ANY = pl.BlockSpec(memory_space=pl.ANY)
LIMIT = pltpu.CompilerParams(vmem_limit_bytes=40 * 2**20)
BRIEF = pl.CostEstimate(flops=1024, bytes_accessed=1024, transcendentals=0)
LONG = pl.CostEstimate(flops=3 * 2**31, bytes_accessed=1024, transcendentals=0)


def device_index(row, col, half):
    return (row * 2 + col) * 2 + half


def round_pairs(blocks):
    pairs = []
    for side in (0, 1):
        for turn in (0, 1):
            for half in (0, 1):
                block = blocks[half][turn]
                if block is None:
                    continue
                i, j = (3 - b if side else b for b in block)
                source = device_index(1 + side, turn ^ side, half)
                pairs.append((source, device_index(i, j // 2, j % 2)))
    return pairs


def held_place(held, rounds):
    return [
        [[0 if b is None else held[half].index(b) for b in rounds_[half]] for half in (0, 1)]
        for rounds_ in rounds
    ]


def split_kernel(bits, values, near, far, far_sum, sems):
    part = far.shape[1]
    step = 512
    copies = []
    for i, (out, start) in enumerate(((far, bits[0]), (near, 1 - bits[0]))):
        columns = pl.ds(pl.multiple_of(start * part, 128), part)
        copies.append(pltpu.make_async_copy(values.at[:, columns], out, sems.at[i]))
    for copy in copies:
        copy.start()
    copies[0].wait()

    @pl.loop(0, part // step)
    def _(j):
        columns = pl.ds(pl.multiple_of(j * step, step), step)
        block = far[:, columns].astype(jnp.float32)
        far_sum[:, columns] = jnp.sum(block, axis=0, keepdims=True)

    copies[1].wait()


def block_product(left, right):
    return lax.dot_general(left, right, (((1,), (1,)), ((), ())), preferred_element_type=jnp.float32)


def sum_kernel(other, near, far_sum, partial):
    step = 512

    @pl.loop(0, near.shape[1] // step)
    def _(n):
        columns = pl.ds(pl.multiple_of(n * step, step), step)
        rows = other[:, columns].astype(jnp.float32) + near[:, columns].astype(jnp.float32)
        partial[:, columns] = far_sum[:, columns] + jnp.sum(rows, axis=0, keepdims=True)


def early_kernel(bits, other, edge, near, partial, centred, mean, own, send, both):
    rows, part = near.shape
    step = 512

    @pl.loop(0, part // step)
    def _(n):
        columns = pl.ds(pl.multiple_of(n * step, step), step)
        values = [block[:, columns].astype(jnp.float32) for block in (edge, near, other)]
        total = partial[:, columns] + jnp.sum(values[0], axis=0, keepdims=True)
        average = total * (1.0 / (4 * rows))
        mean[:, columns] = average
        for i in range(3):
            centred[i, :, columns] = (values[i] - average).astype(jnp.bfloat16)

    for core in (0, 1):
        for place, (i, j) in enumerate(EARLY_SUMS[core]):
            both[core, place] = block_product(centred[i], centred[j]) * (1.0 / (4 * rows))
    own[...] = both[bits[1]]
    send[...] = both[1 - bits[1]]


def late_products(core, last, centred, out):
    for place, (_, j) in enumerate(LATE_SUMS[core]):
        product = block_product(last[...], last[...] if j == 3 else centred[j])
        out[place] = product * (1.0 / (4 * last.shape[0]))


def late_kernel(bits, far_edge, mean, centred, *rest):
    own, send = rest[(len(rest) - 3) // 2 :][:2]
    last = rest[-1]
    last[...] = (far_edge[...].astype(jnp.float32) - mean[...]).astype(jnp.bfloat16)
    for core in (0, 1):

        @pl.when(bits[1] == core)
        def _():
            late_products(core, last, centred, own)
            late_products(1 - core, last, centred, send)


def combine_kernel(flips, pieces, spares, bits, places, own, *rest):
    others, spare = rest[:pieces], rest[pieces : pieces + spares]
    outs, held = rest[pieces + spares : -1], rest[-1]
    count = own.shape[0]
    for i in range(count):
        other = others[0][i] if pieces == 1 else others[i][0]
        held[i] = own[i] + other
    for n, i in enumerate(flips):
        held[count + n] = held[i].T
    for i in range(spares):
        held[count + len(flips) + i] = spare[i][...]
    for r, out in enumerate(outs):
        out[...] = held[places[r, bits[1], bits[2]]]


def shape_of(shape, dtype):
    return jax.ShapeDtypeStruct(shape, dtype)


def combine(bits, own, others, flips, spares, held, places):
    rows = own.shape[1]
    return pl.pallas_call(
        functools.partial(combine_kernel, flips, len(others), len(spares)),
        out_shape=[shape_of((rows, rows), jnp.float32)] * len(places),
        in_specs=[SMEM, SMEM] + [VMEM] * (1 + len(others) + len(spares)),
        out_specs=[VMEM] * len(places),
        scratch_shapes=[pltpu.VMEM((len(held[0]), rows, rows), jnp.float32)],
        compiler_params=LIMIT,
        cost_estimate=BRIEF,
    )(bits, jnp.array(places, jnp.int32), own, *others, *spares)


def two_centres(log_derivs, shift):
    local_rows, local_params = log_derivs.shape
    part = local_params // 2
    everyone = ("row", "col", "half")
    row, col, half = (lax.axis_index(name) for name in everyone)
    side = (row >= 2).astype(jnp.int32)
    bits = jnp.stack([side, half, jnp.bitwise_xor(col, side)]).astype(jnp.int32)

    to_centre = [(1, 2), (2, 1)]
    to_own = [(0, 1), (3, 2)]
    to_far = [(0, 2), (3, 1)]
    centres = [(r * 2 + h, r * 2 + 1 - h) for r in (1, 2) for h in (0, 1)]

    def swap(value):
        narrow = lax.ppermute(value.astype(jnp.float16), ("row", "half"), centres)
        return narrow.astype(jnp.float32)

    def send(value, blocks):
        return lax.ppermute(value.astype(jnp.float16), everyone, round_pairs(blocks))

    near, far, far_sum = pl.pallas_call(
        split_kernel,
        out_shape=[
            shape_of((local_rows, part), jnp.bfloat16),
            shape_of((local_rows, part), jnp.bfloat16),
            shape_of((1, part), jnp.float32),
        ],
        in_specs=[SMEM, ANY],
        out_specs=[VMEM] * 3,
        scratch_shapes=[pltpu.SemaphoreType.DMA((2,))],
        compiler_params=LIMIT,
        cost_estimate=BRIEF,
    )(bits, log_derivs)
    from_centre = lax.ppermute(far, "row", to_centre)
    from_sum = lax.ppermute(far_sum, "row", to_far)
    from_edge = lax.ppermute(near, "row", to_own)
    from_far_edge = lax.ppermute(far, "row", to_far)

    partial = pl.pallas_call(
        sum_kernel,
        out_shape=shape_of((1, part), jnp.float32),
        in_specs=[VMEM] * 3,
        out_specs=VMEM,
        compiler_params=LIMIT,
        cost_estimate=LONG,
    )(from_centre, near, from_sum)
    early_blocks = (3, local_rows, local_rows)
    centred, mean, own, other = pl.pallas_call(
        early_kernel,
        out_shape=[
            shape_of((3, local_rows, part), jnp.bfloat16),
            shape_of((1, part), jnp.float32),
            shape_of(early_blocks, jnp.float32),
            shape_of(early_blocks, jnp.float32),
        ],
        in_specs=[SMEM] + [VMEM] * 4,
        out_specs=[VMEM] * 4,
        scratch_shapes=[pltpu.VMEM((2,) + early_blocks, jnp.float32)],
        compiler_params=LIMIT,
        cost_estimate=BRIEF,
    )(bits, from_centre, from_edge, near, partial)
    others = [swap(other)]
    places = held_place(EARLY_HELD, NEAR_ROUNDS + FAR_ROUNDS) + [[[SPARE] * 2] * 2]
    *early, spare = combine(bits, own, others, (1, 2), (), EARLY_HELD, places)
    near_blocks, far_blocks = early[: len(NEAR_ROUNDS)], early[len(NEAR_ROUNDS) :]
    arrived = [send(value, blocks) for value, blocks in zip(near_blocks, NEAR_ROUNDS)]
    summed = sum(block.astype(jnp.float32) for block in arrived)

    late_blocks = shape_of((2, local_rows, local_rows), jnp.float32)
    handed = [summed] + far_blocks
    own, other, summed, *far_blocks = pl.pallas_call(
        late_kernel,
        out_shape=[late_blocks, late_blocks]
        + [shape_of(value.shape, value.dtype) for value in handed],
        in_specs=[SMEM] + [VMEM] * 3 + [ANY] * len(handed),
        out_specs=[VMEM] * 2 + [ANY] * len(handed),
        scratch_shapes=[pltpu.VMEM((local_rows, part), jnp.bfloat16)],
        input_output_aliases={4 + i: 2 + i for i in range(len(handed))},
        compiler_params=LIMIT,
        cost_estimate=BRIEF,
    )(bits, from_far_edge, mean, centred, *handed)
    other = swap(other)
    arrived = [send(value, blocks) for value, blocks in zip(far_blocks, FAR_ROUNDS)]
    places = held_place(LATE_HELD, LATE_ROUNDS)
    late = combine(bits, own, [other], (0, 1), (spare,), LATE_HELD, places)
    arrived += [send(value, blocks) for value, blocks in zip(late, LATE_ROUNDS)]
    summed = summed + sum(block.astype(jnp.float32) for block in reversed(arrived))
    return add_shift(summed, 1, shift, local_rows)


def solution(mesh):
    shape = mesh.shape
    small = shape["row"] == 4 and shape["col"] == 2 and shape["half"] == 2
    return jax.shard_map(
        two_centres if small else gathered,
        mesh=mesh,
        in_specs=(P(("groups", "row"), ("col", "half")), P("groups")),
        out_specs=P(("groups", "row"), ("col", "half")),
        check_vma=False,
    )
```

```python
import functools

import jax
import jax.numpy as jnp
from jax import lax
from jax.experimental import pallas as pl
from jax.experimental.pallas import tpu as pltpu
from jax.sharding import PartitionSpec as P


def pair_product(left, right):
    return jnp.einsum("ip,jp->ij", left, right, preferred_element_type=jnp.float32)


def add_shift(summed, samples, shift, local_rows):
    width = summed.shape[1]
    first_row = lax.axis_index("row") * local_rows
    block = lax.axis_index("col") * lax.axis_size("half") + lax.axis_index("half")
    row_ids = first_row + lax.broadcasted_iota(jnp.int32, (local_rows, width), 0)
    column_ids = block * width + lax.broadcasted_iota(jnp.int32, (local_rows, width), 1)
    return summed / samples + jnp.where(row_ids == column_ids, shift[0], 0.0)


def gathered(log_derivs, shift):
    local_rows = log_derivs.shape[0]
    samples = local_rows * lax.axis_size("row")
    rows = lax.all_gather(log_derivs, "row", axis=0, tiled=True).astype(jnp.float32)
    mean = jnp.sum(rows, axis=0) / samples
    centered = (rows - mean[None, :]).astype(jnp.bfloat16)
    own = (log_derivs.astype(jnp.float32) - mean[None, :]).astype(jnp.bfloat16)
    tile = pair_product(own, centered)
    summed = lax.psum_scatter(tile, ("col", "half"), scatter_dimension=1, tiled=True)
    return add_shift(summed, samples, shift, local_rows)


NEAR_ROUNDS = (
    (((1, 0), (1, 1)), ((0, 2), (1, 2))),
    (((1, 1), (1, 0)), ((1, 2), (0, 2))),
)
FAR_ROUNDS = (
    (((0, 0), (0, 1)), ((2, 2), (2, 0))),
    (((0, 1), (0, 0)), ((2, 0), (2, 2))),
)
LATE_ROUNDS = (
    (((3, 0), (3, 1)), ((3, 2), (3, 3))),
    (((3, 1), (3, 0)), ((3, 3), (3, 2))),
    (((0, 3), (1, 3)), ((2, 3), (2, 1))),
    (((1, 3), (0, 3)), ((2, 1), (2, 3))),
)
EARLY_SUMS = (((0, 0), (0, 1), (1, 1)), ((2, 2), (2, 0), (2, 1)))
EARLY_HELD = (
    ((0, 0), (0, 1), (1, 1), (1, 0), (1, 1)),
    ((2, 2), (2, 0), (2, 1), (0, 2), (1, 2)),
)
SPARE = 2
LATE_SUMS = (((3, 0), (3, 1)), ((3, 2), (3, 3)))
LATE_HELD = (
    ((3, 0), (3, 1), (0, 3), (1, 3), (1, 1)),
    ((3, 2), (3, 3), (2, 3), (3, 3), (2, 1)),
)
VMEM = pl.BlockSpec(memory_space=pltpu.VMEM)
SMEM = pl.BlockSpec(memory_space=pltpu.SMEM)
ANY = pl.BlockSpec(memory_space=pl.ANY)
LIMIT = pltpu.CompilerParams(vmem_limit_bytes=40 * 2**20)
BRIEF = pl.CostEstimate(flops=1024, bytes_accessed=1024, transcendentals=0)
LONG = pl.CostEstimate(flops=3 * 2**31, bytes_accessed=1024, transcendentals=0)


def device_index(row, col, half):
    return (row * 2 + col) * 2 + half


def round_pairs(blocks):
    pairs = []
    for side in (0, 1):
        for turn in (0, 1):
            for half in (0, 1):
                block = blocks[half][turn]
                if block is None:
                    continue
                i, j = (3 - b if side else b for b in block)
                source = device_index(1 + side, turn ^ side, half)
                pairs.append((source, device_index(i, j // 2, j % 2)))
    return pairs


def held_place(held, rounds):
    return [
        [[0 if b is None else held[half].index(b) for b in rounds_[half]] for half in (0, 1)]
        for rounds_ in rounds
    ]


def split_kernel(bits, values, near, far, far_sum, sems):
    part = far.shape[1]
    step = 512
    copies = []
    for i, (out, start) in enumerate(((far, bits[0]), (near, 1 - bits[0]))):
        columns = pl.ds(pl.multiple_of(start * part, 128), part)
        copies.append(pltpu.make_async_copy(values.at[:, columns], out, sems.at[i]))
    for copy in copies:
        copy.start()
    copies[0].wait()

    @pl.loop(0, part // step)
    def _(j):
        columns = pl.ds(pl.multiple_of(j * step, step), step)
        block = far[:, columns].astype(jnp.float32)
        far_sum[:, columns] = jnp.sum(block, axis=0, keepdims=True)

    copies[1].wait()


def block_product(left, right):
    return lax.dot_general(left, right, (((1,), (1,)), ((), ())), preferred_element_type=jnp.float32)


def sum_kernel(other, near, far_sum, partial):
    step = 512

    @pl.loop(0, near.shape[1] // step)
    def _(n):
        columns = pl.ds(pl.multiple_of(n * step, step), step)
        rows = other[:, columns].astype(jnp.float32) + near[:, columns].astype(jnp.float32)
        partial[:, columns] = far_sum[:, columns] + jnp.sum(rows, axis=0, keepdims=True)


def early_kernel(bits, other, edge, near, partial, centred, mean, own, send, both):
    rows, part = near.shape
    step = 512

    @pl.loop(0, part // step)
    def _(n):
        columns = pl.ds(pl.multiple_of(n * step, step), step)
        values = [block[:, columns].astype(jnp.float32) for block in (edge, near, other)]
        total = partial[:, columns] + jnp.sum(values[0], axis=0, keepdims=True)
        average = total * (1.0 / (4 * rows))
        mean[:, columns] = average
        for i in range(3):
            centred[i, :, columns] = (values[i] - average).astype(jnp.bfloat16)

    for core in (0, 1):
        for place, (i, j) in enumerate(EARLY_SUMS[core]):
            both[core, place] = block_product(centred[i], centred[j]) * (1.0 / (4 * rows))
    own[...] = both[bits[1]]
    send[...] = both[1 - bits[1]]


def late_products(core, last, centred, out):
    for place, (_, j) in enumerate(LATE_SUMS[core]):
        product = block_product(last[...], last[...] if j == 3 else centred[j])
        out[place] = product * (1.0 / (4 * last.shape[0]))


def late_kernel(bits, far_edge, mean, centred, *rest):
    own, send = rest[(len(rest) - 3) // 2 :][:2]
    last = rest[-1]
    last[...] = (far_edge[...].astype(jnp.float32) - mean[...]).astype(jnp.bfloat16)
    for core in (0, 1):

        @pl.when(bits[1] == core)
        def _():
            late_products(core, last, centred, own)
            late_products(1 - core, last, centred, send)


def combine_kernel(flips, pieces, spares, bits, places, own, *rest):
    others, spare = rest[:pieces], rest[pieces : pieces + spares]
    outs, held = rest[pieces + spares : -1], rest[-1]
    count = own.shape[0]
    for i in range(count):
        other = others[0][i] if pieces == 1 else others[i][0]
        held[i] = own[i] + other
    for n, i in enumerate(flips):
        held[count + n] = held[i].T
    for i in range(spares):
        held[count + len(flips) + i] = spare[i][...]
    for r, out in enumerate(outs):
        out[...] = held[places[r, bits[1], bits[2]]]


def shape_of(shape, dtype):
    return jax.ShapeDtypeStruct(shape, dtype)


def combine(bits, own, others, flips, spares, held, places):
    rows = own.shape[1]
    return pl.pallas_call(
        functools.partial(combine_kernel, flips, len(others), len(spares)),
        out_shape=[shape_of((rows, rows), jnp.float32)] * len(places),
        in_specs=[SMEM, SMEM] + [VMEM] * (1 + len(others) + len(spares)),
        out_specs=[VMEM] * len(places),
        scratch_shapes=[pltpu.VMEM((len(held[0]), rows, rows), jnp.float32)],
        compiler_params=LIMIT,
        cost_estimate=BRIEF,
    )(bits, jnp.array(places, jnp.int32), own, *others, *spares)


def two_centres(log_derivs, shift):
    local_rows, local_params = log_derivs.shape
    part = local_params // 2
    everyone = ("row", "col", "half")
    row, col, half = (lax.axis_index(name) for name in everyone)
    side = (row >= 2).astype(jnp.int32)
    bits = jnp.stack([side, half, jnp.bitwise_xor(col, side)]).astype(jnp.int32)

    to_centre = [(1, 2), (2, 1)]
    to_own = [(0, 1), (3, 2)]
    to_far = [(0, 2), (3, 1)]
    centres = [(r * 2 + h, r * 2 + 1 - h) for r in (1, 2) for h in (0, 1)]

    def swap(value):
        narrow = lax.ppermute(value.astype(jnp.float16), ("row", "half"), centres)
        return narrow.astype(jnp.float32)

    def send(value, blocks):
        return lax.ppermute(value.astype(jnp.float16), everyone, round_pairs(blocks))

    near, far, far_sum = pl.pallas_call(
        split_kernel,
        out_shape=[
            shape_of((local_rows, part), jnp.bfloat16),
            shape_of((local_rows, part), jnp.bfloat16),
            shape_of((1, part), jnp.float32),
        ],
        in_specs=[SMEM, ANY],
        out_specs=[VMEM] * 3,
        scratch_shapes=[pltpu.SemaphoreType.DMA((2,))],
        compiler_params=pltpu.CompilerParams(vmem_limit_bytes=57 * 2**20),
        cost_estimate=BRIEF,
    )(bits, log_derivs)
    from_centre = lax.ppermute(far, "row", to_centre)
    from_sum = lax.ppermute(far_sum, "row", to_far)
    from_edge = lax.ppermute(near, "row", to_own)
    from_far_edge = lax.ppermute(far, "row", to_far)

    partial = pl.pallas_call(
        sum_kernel,
        out_shape=shape_of((1, part), jnp.float32),
        in_specs=[VMEM] * 3,
        out_specs=VMEM,
        compiler_params=LIMIT,
        cost_estimate=LONG,
    )(from_centre, near, from_sum)
    early_blocks = (3, local_rows, local_rows)
    centred, mean, own, other = pl.pallas_call(
        early_kernel,
        out_shape=[
            shape_of((3, local_rows, part), jnp.bfloat16),
            shape_of((1, part), jnp.float32),
            shape_of(early_blocks, jnp.float32),
            shape_of(early_blocks, jnp.float32),
        ],
        in_specs=[SMEM] + [VMEM] * 4,
        out_specs=[VMEM] * 4,
        scratch_shapes=[pltpu.VMEM((2,) + early_blocks, jnp.float32)],
        compiler_params=LIMIT,
        cost_estimate=BRIEF,
    )(bits, from_centre, from_edge, near, partial)
    others = [swap(other)]
    places = held_place(EARLY_HELD, NEAR_ROUNDS + FAR_ROUNDS) + [[[SPARE] * 2] * 2]
    *early, spare = combine(bits, own, others, (1, 2), (), EARLY_HELD, places)
    near_blocks, far_blocks = early[: len(NEAR_ROUNDS)], early[len(NEAR_ROUNDS) :]
    arrived = [send(value, blocks) for value, blocks in zip(near_blocks, NEAR_ROUNDS)]
    summed = sum(block.astype(jnp.float32) for block in arrived)

    late_blocks = shape_of((2, local_rows, local_rows), jnp.float32)
    handed = [summed] + far_blocks
    own, other, summed, *far_blocks = pl.pallas_call(
        late_kernel,
        out_shape=[late_blocks, late_blocks]
        + [shape_of(value.shape, value.dtype) for value in handed],
        in_specs=[SMEM] + [VMEM] * 3 + [ANY] * len(handed),
        out_specs=[VMEM] * 2 + [ANY] * len(handed),
        scratch_shapes=[pltpu.VMEM((local_rows, part), jnp.bfloat16)],
        input_output_aliases={4 + i: 2 + i for i in range(len(handed))},
        compiler_params=LIMIT,
        cost_estimate=BRIEF,
    )(bits, from_far_edge, mean, centred, *handed)
    other = swap(other)
    arrived = [send(value, blocks) for value, blocks in zip(far_blocks, FAR_ROUNDS)]
    places = held_place(LATE_HELD, LATE_ROUNDS)
    late = combine(bits, own, [other], (0, 1), (spare,), LATE_HELD, places)
    arrived += [send(value, blocks) for value, blocks in zip(late, LATE_ROUNDS)]
    summed = summed + sum(block.astype(jnp.float32) for block in reversed(arrived))
    return add_shift(summed, 1, shift, local_rows)


def solution(mesh):
    shape = mesh.shape
    small = shape["row"] == 4 and shape["col"] == 2 and shape["half"] == 2
    return jax.shard_map(
        two_centres if small else gathered,
        mesh=mesh,
        in_specs=(P(("groups", "row"), ("col", "half")), P("groups")),
        out_specs=P(("groups", "row"), ("col", "half")),
        check_vma=False,
    )
```

```python
import functools

import jax
import jax.numpy as jnp
from jax import lax
from jax.experimental import pallas as pl
from jax.experimental.pallas import tpu as pltpu
from jax.sharding import PartitionSpec as P


def pair_product(left, right):
    return jnp.einsum("ip,jp->ij", left, right, preferred_element_type=jnp.float32)


def add_shift(summed, samples, shift, local_rows):
    width = summed.shape[1]
    first_row = lax.axis_index("row") * local_rows
    block = lax.axis_index("col") * lax.axis_size("half") + lax.axis_index("half")
    row_ids = first_row + lax.broadcasted_iota(jnp.int32, (local_rows, width), 0)
    column_ids = block * width + lax.broadcasted_iota(jnp.int32, (local_rows, width), 1)
    return summed / samples + jnp.where(row_ids == column_ids, shift[0], 0.0)


def gathered(log_derivs, shift):
    local_rows = log_derivs.shape[0]
    samples = local_rows * lax.axis_size("row")
    rows = lax.all_gather(log_derivs, "row", axis=0, tiled=True).astype(jnp.float32)
    mean = jnp.sum(rows, axis=0) / samples
    centered = (rows - mean[None, :]).astype(jnp.bfloat16)
    own = (log_derivs.astype(jnp.float32) - mean[None, :]).astype(jnp.bfloat16)
    tile = pair_product(own, centered)
    summed = lax.psum_scatter(tile, ("col", "half"), scatter_dimension=1, tiled=True)
    return add_shift(summed, samples, shift, local_rows)


NEAR_ROUNDS = (
    (((1, 0), (1, 1)), ((0, 2), (1, 2))),
    (((1, 1), (1, 0)), ((1, 2), (0, 2))),
)
FAR_ROUNDS = (
    (((0, 1), (0, 0)), ((2, 0), (2, 2))),
    (((0, 0), (0, 1)), ((2, 2), (2, 0))),
)
LATE_ROUNDS = (
    (((3, 0), (3, 1)), ((3, 2), (3, 3))),
    (((3, 1), (3, 0)), ((3, 3), (3, 2))),
    (((0, 3), (1, 3)), ((2, 3), (2, 1))),
    (((1, 3), (0, 3)), ((2, 1), (2, 3))),
)
EARLY_SUMS = (((0, 0), (0, 1), (1, 1)), ((2, 2), (2, 0), (2, 1)))
EARLY_HELD = (
    ((0, 0), (0, 1), (1, 1), (1, 0), (1, 1)),
    ((2, 2), (2, 0), (2, 1), (0, 2), (1, 2)),
)
SPARE = 2
LATE_SUMS = (((3, 0), (3, 1)), ((3, 2), (3, 3)))
LATE_HELD = (
    ((3, 0), (3, 1), (0, 3), (1, 3), (1, 1)),
    ((3, 2), (3, 3), (2, 3), (3, 3), (2, 1)),
)
VMEM = pl.BlockSpec(memory_space=pltpu.VMEM)
SMEM = pl.BlockSpec(memory_space=pltpu.SMEM)
ANY = pl.BlockSpec(memory_space=pl.ANY)
LIMIT = pltpu.CompilerParams(vmem_limit_bytes=40 * 2**20)
BRIEF = pl.CostEstimate(flops=1024, bytes_accessed=1024, transcendentals=0)
LONG = pl.CostEstimate(flops=3 * 2**31, bytes_accessed=1024, transcendentals=0)


def device_index(row, col, half):
    return (row * 2 + col) * 2 + half


def round_pairs(blocks):
    pairs = []
    for side in (0, 1):
        for turn in (0, 1):
            for half in (0, 1):
                block = blocks[half][turn]
                if block is None:
                    continue
                i, j = (3 - b if side else b for b in block)
                source = device_index(1 + side, turn ^ side, half)
                pairs.append((source, device_index(i, j // 2, j % 2)))
    return pairs


def held_place(held, rounds):
    return [
        [[0 if b is None else held[half].index(b) for b in rounds_[half]] for half in (0, 1)]
        for rounds_ in rounds
    ]


def split_kernel(bits, values, near, far, far_sum, sems):
    part = far.shape[1]
    step = 512
    copies = []
    for i, (out, start) in enumerate(((far, bits[0]), (near, 1 - bits[0]))):
        columns = pl.ds(pl.multiple_of(start * part, 128), part)
        copies.append(pltpu.make_async_copy(values.at[:, columns], out, sems.at[i]))
    for copy in copies:
        copy.start()
    copies[0].wait()

    @pl.loop(0, part // step)
    def _(j):
        columns = pl.ds(pl.multiple_of(j * step, step), step)
        block = far[:, columns].astype(jnp.float32)
        far_sum[:, columns] = jnp.sum(block, axis=0, keepdims=True)

    copies[1].wait()


def block_product(left, right):
    return lax.dot_general(left, right, (((1,), (1,)), ((), ())), preferred_element_type=jnp.float32)


def sum_kernel(other, near, far_sum, partial):
    step = 512

    @pl.loop(0, near.shape[1] // step)
    def _(n):
        columns = pl.ds(pl.multiple_of(n * step, step), step)
        rows = other[:, columns].astype(jnp.float32) + near[:, columns].astype(jnp.float32)
        partial[:, columns] = far_sum[:, columns] + jnp.sum(rows, axis=0, keepdims=True)


def early_kernel(bits, other, edge, near, partial, centred, mean, own, send, both):
    rows, part = near.shape
    step = 512

    @pl.loop(0, part // step)
    def _(n):
        columns = pl.ds(pl.multiple_of(n * step, step), step)
        values = [block[:, columns].astype(jnp.float32) for block in (edge, near, other)]
        total = partial[:, columns] + jnp.sum(values[0], axis=0, keepdims=True)
        average = total * (1.0 / (4 * rows))
        mean[:, columns] = average
        for i in range(3):
            centred[i, :, columns] = (values[i] - average).astype(jnp.bfloat16)

    for core in (0, 1):
        for place, (i, j) in enumerate(EARLY_SUMS[core]):
            both[core, place] = block_product(centred[i], centred[j]) * (1.0 / (4 * rows))
    own[...] = both[bits[1]]
    send[...] = both[1 - bits[1]]


def late_products(core, last, centred, out):
    for place, (_, j) in enumerate(LATE_SUMS[core]):
        product = block_product(last[...], last[...] if j == 3 else centred[j])
        out[place] = product * (1.0 / (4 * last.shape[0]))


def late_kernel(bits, far_edge, mean, centred, *rest):
    own, send = rest[(len(rest) - 3) // 2 :][:2]
    last = rest[-1]
    last[...] = (far_edge[...].astype(jnp.float32) - mean[...]).astype(jnp.bfloat16)
    for core in (0, 1):

        @pl.when(bits[1] == core)
        def _():
            late_products(core, last, centred, own)
            late_products(1 - core, last, centred, send)


def combine_kernel(flips, pieces, spares, bits, places, own, *rest):
    others, spare = rest[:pieces], rest[pieces : pieces + spares]
    outs, held = rest[pieces + spares : -1], rest[-1]
    count = own.shape[0]
    for i in range(count):
        other = others[0][i] if pieces == 1 else others[i][0]
        held[i] = own[i] + other
    for n, i in enumerate(flips):
        held[count + n] = held[i].T
    for i in range(spares):
        held[count + len(flips) + i] = spare[i][...]
    for r, out in enumerate(outs):
        out[...] = held[places[r, bits[1], bits[2]]]


def shape_of(shape, dtype):
    return jax.ShapeDtypeStruct(shape, dtype)


def combine(bits, own, others, flips, spares, held, places):
    rows = own.shape[1]
    return pl.pallas_call(
        functools.partial(combine_kernel, flips, len(others), len(spares)),
        out_shape=[shape_of((rows, rows), jnp.float32)] * len(places),
        in_specs=[SMEM, SMEM] + [VMEM] * (1 + len(others) + len(spares)),
        out_specs=[VMEM] * len(places),
        scratch_shapes=[pltpu.VMEM((len(held[0]), rows, rows), jnp.float32)],
        compiler_params=LIMIT,
        cost_estimate=BRIEF,
    )(bits, jnp.array(places, jnp.int32), own, *others, *spares)


def two_centres(log_derivs, shift):
    local_rows, local_params = log_derivs.shape
    part = local_params // 2
    everyone = ("row", "col", "half")
    row, col, half = (lax.axis_index(name) for name in everyone)
    side = (row >= 2).astype(jnp.int32)
    bits = jnp.stack([side, half, jnp.bitwise_xor(col, side)]).astype(jnp.int32)

    to_centre = [(1, 2), (2, 1)]
    to_own = [(0, 1), (3, 2)]
    to_far = [(0, 2), (3, 1)]
    centres = [(r * 2 + h, r * 2 + 1 - h) for r in (1, 2) for h in (0, 1)]

    def swap(value):
        narrow = lax.ppermute(value.astype(jnp.float16), ("row", "half"), centres)
        return narrow.astype(jnp.float32)

    def send(value, blocks):
        return lax.ppermute(value.astype(jnp.float16), everyone, round_pairs(blocks))

    near, far, far_sum = pl.pallas_call(
        split_kernel,
        out_shape=[
            shape_of((local_rows, part), jnp.bfloat16),
            shape_of((local_rows, part), jnp.bfloat16),
            shape_of((1, part), jnp.float32),
        ],
        in_specs=[SMEM, ANY],
        out_specs=[VMEM] * 3,
        scratch_shapes=[pltpu.SemaphoreType.DMA((2,))],
        compiler_params=LIMIT,
        cost_estimate=BRIEF,
    )(bits, log_derivs)
    from_centre = lax.ppermute(far, "row", to_centre)
    from_sum = lax.ppermute(far_sum, "row", to_far)
    from_edge = lax.ppermute(near, "row", to_own)
    from_far_edge = lax.ppermute(far, "row", to_far)

    partial = pl.pallas_call(
        sum_kernel,
        out_shape=shape_of((1, part), jnp.float32),
        in_specs=[VMEM] * 3,
        out_specs=VMEM,
        compiler_params=LIMIT,
        cost_estimate=LONG,
    )(from_centre, near, from_sum)
    early_blocks = (3, local_rows, local_rows)
    centred, mean, own, other = pl.pallas_call(
        early_kernel,
        out_shape=[
            shape_of((3, local_rows, part), jnp.bfloat16),
            shape_of((1, part), jnp.float32),
            shape_of(early_blocks, jnp.float32),
            shape_of(early_blocks, jnp.float32),
        ],
        in_specs=[SMEM] + [VMEM] * 4,
        out_specs=[VMEM] * 4,
        scratch_shapes=[pltpu.VMEM((2,) + early_blocks, jnp.float32)],
        compiler_params=LIMIT,
        cost_estimate=BRIEF,
    )(bits, from_centre, from_edge, near, partial)
    others = [swap(other)]
    places = held_place(EARLY_HELD, NEAR_ROUNDS + FAR_ROUNDS) + [[[SPARE] * 2] * 2]
    *early, spare = combine(bits, own, others, (1, 2), (), EARLY_HELD, places)
    near_blocks, far_blocks = early[: len(NEAR_ROUNDS)], early[len(NEAR_ROUNDS) :]
    arrived = [send(value, blocks) for value, blocks in zip(near_blocks, NEAR_ROUNDS)]
    summed = sum(block.astype(jnp.float32) for block in arrived)

    late_blocks = shape_of((2, local_rows, local_rows), jnp.float32)
    handed = [summed] + far_blocks
    own, other, summed, *far_blocks = pl.pallas_call(
        late_kernel,
        out_shape=[late_blocks, late_blocks]
        + [shape_of(value.shape, value.dtype) for value in handed],
        in_specs=[SMEM] + [VMEM] * 3 + [ANY] * len(handed),
        out_specs=[VMEM] * 2 + [ANY] * len(handed),
        scratch_shapes=[pltpu.VMEM((local_rows, part), jnp.bfloat16)],
        input_output_aliases={4 + i: 2 + i for i in range(len(handed))},
        compiler_params=LIMIT,
        cost_estimate=BRIEF,
    )(bits, from_far_edge, mean, centred, *handed)
    other = swap(other)
    arrived = [send(value, blocks) for value, blocks in zip(far_blocks, FAR_ROUNDS)]
    places = held_place(LATE_HELD, LATE_ROUNDS)
    late = combine(bits, own, [other], (0, 1), (spare,), LATE_HELD, places)
    arrived += [send(value, blocks) for value, blocks in zip(late, LATE_ROUNDS)]
    summed = summed + sum(block.astype(jnp.float32) for block in reversed(arrived))
    return add_shift(summed, 1, shift, local_rows)


def solution(mesh):
    shape = mesh.shape
    small = shape["row"] == 4 and shape["col"] == 2 and shape["half"] == 2
    return jax.shard_map(
        two_centres if small else gathered,
        mesh=mesh,
        in_specs=(P(("groups", "row"), ("col", "half")), P("groups")),
        out_specs=P(("groups", "row"), ("col", "half")),
        check_vma=False,
    )
```
